32 devices in a mesh: dp: 8 (over z, y), blk: 4 (over x, core).
Axes of the slice: x: 2, y: 2, z: 4, core: 2. Of those that a mesh axis runs over, the one named last changes fastest.
Arguments:
- tokens: bfloat16 [4, 8192, 512], P(None, ('dp', 'blk')), may hold values from -6 to 6
- lengths: int32 [4, 8, 2], P(None, 'dp'), may hold values from 196 to 784, as said below
- attn_gain: bfloat16 [512], P(('dp', 'blk')), may hold values from 0.5 to 1.5
- attn_shift: bfloat16 [512], P(('dp', 'blk')), may hold values from -1.75 to 1.75
- w_qkv: bfloat16 [512, 1536], P(('dp', 'blk')), may hold values from -0.25 to 0.25
- qv_bias: bfloat16 [1024], P(('dp', 'blk')), may hold values from -1.75 to 1.75
- w_proj: bfloat16 [512, 512], P(('dp', 'blk')), may hold values from -1 to 1
- proj_bias: bfloat16 [512], P(('dp', 'blk')), may hold values from -1.75 to 1.75
- mlp_gain: bfloat16 [512], P(('dp', 'blk')), may hold values from 0.5 to 1.5
- mlp_shift: bfloat16 [512], P(('dp', 'blk')), may hold values from -1.75 to 1.75
- w_expand: bfloat16 [512, 2048], P(('dp', 'blk')), may hold values from -0.25 to 0.25
- expand_bias: bfloat16 [2048], P(('dp', 'blk')), may hold values from -3 to 3
- w_reduce: bfloat16 [2048, 512], P(('dp', 'blk')), may hold values from -0.125 to 0.125
- reduce_bias: bfloat16 [512], P(('dp', 'blk')), may hold values from -1.75 to 1.75
- cotangent: bfloat16 [4, 8192, 512], P(None, ('dp', 'blk')), may hold values from -6 to 6
Outputs:
- result: bfloat16 [4, 8192, 512], P(None, ('dp', 'blk'))
- grad_tokens: bfloat16 [4, 8192, 512], P(None, ('dp', 'blk'))
- grad_attn_gain: float32 [512], P(('dp', 'blk'))
- grad_attn_shift: float32 [512], P(('dp', 'blk'))
- grad_w_qkv: float32 [512, 1536], P(('dp', 'blk'))
- grad_qv_bias: float32 [1024], P(('dp', 'blk'))
- grad_w_proj: float32 [512, 512], P(('dp', 'blk'))
- grad_proj_bias: float32 [512], P(('dp', 'blk'))
- grad_mlp_gain: float32 [512], P(('dp', 'blk'))
- grad_mlp_shift: float32 [512], P(('dp', 'blk'))
- grad_w_expand: float32 [512, 2048], P(('dp', 'blk'))
- grad_expand_bias: float32 [2048], P(('dp', 'blk'))
- grad_w_reduce: float32 [2048, 512], P(('dp', 'blk'))
- grad_reduce_bias: float32 [512], P(('dp', 'blk'))
The draws below stay inside these ranges and needn't reach their ends.
Inputs may be any that keep to these rules, and one draw needn't show every extreme that they name: `lengths`: each group holds one image of 784 tokens and one of 196 tokens, in an order drawn from the seed.
All inputs are finite; a program needn't handle non-finite values.
Results may differ from the reference program's by a relative error of at most 0.01.
Values may be sent and summed in bfloat16 or wider, within the bound.
A program may use at most 128 MiB of HBM per device.

```python
import math
from functools import partial
import jax
import jax.numpy as jnp
from jax import lax

D = 512
HEAD_DIM = 32
FF = 2048
TOK_DEV = 256
MICRO = 4
LONG_IMG = 784
SHORT_IMG = 196
TOKENS = 8192
N_DP = 8
N_BLK = 4


def draw_lengths(key, part):
    key = jax.random.fold_in(key, 7)
    ordering = jax.random.randint(key, (MICRO, N_DP), 0, 2)
    first_len = jnp.where(ordering == 1, LONG_IMG, SHORT_IMG).astype(jnp.int32)
    second_len = (LONG_IMG + SHORT_IMG - first_len).astype(jnp.int32)
    return jnp.stack([first_len, second_len], axis=-1)


def level_of(stream_key, dims, shards, smallest, top_value):
    level = 1.0
    for axis_at, shards_of in shards:
        steps = jax.random.uniform(jax.random.fold_in(jax.random.fold_in(stream_key, 6), axis_at), (shards_of,), jnp.float32, smallest / len(shards), top_value / len(shards))
        level = level * jnp.repeat(jnp.exp(steps), dims[axis_at] // shards_of).reshape((-1,) + (1,) * (len(dims) - 1 - axis_at))
    return level


def gaussian(rng, dims, scale, reach, split=(), kind=jnp.bfloat16):
    values = scale * jax.random.normal(rng, dims, jnp.float32)
    if split:
        values = values * level_of(rng, dims, split, -0.22, 0.18)
    return jnp.clip(values, -reach, reach).astype(kind)


def setup_inputs(seed: int = 0) -> dict:
    key_of = jax.random.split(jax.random.key(seed), 16)
    tokens = gaussian(key_of[0], (MICRO, TOKENS, D), 1.0, 6.0, ((1, 32),))
    lengths = draw_lengths(jax.random.fold_in(key_of[15], 71), 0)
    attn_gain = jnp.clip(1.0 + 0.1 * jax.random.normal(key_of[2], (D,), jnp.float32), 0.5, 1.5).astype(jnp.bfloat16)
    attn_shift = gaussian(key_of[3], (D,), 0.3, 1.75, ((0, 32),))
    w_qkv = gaussian(key_of[4], (D, 3 * D), D ** -0.5, 0.25, ((0, 32),))
    qv_bias = gaussian(key_of[5], (2 * D,), 0.3, 1.75, ((0, 32),))
    w_proj = gaussian(key_of[6], (D, D), (D // 16) ** -0.5, 1.0, ((0, 32),))
    proj_bias = gaussian(key_of[7], (D,), 0.3, 1.75, ((0, 32),))
    mlp_gain = jnp.clip(1.0 + 0.1 * jax.random.normal(key_of[8], (D,), jnp.float32), 0.5, 1.5).astype(jnp.bfloat16)
    mlp_shift = gaussian(key_of[9], (D,), 0.3, 1.75, ((0, 32),))
    w_expand = gaussian(key_of[10], (D, FF), D ** -0.5, 0.25, ((0, 32),))
    expand_bias = gaussian(key_of[11], (FF,), 0.5, 3.0, ((0, 32),))
    w_reduce = gaussian(key_of[12], (FF, D), FF ** -0.5, 0.125, ((0, 32),))
    reduce_bias = gaussian(key_of[13], (D,), 0.3, 1.75, ((0, 32),))
    cotangent = gaussian(key_of[14], (MICRO, TOKENS, D), 1.0, 6.0, ((1, 32),))
    return {"tokens": tokens, "lengths": lengths, "attn_gain": attn_gain, "attn_shift": attn_shift, "w_qkv": w_qkv, "qv_bias": qv_bias, "w_proj": w_proj, "proj_bias": proj_bias, "mlp_gain": mlp_gain, "mlp_shift": mlp_shift, "w_expand": w_expand, "expand_bias": expand_bias, "w_reduce": w_reduce, "reduce_bias": reduce_bias, "cotangent": cotangent}


@jax.custom_vjp
def low(v):
    return lax.optimization_barrier(v.astype(jnp.bfloat16)).astype(jnp.float32)

@jax.custom_vjp
def low_back(v):
    return v

def low_keep(v):
    return (low(v), None)

def low_pass(kept, grad):
    return (grad,)

def back_keep(v):
    return (v, None)

def back_low(kept, grad):
    return (low(grad),)
low.defvjp(low_keep, low_pass)
low_back.defvjp(back_keep, back_low)
epsilon = 1e-06
masked_score = -1e+30
highest = lax.Precision.HIGHEST

def segment_ids(positions, bounds):
    first_end = bounds[0]
    second_end = bounds[0] + bounds[1]
    return (positions >= first_end).astype(jnp.int32) + (positions >= second_end).astype(jnp.int32)

def normalize(values, norm_gain, norm_shift):
    centered = values - lax.optimization_barrier(jnp.mean(values, axis=-1, keepdims=True))
    inverse = lax.rsqrt(lax.optimization_barrier(jnp.mean(centered * centered, axis=-1, keepdims=True)) + epsilon)
    normed = centered * inverse
    return normed * norm_gain + norm_shift

def product(left_hand, right_hand):
    return jnp.dot(left_hand, right_hand, precision=highest, preferred_element_type=jnp.float32)

def attend(block_pair, key_heads, value_heads, key_segment, scaling):
    query_heads, query_segment = block_pair
    raw_scores = jnp.einsum('qhd,khd->hqk', query_heads, key_heads, precision=highest) * scaling
    raw_scores = low_back(raw_scores)
    same_segment = query_segment[:, None] == key_segment[None, :]
    scores = jnp.where(same_segment[None], raw_scores, masked_score)
    row_top = lax.optimization_barrier(jnp.max(scores, axis=-1, keepdims=True))
    exps = jnp.where(same_segment[None], jnp.exp(scores - row_top), 0.0)
    probs = exps / lax.optimization_barrier(jnp.sum(exps, axis=-1, keepdims=True))
    return jnp.einsum('hqk,khd->qhd', low(probs), value_heads, precision=highest)

def forward(inputs, bounds, params):
    attn_gain, attn_shift, w_qkv, qv_bias, w_proj, proj_bias, mlp_gain, mlp_shift, w_expand, expand_bias, w_reduce, reduce_bias = params
    height = inputs.shape[0]
    width = inputs.shape[1]
    heads = width // HEAD_DIM
    scaling = 1.0 / math.sqrt(HEAD_DIM)
    normed_a = low(normalize(inputs, attn_gain, attn_shift))
    shift_qkv = jnp.concatenate([qv_bias[:width], jnp.zeros((width,), jnp.float32), qv_bias[width:]])
    projected = low_back(low(product(normed_a, w_qkv) + shift_qkv))
    query_heads = projected[:, :width].reshape(height, heads, HEAD_DIM)
    key_heads = projected[:, width:2 * width].reshape(height, heads, HEAD_DIM)
    value_heads = projected[:, 2 * width:].reshape(height, heads, HEAD_DIM)
    segment = segment_ids(jnp.arange(height, dtype=jnp.int32), bounds)
    block_rows = min(512, height)
    blocks = height // block_rows
    mapped = lax.map(jax.checkpoint(partial(attend, key_heads=key_heads, value_heads=value_heads, key_segment=segment, scaling=scaling)), (query_heads.reshape(blocks, block_rows, heads, HEAD_DIM), segment.reshape(blocks, block_rows)))
    attended = low_back(low(mapped.reshape(height, width)))
    branch_a = low_back(product(attended, w_proj) + proj_bias)
    middle = inputs + branch_a
    normed_b = low(normalize(middle, mlp_gain, mlp_shift))
    expanded = low_back(product(normed_b, w_expand) + expand_bias)
    activated = low(jax.nn.gelu(expanded, approximate=False))
    return middle + (product(activated, w_reduce) + reduce_bias)

def reference(tokens, lengths, attn_gain, attn_shift, w_qkv, qv_bias, w_proj, proj_bias, mlp_gain, mlp_shift, w_expand, expand_bias, w_reduce, reduce_bias, cotangent):
    params = tuple((weight.astype(jnp.float32) for weight in (attn_gain, attn_shift, w_qkv, qv_bias, w_proj, proj_bias, mlp_gain, mlp_shift, w_expand, expand_bias, w_reduce, reduce_bias)))
    groups = MICRO * N_DP
    group_rows = N_BLK * TOK_DEV
    token_groups = tokens.reshape(groups, group_rows, D)
    cotan_groups = cotangent.reshape(groups, group_rows, D)
    bound_groups = lengths.reshape(groups, 2)

    def one_group(summed, element):
        token_rows, cotan_rows, bounds = element
        outputs, pullback = jax.vjp(lambda values, weights: forward(values, bounds, weights), token_rows.astype(jnp.float32), params)
        grad_rows, grad_params = pullback(cotan_rows.astype(jnp.float32))
        summed = tuple((earlier + addend for earlier, addend in zip(summed, grad_params)))
        return (summed, (outputs.astype(jnp.bfloat16), grad_rows.astype(jnp.bfloat16)))
    starting = tuple((jnp.zeros(weight.shape, jnp.float32) for weight in params))
    summed, stacked = lax.scan(one_group, starting, (token_groups, cotan_groups, bound_groups))
    results = stacked[0].reshape(tokens.shape)
    grad_tokens = stacked[1].reshape(tokens.shape)
    return (results, grad_tokens, summed[0], summed[1], summed[2], summed[3], summed[4], summed[5], summed[6], summed[7], summed[8], summed[9], summed[10], summed[11])
```

```python
import functools
import math

import jax
import jax.numpy as jnp
from jax import lax
from jax.experimental import pallas as pl
from jax.experimental.pallas import tpu as pltpu
from jax.sharding import PartitionSpec as P

HEAD_DIM = 32
LONG_IMG = 784
SHORT_IMG = 196
LANES = 128
HEADS_IN_BLOCK = LANES // HEAD_DIM
LONG_KEYS = 896
BF = jnp.bfloat16
F32 = jnp.float32
epsilon = 1e-06
LOG2E = math.log2(math.e)
SCALE = 1.0 / math.sqrt(HEAD_DIM)
MASKED = -1e30
ROWS = 256
A_GAIN, A_SHIFT, Q_BIAS, V_BIAS, P_BIAS, M_GAIN, M_SHIFT, R_BIAS, E_BIAS = range(9)
VEC_ROWS = 16


def nt(left, right):
    return lax.dot_general(left, right, (((1,), (1,)), ((), ())), preferred_element_type=F32)


def nn(left, right):
    return lax.dot_general(left, right, (((1,), (0,)), ((), ())), preferred_element_type=F32)


def tn(left, right):
    return lax.dot_general(left, right, (((0,), (0,)), ((), ())), preferred_element_type=F32)


def pieces(total, size):
    return [(at, min(size, total - at)) for at in range(0, total, size)]


def lanes(rows, width=LANES):
    return lax.broadcasted_iota(jnp.int32, (rows, width), 1)


def to_canonical(swapped, natural, moved):
    total = natural.shape[0]
    tail = LONG_IMG + SHORT_IMG
    moved[0:LONG_IMG] = natural[SHORT_IMG:tail]
    moved[LONG_IMG:tail] = natural[0:SHORT_IMG]
    moved[tail:total] = natural[tail:total]


def to_natural(ordered, moved):
    total = ordered.shape[0]
    tail = LONG_IMG + SHORT_IMG
    moved[SHORT_IMG:tail] = ordered[0:LONG_IMG]
    moved[0:SHORT_IMG] = ordered[LONG_IMG:tail]
    moved[tail:total] = ordered[tail:total]


def norm_parts(values):
    centered = values - jnp.mean(values, axis=-1, keepdims=True)
    inverse = lax.rsqrt(jnp.mean(centered * centered, axis=-1, keepdims=True) + epsilon)
    return centered * inverse, inverse


def norm_back(gradient, normed, inverse, gain):
    scaled = gradient * gain
    return inverse * (
        scaled
        - jnp.mean(scaled, axis=-1, keepdims=True)
        - normed * jnp.mean(scaled * normed, axis=-1, keepdims=True)
    )


def gelu_parts(values):
    size = jnp.abs(values)
    z = size * math.sqrt(0.5)
    t = 1.0 / (1.0 + 0.5 * z)
    poly = 0.17087277
    for factor in (-0.82215223, 1.48851587, -1.13520398, 0.27886807, -0.18628806, 0.09678418,
                   0.37409196, 1.00002368, -1.26551223):
        poly = poly * t + factor
    bell = jnp.exp(-z * z)
    tail = 0.5 * t * bell * jnp.exp(poly)
    phi = jnp.where(values >= 0.0, 1.0 - tail, tail)
    return values * phi, phi + values * (bell * (1.0 / math.sqrt(2.0 * math.pi)))


def fill_masks(aug_q, aug_k):
    total = aug_q.shape[0]
    row = lax.broadcasted_iota(jnp.int32, (total, LANES), 0)
    segment = (row >= LONG_IMG).astype(jnp.int32) + (row >= LONG_IMG + SHORT_IMG).astype(jnp.int32)
    place = lanes(total) % HEAD_DIM
    aug_q[...] = jnp.where(place == segment, 1.0, 0.0).astype(BF)
    aug_k[...] = jnp.where((place < 3) & (place != segment), MASKED, 0.0).astype(BF)


def attend_tiles(total, size):
    tail = total - LONG_IMG
    first = total - 2 * LANES
    return [(at, n, 0, LONG_KEYS, True, at) for at, n in pieces(LONG_IMG, size)] + [
        (LONG_IMG + at, n, first, 2 * LANES, False, at) for at, n in pieces(tail, size)
    ]


def block_columns(ref, j, offset=0):
    return ref[:, pl.ds(pl.multiple_of(offset + j * LANES, LANES), LANES)]


def forward_block(j, qkv, attended, inverse, e_long, e_tail, aug_q, aug_k, size=400):
    total, width = attended.shape
    cols = pl.ds(pl.multiple_of(j * LANES, LANES), LANES)
    qb, kb, vb = (block_columns(qkv, j, width * i) for i in range(3))
    group = lanes(total) // HEAD_DIM
    for head in range(HEADS_IN_BLOCK):
        mine = group == head
        qa = jnp.where(mine, qb, aug_q[...])
        ka = jnp.where(mine, kb, aug_k[...])
        va = jnp.where(mine, vb, jnp.ones_like(vb))
        at = j * HEADS_IN_BLOCK + head
        for row, rows, key, keys, is_long, place in attend_tiles(total, size):
            scores = nt(qa[row : row + rows], ka[key : key + keys])
            exps = jnp.exp2(scores - jnp.max(scores, axis=1, keepdims=True)).astype(BF)
            store = e_long if is_long else e_tail
            store[at, place : place + rows, :] = exps
            product = nn(exps, va[key : key + keys])
            inv = 1.0 / pltpu.roll(product, HEAD_DIM, 1)
            out = (product * inv).astype(BF)
            here = (pl.ds(row, rows), cols)
            if head == 0:
                attended[here] = out
                inverse[here] = inv
            else:
                keep = lanes(rows) // HEAD_DIM == head
                attended[here] = jnp.where(keep, out, attended[here])
                inverse[here] = jnp.where(keep, inv, inverse[here])


def backward_block(j, qkv, attended, inverse, e_long, e_tail, d_att, dq_b, dk_t, dv_t, size=400):
    total, width = attended.shape
    qb, kb, vb = (block_columns(qkv, j, width * i) for i in range(3))
    group = lanes(total) // HEAD_DIM
    scaled = block_columns(d_att, j).astype(F32) * block_columns(inverse, j)
    inner = scaled * block_columns(attended, j).astype(F32)
    from_group = lax.broadcasted_iota(jnp.int32, (LANES, LANES), 0) // HEAD_DIM
    to_group = lanes(LANES) // HEAD_DIM
    spread = jnp.where((from_group + 1) % HEADS_IN_BLOCK == to_group, 1.0, 0.0).astype(BF)
    high = inner.astype(BF)
    low = (inner - high.astype(F32)).astype(BF)
    sums = nn(high, spread) + nn(low, spread)
    sum_high = sums.astype(BF)
    sum_low = (sums - sum_high.astype(F32)).astype(BF)
    place = lanes(total) % HEAD_DIM
    zeros = jnp.zeros_like(sum_high)
    aug = jnp.where(place == 0, -sum_high, jnp.where(place == 1, -sum_low, zeros))
    scaled = scaled.astype(BF)
    q_t, s_t = qb.T, scaled.T
    for head in range(HEADS_IN_BLOCK):
        mine = group == head
        left = jnp.where(mine, scaled, jnp.where(group == (head + 1) % HEADS_IN_BLOCK, aug, zeros))
        va = jnp.where(mine, vb, jnp.ones_like(vb))
        at = j * HEADS_IN_BLOCK + head
        of_head = slice(HEAD_DIM * head, HEAD_DIM * (head + 1))
        sums_of = {}
        for row, rows, key, keys, is_long, where in attend_tiles(total, size):
            store = e_long if is_long else e_tail
            exps = store[at, where : where + rows, :]
            d_scores = (exps.astype(F32) * nt(left[row : row + rows], va[key : key + keys])).astype(BF)
            dq = (nn(d_scores, kb[key : key + keys]) * SCALE).astype(BF)
            here = pl.ds(row, rows)
            dq_b[here] = dq if head == 0 else jnp.where(lanes(rows) // HEAD_DIM == head, dq, dq_b[here])
            more_v = nn(s_t[of_head, row : row + rows], exps)
            more_k = nn(q_t[of_head, row : row + rows], d_scores)
            if is_long in sums_of:
                more_v, more_k = sums_of[is_long][0] + more_v, sums_of[is_long][1] + more_k
            sums_of[is_long] = (more_v, more_k)
        first = total - 2 * LANES
        both = LONG_KEYS - first
        for ref, which, factor in ((dv_t, 0, None), (dk_t, 1, 1.0 / LOG2E)):
            long_part, tail_part = sums_of[True][which], sums_of[False][which]
            if factor is not None:
                long_part, tail_part = long_part * factor, tail_part * factor
            ref[of_head, 0:first] = long_part[:, :first]
            ref[of_head, first:LONG_KEYS] = long_part[:, first:] + tail_part[:, :both]
            ref[of_head, LONG_KEYS:total] = tail_part[:, both:]
    for i, value in enumerate((dq_b[...], dk_t[...].T.astype(BF), dv_t[...].T.astype(BF))):
        qkv[:, pl.ds(pl.multiple_of(i * width + j * LANES, LANES), LANES)] = value


BUFFERS = (
    "x_in", "cot", "xc", "qkv", "attended", "inverse", "e_long", "e_tail", "aug_q", "aug_k", "middle",
    "acc_a", "acc_b", "hb", "act", "d_exp", "dq_b", "dk_t", "dv_t",
    "w_qkv", "w_proj", "w_expand", "w_reduce",
)


def buffers(total, width, ff):
    heads = width // HEAD_DIM
    rows = (total, width)
    return {
        "x_in": (rows, BF),
        "cot": (rows, BF),
        "xc": (rows, BF),
        "qkv": ((total, 3 * width), BF),
        "attended": (rows, BF),
        "inverse": (rows, F32),
        "e_long": ((heads, LONG_IMG, LONG_KEYS), BF),
        "e_tail": ((heads, total - LONG_IMG, 2 * LANES), BF),
        "aug_q": ((total, LANES), BF),
        "aug_k": ((total, LANES), BF),
        "middle": (rows, F32),
        "acc_a": (rows, F32),
        "acc_b": (rows, F32),
        "hb": (rows, BF),
        "act": (rows, BF),
        "d_exp": (rows, BF),
        "dq_b": ((total, LANES), BF),
        "dk_t": ((LANES, total), F32),
        "dv_t": ((LANES, total), F32),
        "w_qkv": ((width, 3 * width), BF),
        "w_proj": ((width, width), BF),
        "w_expand": ((width, ff), BF),
        "w_reduce": ((ff, width), BF),
    }


def compute(b, flag, vec, g_vec, hooks):
    total, width = b["xc"].shape
    ff = b["w_expand"].shape[1]
    row_tiles = pieces(total, ROWS)
    swapped = flag[0:1, :] > 0.5
    acc_a, acc_b = b["acc_a"], b["acc_b"]

    def vector(row):
        return vec[row : row + 1, :]

    def add_sum(row, values):
        g_vec[row : row + 1, :] = g_vec[row : row + 1, :] + jnp.sum(values, axis=0, keepdims=True)

    def load(source, target):
        for at, n in row_tiles:
            acc_a[at : at + n] = source[at : at + n].astype(F32)
        to_canonical(swapped, acc_a, acc_b)
        for at, n in row_tiles:
            target[at : at + n] = jnp.where(swapped, acc_b[at : at + n], acc_a[at : at + n]).astype(BF)

    def unload(values, moved, target):
        to_natural(values, moved)
        for at, n in row_tiles:
            target[at : at + n] = jnp.where(swapped, moved[at : at + n], values[at : at + n]).astype(BF)

    g_vec[...] = jnp.zeros_like(g_vec)
    fill_masks(b["aug_q"], b["aug_k"])
    hooks("need tokens")
    load(b["x_in"], b["xc"])
    hooks("need qkv")
    ha, qkv, w_qkv = b["x_in"], b["qkv"], b["w_qkv"]
    for at, n in row_tiles:
        rows = slice(at, at + n)
        normed, _ = norm_parts(b["xc"][rows].astype(F32))
        lowered = (normed * vector(A_GAIN) + vector(A_SHIFT)).astype(BF)
        ha[rows] = lowered
        projected = nn(lowered, w_qkv[...])
        qkv[rows, 0:width] = ((projected[:, :width] + vector(Q_BIAS)) * (SCALE * LOG2E)).astype(BF)
        qkv[rows, width : 2 * width] = projected[:, width : 2 * width].astype(BF)
        qkv[rows, 2 * width : 3 * width] = (projected[:, 2 * width :] + vector(V_BIAS)).astype(BF)

    blocks = width // LANES
    attended, inverse, e_long, e_tail = b["attended"], b["inverse"], b["e_long"], b["e_tail"]

    def one_forward(j, carried):
        forward_block(j, qkv, attended, inverse, e_long, e_tail, b["aug_q"], b["aug_k"])
        return carried

    lax.fori_loop(0, blocks, one_forward, 0)

    hooks("need cotangent")
    cot, middle, hb, act, d_exp = b["cot"], b["middle"], b["hb"], b["act"], b["d_exp"]
    w_proj, w_expand, w_reduce = b["w_proj"], b["w_expand"], b["w_reduce"]
    load(cot, cot)
    hooks("need proj")
    for at, n in row_tiles:
        rows = slice(at, at + n)
        mid = b["xc"][rows].astype(F32) + (nn(attended[rows], w_proj[...]) + vector(P_BIAS))
        middle[rows] = mid
        normed, _ = norm_parts(mid)
        hb[rows] = (normed * vector(M_GAIN) + vector(M_SHIFT)).astype(BF)
        acc_a[rows] = mid + vector(R_BIAS)
        add_sum(R_BIAS, cot[rows].astype(F32))

    hooks("need expand")
    hooks("need reduce")
    for part in range(ff // width):
        cols = slice(part * width, (part + 1) * width)
        for at, n in row_tiles:
            rows = slice(at, at + n)
            value, slope = gelu_parts(nn(hb[rows], w_expand[:, cols]) + vector(E_BIAS + part))
            low = value.astype(BF)
            act[rows] = low
            acc_a[rows] = acc_a[rows] + nn(low, w_reduce[cols, :])
            d_low = (nt(cot[rows], w_reduce[cols, :]) * slope).astype(BF)
            d_exp[rows] = d_low
            more = nt(d_low, w_expand[:, cols])
            acc_b[rows] = more if part == 0 else acc_b[rows] + more
            add_sum(E_BIAS + part, d_low.astype(F32))
        w_reduce[cols, :] = tn(act[...], cot[...]).astype(BF)
        w_expand[:, cols] = tn(hb[...], d_exp[...]).astype(BF)
    hooks("have reduce")
    hooks("have expand")

    d_att = d_exp
    for at, n in row_tiles:
        rows = slice(at, at + n)
        gradient = acc_b[rows]
        normed, inv = norm_parts(middle[rows])
        d_mid = cot[rows].astype(F32) + norm_back(gradient, normed, inv, vector(M_GAIN))
        add_sum(M_GAIN, gradient * normed)
        add_sum(M_SHIFT, gradient)
        middle[rows] = d_mid
        d_branch = d_mid.astype(BF)
        act[rows] = d_branch
        add_sum(P_BIAS, d_branch.astype(F32))
        d_att[rows] = nt(d_branch, w_proj[...]).astype(BF)
    w_proj[...] = tn(attended[...], act[...]).astype(BF)
    hooks("have proj")
    unload(acc_a, acc_b, hb)
    hooks("have result")

    def one_backward(j, carried):
        backward_block(j, qkv, attended, inverse, e_long, e_tail, d_att, b["dq_b"], b["dk_t"], b["dv_t"])
        return carried

    lax.fori_loop(0, blocks, one_backward, 0)

    for at, n in row_tiles:
        rows = slice(at, at + n)
        acc_b[rows] = nt(qkv[rows], w_qkv[...])
        add_sum(Q_BIAS, qkv[rows, 0:width].astype(F32))
        add_sum(V_BIAS, qkv[rows, 2 * width : 3 * width].astype(F32))
    w_qkv[...] = tn(ha[...], qkv[...]).astype(BF)
    hooks("have qkv")
    for at, n in row_tiles:
        rows = slice(at, at + n)
        gradient = acc_b[rows]
        normed, inv = norm_parts(b["xc"][rows].astype(F32))
        add_sum(A_GAIN, gradient * normed)
        add_sum(A_SHIFT, gradient)
        acc_a[rows] = middle[rows] + norm_back(gradient, normed, inv, vector(A_GAIN))
    hooks("have vectors")
    unload(acc_a, acc_b, act)
    hooks("have grad")


def local_kernel(flag, vec, x_in, cot_in, w_qkv, w_proj, w_expand, w_reduce,
                 result, grad_x, g_qkv, g_proj, g_expand, g_reduce, g_vec, *scratch):
    b = dict(zip(BUFFERS, scratch))
    sems = scratch[len(BUFFERS)]
    weights = {"qkv": (w_qkv, g_qkv), "proj": (w_proj, g_proj), "expand": (w_expand, g_expand), "reduce": (w_reduce, g_reduce)}
    moves = {"need tokens": (x_in, b["x_in"]), "need cotangent": (cot_in, b["cot"])}
    for name, (source, target) in weights.items():
        moves["need " + name] = (source, b["w_" + name])
        moves["have " + name] = (b["w_" + name], target)
    moves["have result"] = (b["hb"], result)
    moves["have grad"] = (b["act"], grad_x)
    copies = {name: pltpu.make_async_copy(source, target, sems.at[i]) for i, (name, (source, target)) in enumerate(moves.items())}
    for name, copy in copies.items():
        if name.startswith("need"):
            copy.start()

    def hooks(name):
        if name in copies:
            if name.startswith("need"):
                copies[name].wait()
            else:
                copies[name].start()

    compute(b, flag, vec, g_vec, hooks)
    for name, copy in copies.items():
        if name.startswith("have"):
            copy.wait()


def run_block(flag, vec, x_in, cot_in, w_qkv, w_proj, w_expand, w_reduce):
    vmem, anywhere = pl.BlockSpec(memory_space=pltpu.VMEM), pl.BlockSpec(memory_space=pl.ANY)
    total, width = x_in.shape
    scratch = buffers(total, width, w_expand.shape[1])
    like = (x_in, x_in, w_qkv, w_proj, w_expand, w_reduce)
    return pl.pallas_call(
        local_kernel,
        out_shape=[jax.ShapeDtypeStruct(one.shape, BF) for one in like]
        + [jax.ShapeDtypeStruct((VEC_ROWS, width), F32)],
        in_specs=[vmem] * 2 + [anywhere] * 6,
        out_specs=[anywhere] * 6 + [vmem],
        scratch_shapes=[pltpu.VMEM(*scratch[name]) for name in BUFFERS] + [pltpu.SemaphoreType.DMA((12,))],
        compiler_params=pltpu.CompilerParams(vmem_limit_bytes=63 * 2**20),
    )(flag, vec, x_in, cot_in, w_qkv, w_proj, w_expand, w_reduce)


def body(
    tokens, lengths, attn_gain, attn_shift, w_qkv, qv_bias, w_proj, proj_bias,
    mlp_gain, mlp_shift, w_expand, expand_bias, w_reduce, reduce_bias, cotangent,
):
    axes = ("dp", "blk")
    width = tokens.shape[2]
    me = lax.axis_index("blk")
    devices = lax.axis_size(axes)
    index = lax.axis_index("dp") * lax.axis_size("blk") + me
    first = lax.dynamic_index_in_dim(lengths, me, 0, keepdims=False)[0, 0]
    flag = jnp.broadcast_to((first == SHORT_IMG).astype(F32), (8, width))

    def exchange(rows):
        return lax.all_to_all(rows, "blk", 0, 0, tiled=True)

    def gather(shard):
        return lax.all_gather(shard, axes, axis=0, tiled=True)

    vectors = (attn_gain, attn_shift, qv_bias, proj_bias, mlp_gain, mlp_shift, reduce_bias, expand_bias)
    sizes = [one.shape[0] for one in vectors]
    packed = lax.all_gather(jnp.concatenate(vectors), axes, axis=0)
    starts = [sum(sizes[:i]) for i in range(len(sizes))]
    full = [packed[:, at : at + size].reshape(-1, width) for at, size in zip(starts, sizes)]
    vec = jnp.concatenate(full, axis=0).astype(F32)
    vec = jnp.pad(vec, ((0, VEC_ROWS - vec.shape[0]), (0, 0)))
    result, grad_x, g_qkv, g_proj, g_expand, g_reduce, g_vec = run_block(
        flag, vec, exchange(tokens).reshape(-1, width), exchange(cotangent).reshape(-1, width),
        gather(w_qkv), gather(w_proj), gather(w_expand), gather(w_reduce),
    )

    def scatter(whole):
        return lax.psum_scatter(whole.astype(F32), axes, scatter_dimension=0, tiled=True)

    g_vec = lax.psum(g_vec, axes).reshape(-1)
    offsets = {}
    at = 0
    for name, size in zip(("ag", "as", "qv", "pb", "mg", "ms", "rb", "eb"), sizes):
        offsets[name] = lax.dynamic_slice(g_vec, (at + index * size,), (size,))
        at += size * devices
    return (
        exchange(result.reshape(tokens.shape)),
        exchange(grad_x.reshape(tokens.shape)),
        offsets["ag"],
        offsets["as"],
        scatter(g_qkv),
        offsets["qv"],
        scatter(g_proj),
        offsets["pb"],
        offsets["mg"],
        offsets["ms"],
        scatter(g_expand),
        offsets["eb"],
        scatter(g_reduce),
        offsets["rb"],
    )


def solution(mesh):
    both = ("dp", "blk")
    rows = P(None, both, None)
    vector, matrix = P(both), P(both, None)
    weights = (
        vector, vector, matrix, vector, matrix, vector, vector, vector, matrix, vector, matrix, vector,
    )
    return jax.shard_map(
        body,
        mesh=mesh,
        in_specs=(rows, P(None, "dp", None)) + weights + (rows,),
        out_specs=(rows, rows) + weights,
        check_vma=False,
    )
```

```python
import math
import typing

import jax
import jax.numpy as jnp
from jax import lax
from jax.experimental import pallas as pl
from jax.experimental.pallas import tpu as pltpu
from jax.sharding import PartitionSpec as P

HEAD_DIM = 32
LONG_IMG = 784
SHORT_IMG = 196
LANES = 128
HEADS_IN_BLOCK = LANES // HEAD_DIM
LONG_KEYS = 896
BF = jnp.bfloat16
F32 = jnp.float32
epsilon = 1e-06
LOG2E = math.log2(math.e)
SCALE = 1.0 / math.sqrt(HEAD_DIM)
MASKED = -1e30
ROWS = 256
A_GAIN, A_SHIFT, Q_BIAS, V_BIAS, P_BIAS, M_GAIN, M_SHIFT, R_BIAS, E_BIAS = range(9)
VEC_ROWS = 16
PACKED = 16
TRIO = 3 * LANES
CHUNKS = 4
Z, Y, X, C = range(4)
SPREAD = (4, 2, 2, 2)
QKV, PROJ, EXPAND, REDUCE = range(4)
GATHER_ORDER = ((X, Z, Y), (X, Z, Y), (X, Z, Y), (Z, Y, X))
SCATTER_ORDER = tuple((C,) + order[::-1] for order in GATHER_ORDER)


def nt(left, right):
    return lax.dot_general(left, right, (((1,), (1,)), ((), ())), preferred_element_type=F32)


def nn(left, right):
    return lax.dot_general(left, right, (((1,), (0,)), ((), ())), preferred_element_type=F32)


def tn(left, right):
    return lax.dot_general(left, right, (((0,), (0,)), ((), ())), preferred_element_type=F32)


def pieces(total, size):
    return [(at, min(size, total - at)) for at in range(0, total, size)]


def lanes(rows, width=LANES):
    return lax.broadcasted_iota(jnp.int32, (rows, width), 1)


def to_canonical(swapped, natural, moved):
    total = natural.shape[0]
    tail = LONG_IMG + SHORT_IMG
    moved[0:LONG_IMG] = natural[SHORT_IMG:tail]
    moved[LONG_IMG:tail] = natural[0:SHORT_IMG]
    moved[tail:total] = natural[tail:total]


def to_natural(ordered, moved):
    total = ordered.shape[0]
    tail = LONG_IMG + SHORT_IMG
    moved[SHORT_IMG:tail] = ordered[0:LONG_IMG]
    moved[0:SHORT_IMG] = ordered[LONG_IMG:tail]
    moved[tail:total] = ordered[tail:total]


def norm_parts(values):
    centered = values - jnp.mean(values, axis=-1, keepdims=True)
    inverse = lax.rsqrt(jnp.mean(centered * centered, axis=-1, keepdims=True) + epsilon)
    return centered * inverse, inverse


def norm_back(gradient, normed, inverse, gain):
    scaled = gradient * gain
    return inverse * (
        scaled
        - jnp.mean(scaled, axis=-1, keepdims=True)
        - normed * jnp.mean(scaled * normed, axis=-1, keepdims=True)
    )


def gelu_parts(values):
    size = jnp.abs(values)
    z = size * math.sqrt(0.5)
    t = 1.0 / (1.0 + 0.5 * z)
    poly = 0.17087277
    for factor in (-0.82215223, 1.48851587, -1.13520398, 0.27886807, -0.18628806, 0.09678418,
                   0.37409196, 1.00002368, -1.26551223):
        poly = poly * t + factor
    bell = jnp.exp(-z * z)
    tail = 0.5 * t * bell * jnp.exp(poly)
    phi = jnp.where(values >= 0.0, 1.0 - tail, tail)
    return values * phi, phi + values * (bell * (1.0 / math.sqrt(2.0 * math.pi)))


def fill_masks(aug_q, aug_k):
    total = aug_q.shape[0]
    row = lax.broadcasted_iota(jnp.int32, (total, LANES), 0)
    segment = (row >= LONG_IMG).astype(jnp.int32) + (row >= LONG_IMG + SHORT_IMG).astype(jnp.int32)
    place = lanes(total) % HEAD_DIM
    aug_q[...] = jnp.where(place == segment, 1.0, 0.0).astype(BF)
    aug_k[...] = jnp.where((place < 3) & (place != segment), MASKED, 0.0).astype(BF)


def attend_tiles(total, size):
    tail = total - LONG_IMG
    first = total - 2 * LANES
    return [(at, n, 0, LONG_KEYS, True, at) for at, n in pieces(LONG_IMG, size)] + [
        (LONG_IMG + at, n, first, 2 * LANES, False, at) for at, n in pieces(tail, size)
    ]


def get(ref, at, n):
    cols = pl.ds(at if isinstance(at, int) else pl.multiple_of(at, LANES), n)
    value = ref[:, cols] if len(ref.shape) == 2 else ref[:, :, :, :, :, cols]
    return value.reshape(-1, n)


def put(ref, value, at, n):
    cols = pl.ds(at if isinstance(at, int) else pl.multiple_of(at, LANES), n)
    if len(ref.shape) == 2:
        ref[:, cols] = value
    else:
        ref[:, :, :, :, :, cols] = value.reshape(ref.shape[:-1] + (n,))


def get_rows(ref, part, parts):
    if len(ref.shape) == 2:
        rows = ref.shape[0] // parts
        return ref[pl.ds(pl.multiple_of(part * rows, rows), rows)]
    each = ref.shape[0] // parts
    value = ref[pl.ds(part * each, each)]
    return value.reshape(-1, value.shape[-1])


def put_rows(ref, value, part, parts):
    if len(ref.shape) == 2:
        rows = ref.shape[0] // parts
        ref[pl.ds(pl.multiple_of(part * rows, rows), rows)] = value
    else:
        each = ref.shape[0] // parts
        ref[pl.ds(part * each, each)] = value.reshape((each,) + ref.shape[1:])


def of_block(ref, j, offset=0):
    return ref.at[:, pl.ds(pl.multiple_of(offset + j * LANES, LANES), LANES)]


def of_trio(ref, j, which):
    return ref.at[:, pl.ds(pl.multiple_of(j * TRIO + which * LANES, LANES), LANES)]


def forward_head(j, head, qkv, attended, inverse, e_long, e_tail, aug_q, aug_k, size=400):
    total, width = attended.shape
    q, k, v = (of_trio(qkv, j, i) for i in range(3))
    attended, inverse = of_block(attended, j), of_block(inverse, j)
    mine = lanes(1) // HEAD_DIM == head
    ka = jnp.where(mine, k[...], aug_k[...])
    va = jnp.where(mine, v[...], jnp.ones_like(aug_k[...]))
    at = j * HEADS_IN_BLOCK + head
    for row, rows, key, keys, is_long, place in attend_tiles(total, size):
        here = pl.ds(row, rows)
        scores = nt(jnp.where(mine, q[here], aug_q[here]), ka[key : key + keys])
        exps = jnp.exp2(scores - jnp.max(scores, axis=1, keepdims=True)).astype(BF)
        store = e_long if is_long else e_tail
        store[at, place : place + rows, :] = exps
        product = nn(exps, va[key : key + keys])
        inv = 1.0 / pltpu.roll(product, HEAD_DIM, 1)
        attended[here] = jnp.where(mine, (product * inv).astype(BF), attended[here])
        inverse[here] = jnp.where(mine, inv, inverse[here])


def backward_prepare(j, qkv, attended, inverse, d_att, scaled_b, aug_b, q_t, s_t, k_b):
    total, width = attended.shape
    for at, n in pieces(total, ROWS):
        here = pl.ds(at, n)
        scaled = of_block(d_att, j)[here].astype(F32) * of_block(inverse, j)[here]
        inner = scaled * of_block(attended, j)[here].astype(F32)
        from_group = lax.broadcasted_iota(jnp.int32, (LANES, LANES), 0) // HEAD_DIM
        to_group = lanes(LANES) // HEAD_DIM
        spread = jnp.where((from_group + 1) % HEADS_IN_BLOCK == to_group, 1.0, 0.0).astype(BF)
        high = inner.astype(BF)
        low = (inner - high.astype(F32)).astype(BF)
        sums = nn(high, spread) + nn(low, spread)
        sum_high = sums.astype(BF)
        sum_low = (sums - sum_high.astype(F32)).astype(BF)
        place = lanes(n) % HEAD_DIM
        zeros = jnp.zeros_like(sum_high)
        aug_b[here] = jnp.where(place == 0, -sum_high, jnp.where(place == 1, -sum_low, zeros))
        scaled = scaled.astype(BF)
        scaled_b[here] = scaled
        s_t[:, at : at + n] = scaled.T
        q_t[:, at : at + n] = of_trio(qkv, j, 0)[here].T
        k_b[here] = of_trio(qkv, j, 1)[here]


def backward_head(j, head, qkv, e_long, e_tail, scaled_b, aug_b, q_t, s_t, k_b, dk_t, dv_t, size=400):
    total = scaled_b.shape[0]
    dq, v = of_trio(qkv, j, 0), of_trio(qkv, j, 2)
    mine = lanes(1) // HEAD_DIM == head
    following = lanes(1) // HEAD_DIM == (head + 1) % HEADS_IN_BLOCK
    va = jnp.where(mine, v[...], jnp.ones_like(k_b[...]))
    at = j * HEADS_IN_BLOCK + head
    of_head = pl.ds(pl.multiple_of(head * HEAD_DIM, HEAD_DIM), HEAD_DIM)
    sums_of = {}
    for row, rows, key, keys, is_long, where in attend_tiles(total, size):
        here = pl.ds(row, rows)
        store = e_long if is_long else e_tail
        exps = store[at, where : where + rows, :]
        side = jnp.where(following, aug_b[here], jnp.zeros_like(aug_b[here]))
        left = jnp.where(mine, scaled_b[here], side)
        d_scores = (exps.astype(F32) * nt(left, va[key : key + keys])).astype(BF)
        dq_here = (nn(d_scores, k_b[key : key + keys]) * SCALE).astype(BF)
        dq[here] = jnp.where(mine, dq_here, dq[here])
        more_v = nn(s_t[of_head, row : row + rows], exps)
        more_k = nn(q_t[of_head, row : row + rows], d_scores)
        if is_long in sums_of:
            more_v, more_k = sums_of[is_long][0] + more_v, sums_of[is_long][1] + more_k
        sums_of[is_long] = (more_v, more_k)
    first = total - 2 * LANES
    both = LONG_KEYS - first
    for ref, which, factor in ((dv_t, 0, 1.0), (dk_t, 1, 1.0 / LOG2E)):
        long_part, tail_part = (sums_of[is_long][which] * factor for is_long in (True, False))
        ref[of_head, 0:first] = long_part[:, :first].astype(BF)
        ref[of_head, first:LONG_KEYS] = (long_part[:, first:] + tail_part[:, :both]).astype(BF)
        ref[of_head, LONG_KEYS:total] = tail_part[:, both:].astype(BF)


def all_forward(b, transfers):
    unrolled = 2

    def step(i, carried):
        for one in range(unrolled):
            at = i * unrolled + one
            forward_head(
                at // HEADS_IN_BLOCK, at % HEADS_IN_BLOCK, b.qkv, b.attended, b.inverse,
                b.e_long, b.e_tail, b.aug_q, b.aug_k,
            )
        transfers.after_forward(i)
        return carried

    lax.fori_loop(0, b.attended.shape[1] // HEAD_DIM // unrolled, step, 0)


def all_backward(b, transfers):
    total, width = b.attended.shape
    unrolled = 2
    keep = (b.scaled_b, b.aug_b, b.q_t, b.s_t, b.k_b)

    def block(j, carried):
        backward_prepare(j, b.qkv, b.attended, b.inverse, b.d_exp, *keep)

        def step(i, inside):
            for one in range(unrolled):
                backward_head(
                    j, i * unrolled + one, b.qkv, b.e_long, b.e_tail, *keep, b.dk_t, b.dv_t
                )
            return inside

        lax.fori_loop(0, HEADS_IN_BLOCK // unrolled, step, 0)
        of_trio(b.qkv, j, 1)[...] = b.dk_t[...].T
        of_trio(b.qkv, j, 2)[...] = b.dv_t[...].T
        here = pl.ds(pl.multiple_of(j * LANES, LANES), LANES)
        trio = pl.ds(pl.multiple_of(j * TRIO, LANES), TRIO)
        for row, which in ((Q_BIAS, 0), (V_BIAS, 2)):
            values = of_trio(b.qkv, j, which)[...].astype(F32)
            b.g_vec[row : row + 1, here] = jnp.sum(values, axis=0, keepdims=True)

        def rows_of(i, inside):
            rows = pl.ds(pl.multiple_of(i * ROWS, ROWS), ROWS)
            b.acc_b[rows] = b.acc_b[rows] + nt(b.qkv[rows, trio], get(b.w_qkv, j * TRIO, TRIO))
            return inside

        lax.fori_loop(0, total // ROWS, rows_of, 0)
        put(b.w_qkv, tn(b.x_in[...], b.qkv[:, trio]).astype(BF), j * TRIO, TRIO)
        transfers.after_backward(j)
        return carried

    lax.fori_loop(0, width // LANES, block, 0)


class Buffers(typing.NamedTuple):
    x_in: typing.Any
    cot: typing.Any
    xc: typing.Any
    qkv: typing.Any
    attended: typing.Any
    inverse: typing.Any
    e_long: typing.Any
    e_tail: typing.Any
    aug_q: typing.Any
    aug_k: typing.Any
    middle: typing.Any
    acc_a: typing.Any
    acc_b: typing.Any
    hb: typing.Any
    act: typing.Any
    d_exp: typing.Any
    scaled_b: typing.Any
    aug_b: typing.Any
    q_t: typing.Any
    s_t: typing.Any
    k_b: typing.Any
    dk_t: typing.Any
    dv_t: typing.Any
    vec: typing.Any
    g_vec: typing.Any
    w_qkv: typing.Any
    w_proj: typing.Any
    w_expand: typing.Any
    w_reduce: typing.Any


def buffers(total, width, weights):
    heads = width // HEAD_DIM
    rows, lane, turned = (total, width), (total, LANES), (LANES, total)
    shapes = Buffers(
        x_in=(rows, BF),
        cot=(rows, BF),
        xc=(rows, BF),
        qkv=((total, 3 * width), BF),
        attended=(rows, BF),
        inverse=(rows, F32),
        e_long=((heads, LONG_IMG, LONG_KEYS), BF),
        e_tail=((heads, total - LONG_IMG, 2 * LANES), BF),
        aug_q=(lane, BF),
        aug_k=(lane, BF),
        middle=(rows, F32),
        acc_a=(rows, F32),
        acc_b=(rows, F32),
        hb=(rows, BF),
        act=(rows, BF),
        d_exp=(rows, BF),
        scaled_b=(lane, BF),
        aug_b=(lane, BF),
        q_t=(turned, BF),
        s_t=(turned, BF),
        k_b=(lane, BF),
        dk_t=(turned, BF),
        dv_t=(turned, BF),
        vec=((VEC_ROWS, width), F32),
        g_vec=((VEC_ROWS, width), F32),
        w_qkv=(weights[QKV], BF),
        w_proj=(weights[PROJ], BF),
        w_expand=(weights[EXPAND], BF),
        w_reduce=(weights[REDUCE], BF),
    )
    return [pltpu.VMEM(*one) for one in shapes]


def compute(b, first_length, transfers):
    total, width = b.xc.shape
    ff = b.w_expand.shape[-1]
    swapped = jnp.full((1, width), first_length, jnp.int32) == SHORT_IMG
    acc_a, acc_b, vec, g_vec = b.acc_a, b.acc_b, b.vec, b.g_vec

    def by_rows(function):
        def step(i, carried):
            function(pl.ds(pl.multiple_of(i * ROWS, ROWS), ROWS))
            return carried

        lax.fori_loop(0, total // ROWS, step, 0)

    def vector(row):
        return vec[pl.ds(row, 1), :]

    def add_sum(row, values):
        g_vec[pl.ds(row, 1), :] = g_vec[pl.ds(row, 1), :] + jnp.sum(values, axis=0, keepdims=True)

    def load(source):
        @by_rows
        def _(rows):
            acc_a[rows] = source[rows].astype(F32)

        to_canonical(swapped, acc_a, acc_b)

    def loaded(rows):
        return jnp.where(swapped, acc_b[rows], acc_a[rows])

    def unload(values, moved, target):
        to_natural(values, moved)

        @by_rows
        def _(rows):
            target[rows] = jnp.where(swapped, moved[rows], values[rows]).astype(BF)

    transfers.begin()
    g_vec[...] = jnp.zeros_like(g_vec)
    fill_masks(b.aug_q, b.aug_k)
    transfers.need_tokens()
    load(b.x_in)

    @by_rows
    def _(rows):
        values = loaded(rows)
        b.xc[rows] = values.astype(BF)
        acc_a[rows], _ = norm_parts(values)

    transfers.need_qkv()
    ha, qkv, w_qkv = b.x_in, b.qkv, b.w_qkv

    @by_rows
    def _(rows):
        lowered = (acc_a[rows] * vector(A_GAIN) + vector(A_SHIFT)).astype(BF)
        ha[rows] = lowered
        projected = nn(lowered, get(w_qkv, 0, 3 * width))
        for j in range(width // LANES):
            here = slice(j * LANES, (j + 1) * LANES)
            q, k, v = (projected[:, j * TRIO + i * LANES : j * TRIO + (i + 1) * LANES] for i in range(3))
            q = (q + vec[Q_BIAS : Q_BIAS + 1, here]) * (SCALE * LOG2E)
            v = v + vec[V_BIAS : V_BIAS + 1, here]
            for i, value in enumerate((q, k, v)):
                qkv[rows, j * TRIO + i * LANES : j * TRIO + (i + 1) * LANES] = value.astype(BF)

    transfers.forward()
    all_forward(b, transfers)

    transfers.need_cotangent()
    cot, middle, hb, act, d_exp, attended = b.cot, b.middle, b.hb, b.act, b.d_exp, b.attended
    w_proj, w_expand, w_reduce = b.w_proj, b.w_expand, b.w_reduce
    load(cot)

    @by_rows
    def _(rows):
        cot[rows] = loaded(rows).astype(BF)

    transfers.need_proj()

    @by_rows
    def _(rows):
        mid = b.xc[rows].astype(F32) + (nn(attended[rows], get(w_proj, 0, width)) + vector(P_BIAS))
        middle[rows] = mid
        normed, _ = norm_parts(mid)
        hb[rows] = (normed * vector(M_GAIN) + vector(M_SHIFT)).astype(BF)
        acc_a[rows] = mid + vector(R_BIAS)
        acc_b[rows] = jnp.zeros_like(mid)
        add_sum(R_BIAS, cot[rows].astype(F32))

    transfers.need_mlp()
    parts = ff // width

    def one_part(part, carried):
        for at, n in pieces(total, ROWS):
            rows = slice(at, at + n)
            w_in, w_out = get(w_expand, part * width, width), get_rows(w_reduce, part, parts)
            value, slope = gelu_parts(nn(hb[rows], w_in) + vector(E_BIAS + part))
            low = value.astype(BF)
            act[rows] = low
            acc_a[rows] = acc_a[rows] + nn(low, w_out)
            d_low = (nt(cot[rows], w_out) * slope).astype(BF)
            d_exp[rows] = d_low
            acc_b[rows] = acc_b[rows] + nt(d_low, w_in)
            add_sum(E_BIAS + part, d_low.astype(F32))
        put_rows(w_reduce, tn(act[...], cot[...]).astype(BF), part, parts)
        put(w_expand, tn(hb[...], d_exp[...]).astype(BF), part * width, width)
        transfers.after_part(part)
        return carried

    lax.fori_loop(0, parts, one_part, 0)

    d_att = d_exp

    @by_rows
    def _(rows):
        gradient = acc_b[rows]
        normed, inv = norm_parts(middle[rows])
        d_mid = cot[rows].astype(F32) + norm_back(gradient, normed, inv, vector(M_GAIN))
        add_sum(M_GAIN, gradient * normed)
        add_sum(M_SHIFT, gradient)
        middle[rows] = d_mid
        d_branch = d_mid.astype(BF)
        act[rows] = d_branch
        add_sum(P_BIAS, d_branch.astype(F32))
        d_att[rows] = nt(d_branch, get(w_proj, 0, width)).astype(BF)

    put(w_proj, tn(attended[...], act[...]).astype(BF), 0, width)
    transfers.have_proj()
    unload(acc_a, acc_b, hb)
    transfers.have_result()
    acc_b[...] = jnp.zeros_like(acc_b)
    all_backward(b, transfers)

    @by_rows
    def _(rows):
        gradient = acc_b[rows]
        normed, inv = norm_parts(b.xc[rows].astype(F32))
        add_sum(A_GAIN, gradient * normed)
        add_sum(A_SHIFT, gradient)
        acc_a[rows] = middle[rows] + norm_back(gradient, normed, inv, vector(A_GAIN))

    transfers.have_vectors()
    unload(acc_a, acc_b, act)
    transfers.have_grad()


class Local:
    def __init__(self, b, ins, outs, sems):
        self.b, self.outs = b, outs
        targets = (b.x_in, b.cot) + tuple(b[-4:])
        self.loads = [pltpu.make_async_copy(one, target, sems.at[i]) for i, (one, target) in enumerate(zip(ins, targets))]
        sources = (b.hb, b.act) + tuple(b[-4:])
        self.stores = [pltpu.make_async_copy(one, out, sems.at[6 + i]) for i, (one, out) in enumerate(zip(sources, outs))]

    def begin(self):
        for copy in self.loads:
            copy.start()

    def need_tokens(self):
        self.loads[0].wait()

    def need_qkv(self):
        self.loads[2 + QKV].wait()

    def forward(self):
        pass

    def after_forward(self, i):
        pass

    def need_cotangent(self):
        self.loads[1].wait()

    def need_proj(self):
        self.loads[2 + PROJ].wait()

    def need_mlp(self):
        self.loads[2 + EXPAND].wait()
        self.loads[2 + REDUCE].wait()

    def after_part(self, part):
        pass

    def have_proj(self):
        for which in (PROJ, EXPAND, REDUCE):
            self.stores[2 + which].start()

    def have_result(self):
        self.stores[0].start()

    def after_backward(self, j):
        pass

    def have_vectors(self):
        self.stores[2 + QKV].start()

    def have_grad(self):
        self.stores[1].start()
        for copy in self.stores:
            copy.wait()


def local_kernel(lengths, vec, x_in, cot_in, w_qkv, w_proj, w_expand, w_reduce,
                 result, grad_x, g_qkv, g_proj, g_expand, g_reduce, g_vec, *scratch):
    b = Buffers(*scratch[:-1])
    b.vec[...] = vec[...]
    ins = (x_in, cot_in, w_qkv, w_proj, w_expand, w_reduce)
    outs = (result, grad_x, g_qkv, g_proj, g_expand, g_reduce)
    compute(b, lengths[lax.axis_index("blk"), 0, 0], Local(b, ins, outs, scratch[-1]))
    g_vec[...] = b.g_vec[...]


def run_local(lengths, vec, x_in, cot_in, weights):
    vmem, anywhere = pl.BlockSpec(memory_space=pltpu.VMEM), pl.BlockSpec(memory_space=pl.ANY)
    total, width = x_in.shape
    like = (x_in, x_in) + tuple(weights)
    return pl.pallas_call(
        local_kernel,
        out_shape=[jax.ShapeDtypeStruct(one.shape, BF) for one in like]
        + [jax.ShapeDtypeStruct((VEC_ROWS, width), F32)],
        in_specs=[pl.BlockSpec(memory_space=pltpu.SMEM), vmem] + [anywhere] * 6,
        out_specs=[anywhere] * 6 + [vmem],
        scratch_shapes=buffers(total, width, [one.shape for one in weights]) + [pltpu.SemaphoreType.DMA((12,))],
        compiler_params=pltpu.CompilerParams(vmem_limit_bytes=62 * 2**20),
    )(lengths, vec, x_in, cot_in, *weights)


UNITS = (
    (QKV, 0, 2 * TRIO), (QKV, 2 * TRIO, 2 * TRIO + LANES), (PROJ, 0, 6 * LANES),
    (EXPAND, 0, 8 * LANES), (EXPAND, 8 * LANES, 8 * LANES), (REDUCE, 0, 2 * LANES), (REDUCE, 2 * LANES, 2 * LANES),
)
EARLY_UNITS, PROJ_UNITS, EXPAND_UNITS, REDUCE_UNITS = (0, 1), (2,), (3, 4), (5, 6)
VECTOR_TILES = ((QKV, 4 * TRIO), (PROJ, 4 * LANES), (PROJ, 5 * LANES))


class Group:
    def __init__(self, b, ins, outs, scratch):
        self.b = b
        self.tokens, self.cotangent, self.vectors, self.shards = ins
        self.result, self.grad_x, self.outs, self.g_total = outs
        (self.own_qkv, self.own_vec, self.packed, self.turn, self.arrived, self.v_two, self.v_z,
         self.local_sem, self.token_sem, self.ag_sem, self.rs_sem, self.v_sem) = scratch
        self.weights = tuple(b[-4:])
        dp, blk = lax.axis_index("dp"), lax.axis_index("blk")
        z, y, x, c = dp // SPREAD[Y], dp % SPREAD[Y], blk // SPREAD[C], blk % SPREAD[C]
        self.mine = (z, y, x, c)
        self.index = dp * (SPREAD[X] * SPREAD[C]) + blk
        self.blk = blk
        n_blk = SPREAD[X] * SPREAD[C]
        self.others = [(dp, (blk + k) % n_blk) for k in range(1, n_blk)]
        z_places = [(z + k) % SPREAD[Z] for k in range(1, SPREAD[Z])]
        self.along = (
            [((place * SPREAD[Y] + y, blk), place) for place in z_places],
            [((dp + 1 - 2 * y, blk), 1 - y)],
            [((dp, blk + SPREAD[C] * (1 - 2 * x)), 1 - x)],
            [((dp, blk + 1 - 2 * c), 1 - c)],
        )
        height = self.tokens.shape[1]

        def rows(ref):
            return lambda i: ref.at[pl.ds(pl.multiple_of(i * height, height), height)]

        def part(ref):
            return lambda i: ref.at[i]

        moves = (
            (part(self.tokens), rows(b.x_in)),
            (part(self.cotangent), rows(b.cot)),
            (rows(b.hb), part(self.result)),
            (rows(b.act), part(self.grad_x)),
        )
        self.swaps = [
            [
                self.remote(source(device[1]), target(blk), self.token_sem.at[i, k], self.token_sem.at[4 + i, k], device)
                for k, device in enumerate(self.others)
            ]
            for i, (source, target) in enumerate(moves)
        ]
        self.kept = [
            pltpu.make_async_copy(source(blk), target(blk), self.local_sem.at[i])
            for i, (source, target) in enumerate(moves)
        ]

    @staticmethod
    def remote(source, target, send, recv, device):
        return pltpu.make_async_remote_copy(
            src_ref=source, dst_ref=target, send_sem=send, recv_sem=recv,
            device_id=device, device_id_type=pl.DeviceIdType.MESH,
        )

    @staticmethod
    def start(copies):
        for copy in copies:
            copy.start()

    @staticmethod
    def arrive(copies):
        for copy in copies:
            copy.wait_recv()

    @staticmethod
    def sent(copies):
        for copy in copies:
            copy.wait_send()

    def place(self, free, at=None):
        index = [slice(None) if axis in free else self.mine[axis] for axis in range(4)]
        for axis, value in (at or {}).items():
            index[axis] = value
        return tuple(index)


    def gather(self, unit, stage):
        which, first, columns = UNITS[unit]
        w, order = self.weights[which], GATHER_ORDER[which]
        cols = (slice(None), pl.ds(first, columns))

        def one(i, view, device):
            return self.remote(view, view, self.ag_sem.at[0, unit, i], self.ag_sem.at[1, unit, i], device)

        if stage < 3:
            view = w.at[self.place(order[:stage]) + cols]
            return [one(3 * stage + k, view, device) for k, (device, _) in enumerate(self.along[order[stage]])]
        device, _ = self.along[C][0]
        last = order[2]
        if stage == 3:
            return [one(9, w.at[self.place(order[:2]) + cols], device)]
        (_, other), = self.along[last]
        return [one(10, w.at[self.place(order[:2], {last: other}) + cols], device)]

    def gather_on(self, units, stage):
        for unit in units:
            copies = self.gather(unit, stage)
            self.arrive(copies)
            self.sent(copies)
            if stage < 2:
                self.start(self.gather(unit, stage + 1))
            if stage in (1, 2):
                self.start(self.gather(unit, stage + 2))

    def gathered(self, units):
        for unit in units:
            for stage in (3, 4):
                copies = self.gather(unit, stage)
                self.arrive(copies)
                self.sent(copies)

    def unpack(self, tile):
        which, first = VECTOR_TILES[tile]
        w = self.weights[which]
        all_of = w[:, :, :, :, 0:PACKED, first : first + LANES].astype(F32)
        total = jnp.sum(all_of.reshape(-1, PACKED, LANES), axis=0)
        for i in range(PACKED):
            row, at = divmod(tile * PACKED + i, 4)
            self.b.vec[row : row + 1, at * LANES : (at + 1) * LANES] = total[i : i + 1, :]


    def chunk_view(self, which, chunk):
        if which == REDUCE:
            return chunk, slice(None)
        columns = (TRIO, 4 * LANES, 4 * LANES)[which]
        return None, pl.ds(pl.multiple_of(chunk * columns, LANES), columns)

    def scatter(self, which, stage, chunk):
        w, order = self.weights[which], SCATTER_ORDER[which]
        axis, rest = order[stage], order[stage + 1 :]
        buffer = self.arrived[which][stage]
        at_z, cols = self.chunk_view(which, chunk)
        copies = []
        for k, (device, other) in enumerate(self.along[axis]):
            at = {axis: other}
            if at_z is not None and Z in rest:
                at[Z] = at_z
            source = w.at[self.place(rest, at) + (slice(None), cols)]
            sems = (self.rs_sem.at[i, which, chunk, 3 * stage + k] for i in range(2))
            copies.append(self.remote(source, buffer.at[self.landing(axis, rest, at_z, cols, k)], *sems, device))
        return copies

    @staticmethod
    def landing(axis, rest, at_z, cols, k):
        lead = (k,) if axis == Z else ()
        free = tuple(at_z if one == Z and at_z is not None else slice(None) for one in sorted(rest))
        return lead + free + (slice(None), cols)

    def scatter_on(self, which, stage, chunk):
        w, order = self.weights[which], SCATTER_ORDER[which]
        copies = self.scatter(which, stage, chunk)
        self.arrive(copies)
        axis, rest = order[stage], order[stage + 1 :]
        buffer = self.arrived[which][stage]
        at_z, cols = self.chunk_view(which, chunk)
        at = {Z: at_z} if at_z is not None and Z in rest else None
        here = self.place(rest, at) + (slice(None), cols)
        terms = [buffer[self.landing(axis, rest, at_z, cols, k)] for k in range(len(copies))]
        if not rest:
            total = w[here].astype(F32)
            for term in terms:
                total = total + term.astype(F32)
            self.keep(which, chunk, total)
        elif len(terms) == 1:
            w[here] = w[here] + terms[0]
        else:
            total = w[here].astype(F32)
            for term in terms:
                total = total + term.astype(F32)
            w[here] = total.astype(BF)
        if rest and not (which == REDUCE and rest == (Z,)):
            self.start(self.scatter(which, stage + 1, chunk))
        self.sent(copies)

    def keep(self, which, chunk, total):
        out = self.outs[which]
        if which == QKV:
            width = out.shape[1] // 3
            for i in range(3):
                cols = pl.ds(pl.multiple_of(i * width + chunk * LANES, LANES), LANES)
                out[:, cols] = total[:, i * LANES : (i + 1) * LANES]
        else:
            _, cols = self.chunk_view(which, chunk)
            out[:, cols] = total

    def tick(self, which, t, stages):
        if isinstance(t, int):
            if t < CHUNKS:
                self.start(self.scatter(which, 0, t))
            for stage in range(stages):
                if 0 <= t - stage - 1 < CHUNKS:
                    self.scatter_on(which, stage, t - stage - 1)
            return
        self.start(self.scatter(which, 0, t))
        for stage in range(min(stages, CHUNKS - 1)):
            pl.when(t >= stage + 1)(lambda stage=stage: self.scatter_on(which, stage, t - stage - 1))


    def vector_copies(self, stage):
        axis = (C, Y, X, Z)[stage]
        return [
            self.remote(
                self.b.g_vec, self.v_z.at[k] if axis == Z else self.v_two.at[stage],
                self.v_sem.at[0, 3 * stage + k], self.v_sem.at[1, 3 * stage + k], device,
            )
            for k, (device, _) in enumerate(self.along[axis])
        ]

    def vectors_on(self, stage):
        copies = self.vector_copies(stage)
        self.arrive(copies)
        self.sent(copies)
        g_vec = self.b.g_vec
        if stage < 3:
            g_vec[...] = g_vec[...] + self.v_two[stage]
            self.start(self.vector_copies(stage + 1))
        else:
            self.g_total[...] = g_vec[...] + jnp.sum(self.v_z[...], axis=0)


    def begin(self):
        barrier = pltpu.get_barrier_semaphore()
        peers = self.others + [device for axis in (Y, Z) for device, _ in self.along[axis]]
        for device in peers:
            pl.semaphore_signal(barrier, inc=1, device_id=device, device_id_type=pl.DeviceIdType.MESH)
        count = len(self.vectors)
        loads = [
            pltpu.make_async_copy(one, target, self.local_sem.at[4 + i])
            for i, (one, target) in enumerate(zip(self.vectors, self.own_vec))
        ]
        loads.append(pltpu.make_async_copy(self.shards[QKV], self.own_qkv, self.local_sem.at[4 + count]))
        width = self.shards[PROJ].shape[1]
        slots = [self.weights[which].at[self.mine] for which in range(4)]
        self.own = [
            pltpu.make_async_copy(
                self.shards[which], slots[which].at[:, pl.ds(0, self.shards[which].shape[1])],
                self.local_sem.at[4 + count + which],
            )
            for which in (PROJ, EXPAND, REDUCE)
        ]
        self.start(loads + self.own + self.kept[:2])
        self.packed[...] = jnp.zeros_like(self.packed)
        row = 0
        for load, own in zip(loads, self.own_vec):
            load.wait()
            size = own.shape[0]
            self.turn[...] = jnp.zeros_like(self.turn)
            self.turn[0:1, 0:size] = own[...].astype(F32).reshape(1, size)
            at = self.index * size
            self.packed[pl.ds(row + at // LANES, 1), :] = pltpu.roll(self.turn[...], at % LANES, 1)[0:1, :]
            row += math.prod(SPREAD) * size // LANES
        loads[-1].wait()
        w = self.weights[QKV]
        for j in range(width // LANES):
            for i in range(3):
                to = j * TRIO + i * LANES
                w[self.mine + (slice(None), pl.ds(to, LANES))] = self.own_qkv[:, i * width + j * LANES : i * width + (j + 1) * LANES]
        for tile, (which, first) in enumerate(VECTOR_TILES):
            values = self.packed[tile * PACKED : (tile + 1) * PACKED, :].astype(BF)
            self.weights[which][self.mine + (slice(None), pl.ds(first, LANES))] = values
        pl.semaphore_wait(barrier, len(peers))
        for unit in EARLY_UNITS:
            self.start(self.gather(unit, 0))
        self.start(self.swaps[0])
        for copy in self.own:
            copy.wait()

    def need_tokens(self):
        self.gather_on(EARLY_UNITS, 0)
        for unit in PROJ_UNITS + EXPAND_UNITS:
            self.start(self.gather(unit, 0))
        self.gather_on(EARLY_UNITS, 1)
        for unit in REDUCE_UNITS:
            self.start(self.gather(unit, 0))
        self.gather_on(PROJ_UNITS + EXPAND_UNITS, 0)
        self.kept[0].wait()
        self.arrive(self.swaps[0])
        self.sent(self.swaps[0])
        self.start(self.swaps[1])

    def need_qkv(self):
        self.gather_on(EARLY_UNITS, 2)
        self.gathered(EARLY_UNITS)
        self.unpack(0)

    def forward(self):
        pass

    def after_forward(self, i):
        steps = {
            0: lambda: self.gather_on(REDUCE_UNITS, 0),
            1: lambda: self.gather_on(PROJ_UNITS, 1),
            2: lambda: self.gather_on(REDUCE_UNITS, 1),
            3: lambda: (self.gather_on(EXPAND_UNITS[:1], 1), self.gather_on(PROJ_UNITS, 2)),
            4: lambda: self.gather_on(EXPAND_UNITS[1:], 1),
            5: lambda: self.gather_on(REDUCE_UNITS, 2),
            6: lambda: self.gather_on(EXPAND_UNITS[:1], 2),
            7: lambda: self.gather_on(EXPAND_UNITS[1:], 2),
        }
        for at, step in steps.items():
            pl.when(i == at)(lambda step=step: [step(), None][1])

    def need_cotangent(self):
        self.kept[1].wait()
        self.arrive(self.swaps[1])
        self.sent(self.swaps[1])

    def need_proj(self):
        self.gathered(PROJ_UNITS)
        self.unpack(1)
        self.unpack(2)

    def need_mlp(self):
        self.gathered(EXPAND_UNITS + REDUCE_UNITS)

    def after_part(self, part):
        self.tick(REDUCE, part, 3)
        self.tick(EXPAND, part, 4)

    def have_proj(self):
        self.start(self.scatter(PROJ, 0, 0))
        self.tick(REDUCE, CHUNKS, 3)
        self.tick(EXPAND, CHUNKS, 4)

    def have_result(self):
        self.start(self.swaps[2] + self.kept[2:3])

    def after_backward(self, j):
        self.tick(QKV, j, 4)

        def step(at):
            self.scatter_on(PROJ, at, 0)
            t = CHUNKS + 1 + at
            if t < CHUNKS + 3:
                self.tick(REDUCE, t, 3)
            elif t == CHUNKS + 3:
                self.start(self.scatter(REDUCE, 3, 0))
            else:
                self.scatter_on(REDUCE, 3, 0)
            if t < CHUNKS + 4:
                self.tick(EXPAND, t, 4)

        for at in range(CHUNKS):
            pl.when(j == at)(lambda at=at: step(at))

    def have_vectors(self):
        self.start(self.vector_copies(0))
        self.tick(QKV, CHUNKS, 4)

    def have_grad(self):
        self.start(self.swaps[3] + self.kept[3:4])
        for stage in range(3):
            self.vectors_on(stage)
            self.tick(QKV, CHUNKS + 1 + stage, 4)
        self.vectors_on(3)
        for i in (2, 3):
            self.kept[i].wait()
            self.arrive(self.swaps[i])
            self.sent(self.swaps[i])


N_VECTORS = 8


def group_kernel(*refs):
    refs = list(refs)

    def take(n):
        taken = refs[:n]
        del refs[:n]
        return taken

    (lengths,), vectors, (tokens, cotangent), shards = take(1), take(N_VECTORS), take(2), take(4)
    (result, grad_x), outs, (g_total,) = take(2), take(4), take(1)
    b = Buffers(*take(len(Buffers._fields)))
    (own_qkv,), own_vec, (packed, turn) = take(1), take(N_VECTORS), take(2)
    arrived = [take(4) for _ in range(4)]
    scratch = [own_qkv, own_vec, packed, turn, arrived] + refs
    group = Group(b, (tokens, cotangent, vectors, shards), (result, grad_x, outs, g_total), scratch)
    compute(b, lengths[lax.axis_index("blk"), 0, 0], group)


def run_group(lengths, vectors, tokens, cotangent, weights):
    vmem, anywhere = pl.BlockSpec(memory_space=pltpu.VMEM), pl.BlockSpec(memory_space=pl.ANY)
    blk, height, width = tokens.shape
    extra = [0] * 4
    for which, _ in VECTOR_TILES:
        extra[which] += LANES
    shapes = [SPREAD + (one.shape[0], one.shape[1] + more) for one, more in zip(weights, extra)]
    landing = []
    for which, shape in enumerate(shapes):
        for stage, axis in enumerate(SCATTER_ORDER[which]):
            rest = sorted(SCATTER_ORDER[which][stage + 1 :])
            lead = (SPREAD[Z] - 1,) if axis == Z else ()
            landing.append(pltpu.VMEM(lead + tuple(SPREAD[one] for one in rest) + weights[which].shape, BF))
    sums = (VEC_ROWS, width)
    packed_rows = math.prod(SPREAD) * sum(one.shape[0] for one in vectors) // LANES
    dma = pltpu.SemaphoreType.DMA
    return pl.pallas_call(
        group_kernel,
        out_shape=[jax.ShapeDtypeStruct(tokens.shape, BF)] * 2
        + [jax.ShapeDtypeStruct(one.shape, F32) for one in weights]
        + [jax.ShapeDtypeStruct(sums, F32)],
        in_specs=[pl.BlockSpec(memory_space=pltpu.SMEM)] + [anywhere] * (N_VECTORS + 6),
        out_specs=[anywhere] * 2 + [vmem] * 5,
        scratch_shapes=buffers(blk * height, width, shapes)
        + [pltpu.VMEM(weights[QKV].shape, BF)]
        + [pltpu.VMEM(one.shape, BF) for one in vectors]
        + [pltpu.VMEM((packed_rows, LANES), F32), pltpu.VMEM((8, LANES), F32)]
        + landing
        + [pltpu.VMEM((3,) + sums, F32), pltpu.VMEM((SPREAD[Z] - 1,) + sums, F32)]
        + [dma((16,)), dma((8, 3)), dma((2, len(UNITS), 11)), dma((2, 4, CHUNKS, 12)), dma((2, 12))],
        compiler_params=pltpu.CompilerParams(
            vmem_limit_bytes=62 * 2**20, collective_id=0, has_side_effects=True
        ),
    )(lengths, *vectors, tokens, cotangent, *weights)


def finish_kernel(result, grad_x, g_qkv, g_proj, g_expand, g_reduce, g_vec, *refs):
    sources = (result, grad_x, g_qkv, g_proj, g_expand, g_reduce)
    outs, refs = refs[: 6 + N_VECTORS], refs[6 + N_VECTORS :]
    held, short = refs[:6], refs[6 : 6 + N_VECTORS]
    turn, lines, sems = refs[6 + N_VECTORS :]
    loads = [pltpu.make_async_copy(one, to, sems.at[i]) for i, (one, to) in enumerate(zip(sources, held))]
    stores = [pltpu.make_async_copy(one, to, sems.at[6 + i]) for i, (one, to) in enumerate(zip(held, outs))]
    for load in loads:
        load.start()
    index = lax.axis_index("dp") * lax.axis_size("blk") + lax.axis_index("blk")
    devices = lax.axis_size("dp") * lax.axis_size("blk")
    width = g_vec.shape[1]
    parts = width // LANES
    for i in range(g_vec.shape[0]):
        for part in range(parts):
            lines[i * parts + part : i * parts + part + 1, :] = g_vec[i : i + 1, part * LANES : (part + 1) * LANES]
    row = 0
    for i, one in enumerate(short):
        size = one.shape[0]
        at = index * size
        turn[0:1, :] = lines[pl.ds(row + at // LANES, 1), :]
        turned = pltpu.roll(turn[...], (LANES - at % LANES) % LANES, 1)
        one[...] = turned[0:1, 0:size].reshape(size)
        stores.append(pltpu.make_async_copy(one, outs[6 + i], sems.at[12 + i]))
        stores[-1].start()
        row += devices * size // LANES
    for load, store in zip(loads, stores):
        load.wait()
        store.start()
    for store in stores:
        store.wait()


def finish(values, sizes):
    vmem, anywhere = pl.BlockSpec(memory_space=pltpu.VMEM), pl.BlockSpec(memory_space=pl.ANY)
    long = [(one.shape, one.dtype) for one in values[:6]]
    short = [((size,), F32) for size in sizes]
    return pl.pallas_call(
        finish_kernel,
        out_shape=[jax.ShapeDtypeStruct(*one) for one in long + short],
        in_specs=[anywhere] * 6 + [vmem],
        out_specs=[anywhere] * (6 + len(sizes)),
        scratch_shapes=[pltpu.VMEM(*one) for one in long + short]
        + [pltpu.VMEM((8, LANES), F32), pltpu.VMEM((values[6].size // LANES, LANES), F32)]
        + [pltpu.SemaphoreType.DMA((12 + len(sizes),))],
    )(*values)


def by_collectives(lengths, vectors, sizes, tokens, cotangent, weights):
    axes = ("dp", "blk")
    width = tokens.shape[2]
    blocks = width // LANES

    def exchange(rows):
        return lax.all_to_all(rows.reshape(tokens.shape), "blk", 0, 0, tiled=True)

    packed = lax.all_gather(jnp.concatenate(vectors), axes, axis=0)
    starts = [sum(sizes[:i]) for i in range(len(sizes))]
    full = [packed[:, at : at + size].reshape(-1, width) for at, size in zip(starts, sizes)]
    vec = jnp.concatenate(full, axis=0).astype(F32)
    vec = jnp.pad(vec, ((0, VEC_ROWS - vec.shape[0]), (0, 0)))
    whole = [lax.all_gather(one, axes, axis=0, tiled=True) for one in weights]
    whole[QKV] = whole[QKV].reshape(width, 3, blocks, LANES).swapaxes(1, 2).reshape(width, 3 * width)
    result, grad_x, *grads, g_vec = run_local(
        lengths, vec, exchange(tokens).reshape(-1, width), exchange(cotangent).reshape(-1, width), whole
    )
    grads[QKV] = grads[QKV].reshape(width, blocks, 3, LANES).swapaxes(1, 2).reshape(width, 3 * width)
    grads = [lax.psum_scatter(one.astype(F32), axes, scatter_dimension=0, tiled=True) for one in grads]
    g_vec = lax.psum(g_vec, axes).reshape(-1)
    index = lax.axis_index(axes)
    devices = lax.axis_size(axes)
    own = [
        lax.dynamic_slice(g_vec, (devices * at + index * size,), (size,)) for at, size in zip(starts, sizes)
    ]
    return (exchange(result), exchange(grad_x), *grads, *own)


def body(
    tokens, lengths, attn_gain, attn_shift, w_qkv, qv_bias, w_proj, proj_bias,
    mlp_gain, mlp_shift, w_expand, expand_bias, w_reduce, reduce_bias, cotangent,
):
    vectors = (attn_gain, attn_shift, qv_bias, proj_bias, mlp_gain, mlp_shift, reduce_bias, expand_bias)
    sizes = [one.shape[0] for one in vectors]
    weights = (w_qkv, w_proj, w_expand, w_reduce)
    sized = (lax.axis_size("dp"), lax.axis_size("blk")) == (SPREAD[Z] * SPREAD[Y], SPREAD[X] * SPREAD[C])
    if sized and all(one.shape[0] % 16 == 0 for one in weights):
        outs = finish(run_group(lengths, vectors, tokens, cotangent, weights), sizes)
    else:
        outs = by_collectives(lengths, vectors, sizes, tokens, cotangent, weights)
    result, grad_x, g_qkv, g_proj, g_expand, g_reduce, ag, as_, qv, pb, mg, ms, rb, eb = outs
    return (result, grad_x, ag, as_, g_qkv, qv, g_proj, pb, mg, ms, g_expand, eb, g_reduce, rb)


def solution(mesh):
    both = ("dp", "blk")
    rows = P(None, both, None)
    vector, matrix = P(both), P(both, None)
    weights = (
        vector, vector, matrix, vector, matrix, vector, vector, vector, matrix, vector, matrix, vector,
    )
    return jax.shard_map(
        body,
        mesh=mesh,
        in_specs=(rows, P(None, "dp", None)) + weights + (rows,),
        out_specs=(rows, rows) + weights,
        check_vma=False,
    )
```

```python
import math
import typing

import jax
import jax.numpy as jnp
from jax import lax
from jax.experimental import pallas as pl
from jax.experimental.pallas import tpu as pltpu
from jax.sharding import PartitionSpec as P

HEAD_DIM = 32
LONG_IMG = 784
SHORT_IMG = 196
LANES = 128
HEADS_IN_BLOCK = LANES // HEAD_DIM
LONG_KEYS = 896
BF = jnp.bfloat16
F32 = jnp.float32
epsilon = 1e-06
LOG2E = math.log2(math.e)
SCALE = 1.0 / math.sqrt(HEAD_DIM)
MASKED = -1e30
ROWS = 512
A_GAIN, A_SHIFT, Q_BIAS, V_BIAS, P_BIAS, M_GAIN, M_SHIFT, R_BIAS, E_BIAS = range(9)
VEC_ROWS = 16
PACKED = 16
TRIO = 3 * LANES
CHUNKS = 4
Z, Y, X, C = range(4)
SPREAD = (4, 2, 2, 2)
QKV, PROJ, EXPAND, REDUCE = range(4)
GATHER_ORDER = ((X, Z, Y), (X, Z, Y), (X, Z, Y), (Z, Y, X))
SCATTER_ORDER = tuple((C,) + order[::-1] for order in GATHER_ORDER)


def copies_before(order, stage):
    return sum(SPREAD[axis] - 1 for axis in order[:stage])


def nt(left, right):
    return lax.dot_general(left, right, (((1,), (1,)), ((), ())), preferred_element_type=F32)


def nn(left, right):
    return lax.dot_general(left, right, (((1,), (0,)), ((), ())), preferred_element_type=F32)


def tn(left, right):
    return lax.dot_general(left, right, (((0,), (0,)), ((), ())), preferred_element_type=F32)


def pieces(total, size):
    return [(at, min(size, total - at)) for at in range(0, total, size)]


def lanes(rows, width=LANES):
    return lax.broadcasted_iota(jnp.int32, (rows, width), 1)


def to_canonical(swapped, natural, moved):
    total = natural.shape[0]
    tail = LONG_IMG + SHORT_IMG
    moved[0:LONG_IMG] = natural[SHORT_IMG:tail]
    moved[LONG_IMG:tail] = natural[0:SHORT_IMG]
    moved[tail:total] = natural[tail:total]


def to_natural(ordered, moved):
    total = ordered.shape[0]
    tail = LONG_IMG + SHORT_IMG
    moved[SHORT_IMG:tail] = ordered[0:LONG_IMG]
    moved[0:SHORT_IMG] = ordered[LONG_IMG:tail]
    moved[tail:total] = ordered[tail:total]


def norm_parts(values):
    centered = values - jnp.mean(values, axis=-1, keepdims=True)
    inverse = lax.rsqrt(jnp.mean(centered * centered, axis=-1, keepdims=True) + epsilon)
    return centered * inverse, inverse


def norm_back(gradient, normed, inverse, gain):
    scaled = gradient * gain
    return inverse * (
        scaled
        - jnp.mean(scaled, axis=-1, keepdims=True)
        - normed * jnp.mean(scaled * normed, axis=-1, keepdims=True)
    )


def gelu_parts(values):
    phi = 0.5 + 0.5 * lax.erf(values * math.sqrt(0.5))
    bell = jnp.exp2(values * values * (-0.5 * LOG2E) + math.log2(1.0 / math.sqrt(2.0 * math.pi)))
    return values * phi, phi + values * bell


def fill_masks(aug_q, aug_k):
    total = aug_q.shape[0]
    row = lax.broadcasted_iota(jnp.int32, (total, LANES), 0)
    segment = (row >= LONG_IMG).astype(jnp.int32) + (row >= LONG_IMG + SHORT_IMG).astype(jnp.int32)
    place = lanes(total) % HEAD_DIM
    aug_q[...] = jnp.where(place == segment, 1.0, 0.0).astype(BF)
    aug_k[...] = jnp.where((place < 3) & (place != segment), MASKED, 0.0).astype(BF)


def attend_tiles(total, size):
    tail = total - LONG_IMG
    first = total - 2 * LANES
    return [(at, n, 0, LONG_KEYS, True, at) for at, n in pieces(LONG_IMG, size)] + [
        (LONG_IMG + at, n, first, 2 * LANES, False, at) for at, n in pieces(tail, size)
    ]


def get(ref, at, n):
    cols = pl.ds(at if isinstance(at, int) else pl.multiple_of(at, LANES), n)
    value = ref[:, cols] if len(ref.shape) == 2 else ref[:, :, :, :, :, cols]
    return value.reshape(-1, n)


def put(ref, value, at, n):
    cols = pl.ds(at if isinstance(at, int) else pl.multiple_of(at, LANES), n)
    if len(ref.shape) == 2:
        ref[:, cols] = value
    else:
        ref[:, :, :, :, :, cols] = value.reshape(ref.shape[:-1] + (n,))


def get_rows(ref, part, parts):
    if len(ref.shape) == 2:
        rows = ref.shape[0] // parts
        return ref[pl.ds(pl.multiple_of(part * rows, rows), rows)]
    each = ref.shape[0] // parts
    value = ref[pl.ds(part * each, each)]
    return value.reshape(-1, value.shape[-1])


def put_rows(ref, value, part, parts):
    if len(ref.shape) == 2:
        rows = ref.shape[0] // parts
        ref[pl.ds(pl.multiple_of(part * rows, rows), rows)] = value
    else:
        each = ref.shape[0] // parts
        ref[pl.ds(part * each, each)] = value.reshape((each,) + ref.shape[1:])


def of_block(ref, j, offset=0):
    return ref.at[:, pl.ds(pl.multiple_of(offset + j * LANES, LANES), LANES)]


def of_trio(ref, j, which):
    return ref.at[:, pl.ds(pl.multiple_of(j * TRIO + which * LANES, LANES), LANES)]


def forward_head(j, head, qkv, attended, inverse, e_long, e_tail, aug_q, aug_k, size=400):
    total, width = attended.shape
    q, k, v = (of_trio(qkv, j, i) for i in range(3))
    attended, inverse = of_block(attended, j), of_block(inverse, j)
    mine = lanes(1) // HEAD_DIM == head
    ka = jnp.where(mine, k[...], aug_k[...])
    va = jnp.where(mine, v[...], jnp.ones_like(aug_k[...]))
    at = j * HEADS_IN_BLOCK + head
    for row, rows, key, keys, is_long, place in attend_tiles(total, size):
        here = pl.ds(row, rows)
        scores = nt(jnp.where(mine, q[here], aug_q[here]), ka[key : key + keys])
        exps = jnp.exp2(scores - jnp.max(scores, axis=1, keepdims=True)).astype(BF)
        store = e_long if is_long else e_tail
        store[at, place : place + rows, :] = exps
        product = nn(exps, va[key : key + keys])
        inv = 1.0 / pltpu.roll(product, HEAD_DIM, 1)
        attended[here] = jnp.where(mine, (product * inv).astype(BF), attended[here])
        inverse[here] = jnp.where(mine, inv, inverse[here])


def backward_prepare(j, qkv, attended, inverse, d_att, scaled_b, aug_b, q_t, s_t, k_b):
    total, width = attended.shape
    for at, n in pieces(total, ROWS):
        here = pl.ds(at, n)
        scaled = of_block(d_att, j)[here].astype(F32) * of_block(inverse, j)[here]
        inner = scaled * of_block(attended, j)[here].astype(F32)
        from_group = lax.broadcasted_iota(jnp.int32, (LANES, LANES), 0) // HEAD_DIM
        to_group = lanes(LANES) // HEAD_DIM
        spread = jnp.where((from_group + 1) % HEADS_IN_BLOCK == to_group, 1.0, 0.0).astype(BF)
        high = inner.astype(BF)
        low = (inner - high.astype(F32)).astype(BF)
        sums = nn(high, spread) + nn(low, spread)
        sum_high = sums.astype(BF)
        sum_low = (sums - sum_high.astype(F32)).astype(BF)
        place = lanes(n) % HEAD_DIM
        zeros = jnp.zeros_like(sum_high)
        aug_b[here] = jnp.where(place == 0, -sum_high, jnp.where(place == 1, -sum_low, zeros))
        scaled = scaled.astype(BF)
        scaled_b[here] = scaled
        s_t[:, at : at + n] = scaled.T
        q_t[:, at : at + n] = of_trio(qkv, j, 0)[here].T
        k_b[here] = of_trio(qkv, j, 1)[here]


def backward_head(j, head, qkv, e_long, e_tail, scaled_b, aug_b, q_t, s_t, k_b, dk_t, dv_t, size=400):
    total = scaled_b.shape[0]
    dq, v = of_trio(qkv, j, 0), of_trio(qkv, j, 2)
    mine = lanes(1) // HEAD_DIM == head
    following = lanes(1) // HEAD_DIM == (head + 1) % HEADS_IN_BLOCK
    va = jnp.where(mine, v[...], jnp.ones_like(k_b[...]))
    at = j * HEADS_IN_BLOCK + head
    of_head = pl.ds(pl.multiple_of(head * HEAD_DIM, HEAD_DIM), HEAD_DIM)
    sums_of = {}
    for row, rows, key, keys, is_long, where in attend_tiles(total, size):
        here = pl.ds(row, rows)
        store = e_long if is_long else e_tail
        exps = store[at, where : where + rows, :]
        side = jnp.where(following, aug_b[here], jnp.zeros_like(aug_b[here]))
        left = jnp.where(mine, scaled_b[here], side)
        d_scores = (exps.astype(F32) * nt(left, va[key : key + keys])).astype(BF)
        dq_here = (nn(d_scores, k_b[key : key + keys]) * SCALE).astype(BF)
        dq[here] = jnp.where(mine, dq_here, dq[here])
        more_v = nn(s_t[of_head, row : row + rows], exps)
        more_k = nn(q_t[of_head, row : row + rows], d_scores)
        if is_long in sums_of:
            more_v, more_k = sums_of[is_long][0] + more_v, sums_of[is_long][1] + more_k
        sums_of[is_long] = (more_v, more_k)
    first = total - 2 * LANES
    both = LONG_KEYS - first
    for ref, which, factor in ((dv_t, 0, 1.0), (dk_t, 1, 1.0 / LOG2E)):
        long_part, tail_part = (sums_of[is_long][which] * factor for is_long in (True, False))
        ref[of_head, 0:first] = long_part[:, :first].astype(BF)
        ref[of_head, first:LONG_KEYS] = (long_part[:, first:] + tail_part[:, :both]).astype(BF)
        ref[of_head, LONG_KEYS:total] = tail_part[:, both:].astype(BF)


def all_forward(b, transfers):
    unrolled = 2

    def step(i, carried):
        for one in range(unrolled):
            at = i * unrolled + one
            forward_head(
                at // HEADS_IN_BLOCK, at % HEADS_IN_BLOCK, b.qkv, b.attended, b.inverse,
                b.e_long, b.e_tail, b.aug_q, b.aug_k,
            )
        transfers.after_forward(i)
        return carried

    lax.fori_loop(0, b.attended.shape[1] // HEAD_DIM // unrolled, step, 0)


def all_backward(b, transfers):
    total, width = b.attended.shape
    unrolled = 2
    keep = (b.scaled_b, b.aug_b, b.q_t, b.s_t, b.k_b)

    def block(j, carried):
        backward_prepare(j, b.qkv, b.attended, b.inverse, b.d_exp, *keep)

        def step(i, inside):
            for one in range(unrolled):
                backward_head(
                    j, i * unrolled + one, b.qkv, b.e_long, b.e_tail, *keep, b.dk_t, b.dv_t
                )
            return inside

        lax.fori_loop(0, HEADS_IN_BLOCK // unrolled, step, 0)
        of_trio(b.qkv, j, 1)[...] = b.dk_t[...].T
        of_trio(b.qkv, j, 2)[...] = b.dv_t[...].T
        here = pl.ds(pl.multiple_of(j * LANES, LANES), LANES)
        trio = pl.ds(pl.multiple_of(j * TRIO, LANES), TRIO)
        for row, which in ((Q_BIAS, 0), (V_BIAS, 2)):
            values = of_trio(b.qkv, j, which)[...].astype(F32)
            b.g_vec[row : row + 1, here] = jnp.sum(values, axis=0, keepdims=True)

        w_trio = get(b.w_qkv, j * TRIO, TRIO)
        for at, n in pieces(total, ROWS):
            b.acc_b[at : at + n] = b.acc_b[at : at + n] + nt(b.qkv[at : at + n, trio], w_trio)
        put(b.w_qkv, nn(b.ha_t[...], b.qkv[:, trio]).astype(BF), j * TRIO, TRIO)
        transfers.after_backward(j)
        return carried

    lax.fori_loop(0, width // LANES, block, 0)


class Buffers(typing.NamedTuple):
    x_in: typing.Any
    ha_t: typing.Any
    cot: typing.Any
    xc: typing.Any
    qkv: typing.Any
    attended: typing.Any
    inverse: typing.Any
    e_long: typing.Any
    e_tail: typing.Any
    aug_q: typing.Any
    aug_k: typing.Any
    middle: typing.Any
    acc_a: typing.Any
    acc_b: typing.Any
    hb: typing.Any
    act: typing.Any
    d_exp: typing.Any
    scaled_b: typing.Any
    aug_b: typing.Any
    q_t: typing.Any
    s_t: typing.Any
    k_b: typing.Any
    dk_t: typing.Any
    dv_t: typing.Any
    vec: typing.Any
    g_vec: typing.Any
    w_qkv: typing.Any
    w_proj: typing.Any
    w_expand: typing.Any
    w_reduce: typing.Any


def buffers(total, width, weights):
    heads = width // HEAD_DIM
    rows, lane, turned = (total, width), (total, LANES), (LANES, total)
    shapes = Buffers(
        x_in=(rows, BF),
        ha_t=((width, total), BF),
        cot=(rows, BF),
        xc=(rows, BF),
        qkv=((total, 3 * width), BF),
        attended=(rows, BF),
        inverse=(rows, F32),
        e_long=((heads, LONG_IMG, LONG_KEYS), BF),
        e_tail=((heads, total - LONG_IMG, 2 * LANES), BF),
        aug_q=(lane, BF),
        aug_k=(lane, BF),
        middle=(rows, F32),
        acc_a=(rows, F32),
        acc_b=(rows, F32),
        hb=(rows, BF),
        act=(rows, BF),
        d_exp=(rows, BF),
        scaled_b=(lane, BF),
        aug_b=(lane, BF),
        q_t=(turned, BF),
        s_t=(turned, BF),
        k_b=(lane, BF),
        dk_t=(turned, BF),
        dv_t=(turned, BF),
        vec=((VEC_ROWS, width), F32),
        g_vec=((VEC_ROWS, width), F32),
        w_qkv=(weights[QKV], BF),
        w_proj=(weights[PROJ], BF),
        w_expand=(weights[EXPAND], BF),
        w_reduce=(weights[REDUCE], BF),
    )
    return [pltpu.VMEM(*one) for one in shapes]


def compute(b, transfers):
    total, width = b.xc.shape
    ff = b.w_expand.shape[-1]
    acc_a, acc_b, vec, g_vec = b.acc_a, b.acc_b, b.vec, b.g_vec

    def by_rows(function):
        def step(i, carried):
            function(pl.ds(pl.multiple_of(i * ROWS, ROWS), ROWS))
            return carried

        lax.fori_loop(0, total // ROWS, step, 0)

    def vector(row):
        return vec[pl.ds(row, 1), :]

    def add_sum(row, values):
        g_vec[pl.ds(row, 1), :] = g_vec[pl.ds(row, 1), :] + jnp.sum(values, axis=0, keepdims=True)

    def load(source):
        @by_rows
        def _(rows):
            acc_a[rows] = source[rows].astype(F32)

        to_canonical(swapped, acc_a, acc_b)

    def loaded(rows):
        return jnp.where(swapped, acc_b[rows], acc_a[rows])

    def unload(values, moved, target):
        to_natural(values, moved)

        @by_rows
        def _(rows):
            target[rows] = jnp.where(swapped, moved[rows], values[rows]).astype(BF)

    transfers.begin()
    g_vec[...] = jnp.zeros_like(g_vec)
    fill_masks(b.aug_q, b.aug_k)
    transfers.enter()
    transfers.need_tokens()
    swapped = jnp.broadcast_to(transfers.first_length(), (1, width)) == SHORT_IMG
    load(b.x_in)

    @by_rows
    def _(rows):
        values = loaded(rows)
        b.xc[rows] = values.astype(BF)
        acc_a[rows], _ = norm_parts(values)

    transfers.need_qkv()
    qkv, w_qkv = b.qkv, b.w_qkv

    for at, n in pieces(total, ROWS):
        rows = slice(at, at + n)
        lowered = (acc_a[rows] * vector(A_GAIN) + vector(A_SHIFT)).astype(BF)
        b.ha_t[:, rows] = lowered.T
        for j in range(width // LANES):
            here = slice(j * LANES, (j + 1) * LANES)
            projected = nn(lowered, get(w_qkv, j * TRIO, TRIO))
            q, k, v = (projected[:, i * LANES : (i + 1) * LANES] for i in range(3))
            q = (q + vec[Q_BIAS : Q_BIAS + 1, here]) * (SCALE * LOG2E)
            v = v + vec[V_BIAS : V_BIAS + 1, here]
            for i, value in enumerate((q, k, v)):
                qkv[rows, j * TRIO + i * LANES : j * TRIO + (i + 1) * LANES] = value.astype(BF)

    transfers.forward()
    all_forward(b, transfers)

    transfers.need_cotangent()
    cot, middle, hb, act, d_exp, attended = b.cot, b.middle, b.hb, b.act, b.d_exp, b.attended
    w_proj, w_expand, w_reduce = b.w_proj, b.w_expand, b.w_reduce
    load(cot)

    @by_rows
    def _(rows):
        cot[rows] = loaded(rows).astype(BF)

    transfers.need_proj()

    @by_rows
    def _(rows):
        mid = b.xc[rows].astype(F32) + (nn(attended[rows], get(w_proj, 0, width)) + vector(P_BIAS))
        middle[rows] = mid
        normed, _ = norm_parts(mid)
        hb[rows] = (normed * vector(M_GAIN) + vector(M_SHIFT)).astype(BF)
        acc_a[rows] = mid + vector(R_BIAS)
        acc_b[rows] = jnp.zeros_like(mid)
        add_sum(R_BIAS, cot[rows].astype(F32))

    transfers.need_mlp()
    parts = ff // width

    def one_part(part, carried):
        w_in, w_out = get(w_expand, part * width, width), get_rows(w_reduce, part, parts)
        tiles = pieces(total, ROWS // 2)
        todo = []
        for step in range(len(tiles) + 1):
            if step < len(tiles):
                at, n = tiles[step]
                rows = slice(at, at + n)
                todo.append((rows, nn(hb[rows], w_in) + vector(E_BIAS + part), nt(cot[rows], w_out)))
            if step:
                rows, expanded, d_act = todo.pop(0)
                value, slope = gelu_parts(expanded)
                low = value.astype(BF)
                act[rows] = low
                d_low = (d_act * slope).astype(BF)
                d_exp[rows] = d_low
                acc_a[rows] = acc_a[rows] + nn(low, w_out)
                acc_b[rows] = acc_b[rows] + nt(d_low, w_in)
                add_sum(E_BIAS + part, d_low.astype(F32))
        put_rows(w_reduce, tn(act[...], cot[...]).astype(BF), part, parts)
        put(w_expand, tn(hb[...], d_exp[...]).astype(BF), part * width, width)
        transfers.after_part(part)
        return carried

    lax.fori_loop(0, parts, one_part, 0)

    d_att = d_exp

    @by_rows
    def _(rows):
        gradient = acc_b[rows]
        normed, inv = norm_parts(middle[rows])
        d_mid = cot[rows].astype(F32) + norm_back(gradient, normed, inv, vector(M_GAIN))
        add_sum(M_GAIN, gradient * normed)
        add_sum(M_SHIFT, gradient)
        middle[rows] = d_mid
        d_branch = d_mid.astype(BF)
        act[rows] = d_branch
        add_sum(P_BIAS, d_branch.astype(F32))
        d_att[rows] = nt(d_branch, get(w_proj, 0, width)).astype(BF)

    put(w_proj, tn(attended[...], act[...]).astype(BF), 0, width)
    transfers.have_proj()
    unload(acc_a, acc_b, hb)
    transfers.have_result()
    acc_b[...] = jnp.zeros_like(acc_b)
    all_backward(b, transfers)

    @by_rows
    def _(rows):
        gradient = acc_b[rows]
        normed, inv = norm_parts(b.xc[rows].astype(F32))
        add_sum(A_GAIN, gradient * normed)
        add_sum(A_SHIFT, gradient)
        acc_a[rows] = middle[rows] + norm_back(gradient, normed, inv, vector(A_GAIN))

    unload(acc_a, acc_b, act)
    transfers.have_grad()


class Local:
    def __init__(self, b, lengths, ins, outs, sems):
        self.b, self.lengths, self.outs = b, lengths, outs
        targets = (b.x_in, b.cot) + tuple(b[-4:])
        self.loads = [pltpu.make_async_copy(one, target, sems.at[i]) for i, (one, target) in enumerate(zip(ins, targets))]
        sources = (b.hb, b.act) + tuple(b[-4:])
        self.stores = [pltpu.make_async_copy(one, out, sems.at[6 + i]) for i, (one, out) in enumerate(zip(sources, outs))]

    def begin(self):
        for copy in self.loads:
            copy.start()

    def enter(self):
        pass

    def first_length(self):
        return jnp.full((1, 1), self.lengths[lax.axis_index("blk"), 0, 0], jnp.int32).astype(F32)

    def need_tokens(self):
        self.loads[0].wait()

    def need_qkv(self):
        self.loads[2 + QKV].wait()

    def forward(self):
        pass

    def after_forward(self, i):
        pass

    def need_cotangent(self):
        self.loads[1].wait()

    def need_proj(self):
        self.loads[2 + PROJ].wait()

    def need_mlp(self):
        self.loads[2 + EXPAND].wait()
        self.loads[2 + REDUCE].wait()

    def after_part(self, part):
        pass

    def have_proj(self):
        for which in (PROJ, EXPAND, REDUCE):
            self.stores[2 + which].start()

    def have_result(self):
        self.stores[0].start()

    def after_backward(self, j):
        pass

    def have_grad(self):
        self.stores[2 + QKV].start()
        self.stores[1].start()
        for copy in self.stores:
            copy.wait()


def local_kernel(lengths, vec, x_in, cot_in, w_qkv, w_proj, w_expand, w_reduce,
                 result, grad_x, g_qkv, g_proj, g_expand, g_reduce, g_vec, *scratch):
    b = Buffers(*scratch[:-1])
    b.vec[...] = vec[...]
    ins = (x_in, cot_in, w_qkv, w_proj, w_expand, w_reduce)
    outs = (result, grad_x, g_qkv, g_proj, g_expand, g_reduce)
    compute(b, Local(b, lengths, ins, outs, scratch[-1]))
    g_vec[...] = b.g_vec[...]


def run_local(lengths, vec, x_in, cot_in, weights):
    vmem, anywhere = pl.BlockSpec(memory_space=pltpu.VMEM), pl.BlockSpec(memory_space=pl.ANY)
    total, width = x_in.shape
    like = (x_in, x_in) + tuple(weights)
    return pl.pallas_call(
        local_kernel,
        out_shape=[jax.ShapeDtypeStruct(one.shape, BF) for one in like]
        + [jax.ShapeDtypeStruct((VEC_ROWS, width), F32)],
        in_specs=[pl.BlockSpec(memory_space=pltpu.SMEM), vmem] + [anywhere] * 6,
        out_specs=[anywhere] * 6 + [vmem],
        scratch_shapes=buffers(total, width, [one.shape for one in weights]) + [pltpu.SemaphoreType.DMA((12,))],
        compiler_params=pltpu.CompilerParams(vmem_limit_bytes=62 * 2**20),
    )(lengths, vec, x_in, cot_in, *weights)


UNITS = (
    (QKV, 0, TRIO), (QKV, TRIO, TRIO), (QKV, 2 * TRIO, TRIO), (QKV, 3 * TRIO, TRIO + LANES), (PROJ, 0, 6 * LANES),
    (EXPAND, 0, 8 * LANES), (EXPAND, 8 * LANES, 8 * LANES), (REDUCE, 0, 2 * LANES), (REDUCE, 2 * LANES, 2 * LANES),
)
EARLY_UNITS, PROJ_UNITS, EXPAND_UNITS, REDUCE_UNITS = (0, 1, 2, 3), (4,), (5, 6), (7, 8)
VECTOR_TILES = ((QKV, 4 * TRIO), (PROJ, 4 * LANES), (PROJ, 5 * LANES))


class Group:
    def __init__(self, b, ins, outs, scratch):
        self.b = b
        self.tokens, self.cotangent, self.vectors, self.shards = ins
        self.result, self.grad_x, self.outs, self.g_total = outs
        (self.lengths, self.own_lengths, self.own_qkv, self.own_vec, self.packed, self.turn, self.arrived, self.v_two, self.v_z,
         self.local_sem, self.token_sem, self.ag_sem, self.rs_sem, self.v_sem) = scratch
        self.weights = tuple(b[-4:])
        dp, blk = lax.axis_index("dp"), lax.axis_index("blk")
        z, y, x, c = dp // SPREAD[Y], dp % SPREAD[Y], blk // SPREAD[C], blk % SPREAD[C]
        self.mine = (z, y, x, c)
        self.index = dp * (SPREAD[X] * SPREAD[C]) + blk
        self.blk = blk
        n_blk = SPREAD[X] * SPREAD[C]
        self.others = [(dp, (blk + k) % n_blk) for k in range(1, n_blk)]
        z_places = [(z + k) % SPREAD[Z] for k in range(1, SPREAD[Z])]
        self.along = (
            [((place * SPREAD[Y] + y, blk), place) for place in z_places],
            [((dp + 1 - 2 * y, blk), 1 - y)],
            [((dp, blk + SPREAD[C] * (1 - 2 * x)), 1 - x)],
            [((dp, blk + 1 - 2 * c), 1 - c)],
        )
        height = self.tokens.shape[1]

        def rows(ref):
            return lambda i: ref.at[pl.ds(pl.multiple_of(i * height, height), height)]

        def part(ref):
            return lambda i: ref.at[i]

        moves = (
            (part(self.tokens), rows(b.x_in)),
            (part(self.cotangent), rows(b.cot)),
            (rows(b.hb), part(self.result)),
            (rows(b.act), part(self.grad_x)),
        )
        self.swaps = [
            [
                self.remote(source(device[1]), target(blk), self.token_sem.at[i, k], self.token_sem.at[4 + i, k], device)
                for k, device in enumerate(self.others)
            ]
            for i, (source, target) in enumerate(moves)
        ]
        self.kept = [
            pltpu.make_async_copy(source(blk), target(blk), self.local_sem.at[i])
            for i, (source, target) in enumerate(moves)
        ]

    @staticmethod
    def remote(source, target, send, recv, device):
        return pltpu.make_async_remote_copy(
            src_ref=source, dst_ref=target, send_sem=send, recv_sem=recv,
            device_id=device, device_id_type=pl.DeviceIdType.MESH,
        )

    @staticmethod
    def start(copies):
        for copy in copies:
            copy.start()

    @staticmethod
    def arrive(copies):
        for copy in copies:
            copy.wait_recv()

    @staticmethod
    def sent(copies):
        for copy in copies:
            copy.wait_send()

    def place(self, free, at=None):
        index = [slice(None) if axis in free else self.mine[axis] for axis in range(4)]
        for axis, value in (at or {}).items():
            index[axis] = value
        return tuple(index)


    def gather(self, unit, stage):
        which, first, columns = UNITS[unit]
        w, order = self.weights[which], GATHER_ORDER[which]
        cols = (slice(None), pl.ds(first, columns))

        def one(i, view, device):
            return self.remote(view, view, self.ag_sem.at[0, unit, i], self.ag_sem.at[1, unit, i], device)

        if stage < 3:
            view = w.at[self.place(order[:stage]) + cols]
            return [one(copies_before(order, stage) + k, view, device) for k, (device, _) in enumerate(self.along[order[stage]])]
        device, _ = self.along[C][0]
        last = order[2]
        if stage == 3:
            return [one(5, w.at[self.place(order[:2]) + cols], device)]
        (_, other), = self.along[last]
        return [one(6, w.at[self.place(order[:2], {last: other}) + cols], device)]

    def gather_on(self, units, stage):
        for unit in units:
            copies = self.gather(unit, stage)
            self.arrive(copies)
            self.sent(copies)
            if stage < 2:
                self.start(self.gather(unit, stage + 1))
            if stage in (1, 2):
                self.start(self.gather(unit, stage + 2))

    def gathered(self, units):
        for unit in units:
            for stage in (3, 4):
                copies = self.gather(unit, stage)
                self.arrive(copies)
                self.sent(copies)

    def unpack(self, tile):
        which, first = VECTOR_TILES[tile]
        w = self.weights[which]
        all_of = w[:, :, :, :, 0:PACKED, first : first + LANES].astype(F32)
        total = jnp.sum(all_of.reshape(-1, PACKED, LANES), axis=0)
        for i in range(PACKED):
            row, at = divmod(tile * PACKED + i, 4)
            self.b.vec[row : row + 1, at * LANES : (at + 1) * LANES] = total[i : i + 1, :]


    def chunk_view(self, which, chunk):
        if which == REDUCE:
            return chunk, slice(None)
        columns = (TRIO, 4 * LANES, 4 * LANES)[which]
        return None, pl.ds(pl.multiple_of(chunk * columns, LANES), columns)

    def scatter(self, which, stage, chunk):
        w, order = self.weights[which], SCATTER_ORDER[which]
        axis, rest = order[stage], order[stage + 1 :]
        buffer = self.arrived[which][stage]
        at_z, cols = self.chunk_view(which, chunk)
        copies = []
        for k, (device, other) in enumerate(self.along[axis]):
            at = {axis: other}
            if at_z is not None and Z in rest:
                at[Z] = at_z
            source = w.at[self.place(rest, at) + (slice(None), cols)]
            sems = (self.rs_sem.at[i, which, chunk % 2, copies_before(order, stage) + k] for i in range(2))
            copies.append(self.remote(source, buffer.at[self.landing(axis, rest, at_z, cols, k)], *sems, device))
        return copies

    @staticmethod
    def landing(axis, rest, at_z, cols, k):
        lead = (k,) if axis == Z else ()
        free = tuple(at_z if one == Z and at_z is not None else slice(None) for one in sorted(rest))
        return lead + free + (slice(None), cols)

    def scatter_on(self, which, stage, chunk):
        w, order = self.weights[which], SCATTER_ORDER[which]
        copies = self.scatter(which, stage, chunk)
        self.arrive(copies)
        axis, rest = order[stage], order[stage + 1 :]
        buffer = self.arrived[which][stage]
        at_z, cols = self.chunk_view(which, chunk)
        at = {Z: at_z} if at_z is not None and Z in rest else None
        here = self.place(rest, at) + (slice(None), cols)
        terms = [buffer[self.landing(axis, rest, at_z, cols, k)] for k in range(len(copies))]
        if not rest:
            total = w[here].astype(F32)
            for term in terms:
                total = total + term.astype(F32)
            self.keep(which, chunk, total)
        elif len(terms) == 1:
            w[here] = w[here] + terms[0]
        else:
            total = w[here].astype(F32)
            for term in terms:
                total = total + term.astype(F32)
            w[here] = total.astype(BF)
        if rest and not (which == REDUCE and rest == (Z,)):
            self.start(self.scatter(which, stage + 1, chunk))
        self.sent(copies)

    def keep(self, which, chunk, total):
        out = self.outs[which]
        if which == QKV:
            width = out.shape[1] // 3
            for i in range(3):
                cols = pl.ds(pl.multiple_of(i * width + chunk * LANES, LANES), LANES)
                out[:, cols] = total[:, i * LANES : (i + 1) * LANES]
        else:
            _, cols = self.chunk_view(which, chunk)
            out[:, cols] = total

    def tick(self, which, t, stages):
        if isinstance(t, int):
            for stage in reversed(range(stages)):
                if 0 <= t - stage - 1 < CHUNKS:
                    self.scatter_on(which, stage, t - stage - 1)
            if t < CHUNKS:
                self.start(self.scatter(which, 0, t))
            return
        for stage in reversed(range(min(stages, CHUNKS - 1))):
            pl.when(t >= stage + 1)(lambda stage=stage: self.scatter_on(which, stage, t - stage - 1))
        self.start(self.scatter(which, 0, t))


    def vector_copies(self, stage):
        axis = (C, Y, X, Z)[stage]
        return [
            self.remote(
                self.b.g_vec, self.v_z.at[k] if axis == Z else self.v_two.at[stage],
                self.v_sem.at[0, stage + k], self.v_sem.at[1, stage + k], device,
            )
            for k, (device, _) in enumerate(self.along[axis])
        ]

    def vectors_on(self, stage):
        copies = self.vector_copies(stage)
        self.arrive(copies)
        self.sent(copies)
        g_vec = self.b.g_vec
        if stage < 3:
            g_vec[...] = g_vec[...] + self.v_two[stage]
            self.start(self.vector_copies(stage + 1))
        else:
            self.g_total[...] = g_vec[...] + jnp.sum(self.v_z[...], axis=0)


    def begin(self):
        self.peers = self.others + [device for axis in (Y, Z) for device, _ in self.along[axis]]
        for device in self.peers:
            pl.semaphore_signal(
                pltpu.get_barrier_semaphore(), inc=1, device_id=device, device_id_type=pl.DeviceIdType.MESH
            )
        count = len(self.vectors)
        loads = [
            pltpu.make_async_copy(one, target, self.local_sem.at[4 + i])
            for i, (one, target) in enumerate(zip(self.vectors, self.own_vec))
        ]
        loads.append(pltpu.make_async_copy(self.shards[QKV], self.own_qkv, self.local_sem.at[8 + count]))
        width = self.shards[PROJ].shape[1]
        slots = [self.weights[which].at[self.mine] for which in range(4)]
        self.own = [
            pltpu.make_async_copy(
                self.shards[which], slots[which].at[:, pl.ds(0, self.shards[which].shape[1])],
                self.local_sem.at[4 + count + which],
            )
            for which in (PROJ, EXPAND, REDUCE)
        ]
        loads.append(pltpu.make_async_copy(self.lengths, self.own_lengths, self.local_sem.at[4 + count + QKV]))
        loads[-2], loads[-1] = loads[-1], loads[-2]
        self.start(loads + self.own + self.kept[:2])
        self.packed[...] = jnp.zeros_like(self.packed)
        row = 0
        for load, own in zip(loads, self.own_vec):
            load.wait()
            size = own.shape[0]
            self.turn[...] = jnp.zeros_like(self.turn)
            self.turn[0:1, 0:size] = own[...].astype(F32).reshape(1, size)
            at = self.index * size
            self.packed[pl.ds(row + at // LANES, 1), :] = pltpu.roll(self.turn[...], at % LANES, 1)[0:1, :]
            row += math.prod(SPREAD) * size // LANES
        for load in loads[count:]:
            load.wait()
        w = self.weights[QKV]
        for j in range(width // LANES):
            for i in range(3):
                to = j * TRIO + i * LANES
                w[self.mine + (slice(None), pl.ds(to, LANES))] = self.own_qkv[:, i * width + j * LANES : i * width + (j + 1) * LANES]
        for tile, (which, first) in enumerate(VECTOR_TILES):
            values = self.packed[tile * PACKED : (tile + 1) * PACKED, :].astype(BF)
            self.weights[which][self.mine + (slice(None), pl.ds(first, LANES))] = values

    def enter(self):
        pl.semaphore_wait(pltpu.get_barrier_semaphore(), len(self.peers))
        for unit in EARLY_UNITS:
            self.start(self.gather(unit, 0))
        self.start(self.swaps[0])
        for copy in self.own:
            copy.wait()

    def first_length(self):
        first = self.own_lengths[0][0:1, :].astype(F32)
        lane = lax.broadcasted_iota(jnp.int32, first.shape, 1)
        return jnp.sum(jnp.where(lane == self.blk, first, 0.0), axis=1, keepdims=True)

    def need_tokens(self):
        self.gather_on(EARLY_UNITS, 0)
        for unit in PROJ_UNITS + EXPAND_UNITS:
            self.start(self.gather(unit, 0))
        self.gather_on(EARLY_UNITS, 1)
        for unit in REDUCE_UNITS:
            self.start(self.gather(unit, 0))
        self.gather_on(PROJ_UNITS + EXPAND_UNITS, 0)
        self.kept[0].wait()
        self.arrive(self.swaps[0])
        self.sent(self.swaps[0])
        self.start(self.swaps[1])

    def need_qkv(self):
        self.gather_on(EARLY_UNITS, 2)
        self.gathered(EARLY_UNITS)
        self.unpack(0)

    def forward(self):
        pass

    def after_forward(self, i):
        steps = {
            0: lambda: self.gather_on(REDUCE_UNITS, 0),
            1: lambda: self.gather_on(PROJ_UNITS, 1),
            2: lambda: self.gather_on(REDUCE_UNITS, 1),
            3: lambda: (self.gather_on(EXPAND_UNITS[:1], 1), self.gather_on(PROJ_UNITS, 2)),
            4: lambda: self.gather_on(EXPAND_UNITS[1:], 1),
            5: lambda: self.gather_on(REDUCE_UNITS, 2),
            6: lambda: self.gather_on(EXPAND_UNITS[:1], 2),
            7: lambda: self.gather_on(EXPAND_UNITS[1:], 2),
        }
        for at, step in steps.items():
            pl.when(i == at)(lambda step=step: [step(), None][1])

    def need_cotangent(self):
        self.kept[1].wait()
        self.arrive(self.swaps[1])
        self.sent(self.swaps[1])

    def need_proj(self):
        self.gathered(PROJ_UNITS)
        self.unpack(1)
        self.unpack(2)

    def need_mlp(self):
        self.gathered(EXPAND_UNITS + REDUCE_UNITS)

    def after_part(self, part):
        self.tick(REDUCE, part, 3)
        self.tick(EXPAND, part, 4)

    def have_proj(self):
        self.start(self.scatter(PROJ, 0, 0))
        self.tick(REDUCE, CHUNKS, 3)
        self.tick(EXPAND, CHUNKS, 4)

    def have_result(self):
        self.start(self.swaps[2] + self.kept[2:3])

    def after_backward(self, j):
        self.tick(QKV, j, 4)

        def step(at):
            self.scatter_on(PROJ, at, 0)
            t = CHUNKS + 1 + at
            if t < CHUNKS + 3:
                self.tick(REDUCE, t, 3)
            elif t == CHUNKS + 3:
                self.start(self.scatter(REDUCE, 3, 0))
            else:
                self.scatter_on(REDUCE, 3, 0)
            if t < CHUNKS + 4:
                self.tick(EXPAND, t, 4)

        for at in range(CHUNKS):
            pl.when(j == at)(lambda at=at: step(at))

    def have_grad(self):
        self.start(self.vector_copies(0) + self.swaps[3] + self.kept[3:4])
        self.tick(QKV, CHUNKS, 4)
        for stage in range(3):
            self.vectors_on(stage)
            self.tick(QKV, CHUNKS + 1 + stage, 4)
        self.vectors_on(3)
        for i in (2, 3):
            self.kept[i].wait()
            self.arrive(self.swaps[i])
            self.sent(self.swaps[i])


N_VECTORS = 8


def group_kernel(*refs):
    refs = list(refs)

    def take(n):
        taken = refs[:n]
        del refs[:n]
        return taken

    (lengths,), vectors, (tokens, cotangent), shards = take(1), take(N_VECTORS), take(2), take(4)
    (result, grad_x), outs, (g_total,) = take(2), take(4), take(1)
    b = Buffers(*take(len(Buffers._fields)))
    (own_lengths, own_qkv), own_vec, (packed, turn) = take(2), take(N_VECTORS), take(2)
    arrived = [take(4) for _ in range(4)]
    scratch = [lengths, own_lengths, own_qkv, own_vec, packed, turn, arrived] + refs
    group = Group(b, (tokens, cotangent, vectors, shards), (result, grad_x, outs, g_total), scratch)
    compute(b, group)


def run_group(lengths, vectors, tokens, cotangent, weights):
    vmem, anywhere = pl.BlockSpec(memory_space=pltpu.VMEM), pl.BlockSpec(memory_space=pl.ANY)
    blk, height, width = tokens.shape
    extra = [0] * 4
    for which, _ in VECTOR_TILES:
        extra[which] += LANES
    shapes = [SPREAD + (one.shape[0], one.shape[1] + more) for one, more in zip(weights, extra)]
    landing = []
    for which, shape in enumerate(shapes):
        for stage, axis in enumerate(SCATTER_ORDER[which]):
            rest = sorted(SCATTER_ORDER[which][stage + 1 :])
            lead = (SPREAD[Z] - 1,) if axis == Z else ()
            landing.append(pltpu.VMEM(lead + tuple(SPREAD[one] for one in rest) + weights[which].shape, BF))
    sums = (VEC_ROWS, width)
    packed_rows = math.prod(SPREAD) * sum(one.shape[0] for one in vectors) // LANES
    dma = pltpu.SemaphoreType.DMA
    return pl.pallas_call(
        group_kernel,
        out_shape=[jax.ShapeDtypeStruct(tokens.shape, BF)] * 2
        + [jax.ShapeDtypeStruct(one.shape, F32) for one in weights]
        + [jax.ShapeDtypeStruct(sums, F32)],
        in_specs=[anywhere] * (N_VECTORS + 7),
        out_specs=[anywhere] * 2 + [vmem] * 5,
        scratch_shapes=buffers(blk * height, width, shapes)
        + [pltpu.VMEM(lengths.shape, lengths.dtype), pltpu.VMEM(weights[QKV].shape, BF)]
        + [pltpu.VMEM(one.shape, BF) for one in vectors]
        + [pltpu.VMEM((packed_rows, LANES), F32), pltpu.VMEM((8, LANES), F32)]
        + landing
        + [pltpu.VMEM((3,) + sums, F32), pltpu.VMEM((SPREAD[Z] - 1,) + sums, F32)]
        + [dma((17,)), dma((8, 3)), dma((2, len(UNITS), 7)), dma((2, 4, 2, 6)), dma((2, 6))],
        compiler_params=pltpu.CompilerParams(
            vmem_limit_bytes=62 * 2**20, collective_id=0, has_side_effects=True
        ),
    )(lengths, *vectors, tokens, cotangent, *weights)


def finish_kernel(result, grad_x, g_qkv, g_proj, g_expand, g_reduce, g_vec, *refs):
    sources = (result, grad_x, g_qkv, g_proj, g_expand, g_reduce)
    outs, refs = refs[: 6 + N_VECTORS], refs[6 + N_VECTORS :]
    held, short = refs[:6], refs[6 : 6 + N_VECTORS]
    turn, lines, sems = refs[6 + N_VECTORS :]
    loads, stores = [], []
    for source, to, out in zip(sources, held, outs):
        places = range(source.shape[0]) if len(source.shape) == 3 else (slice(None),)
        for place in places:
            sem = len(loads)
            loads.append(pltpu.make_async_copy(source.at[place], to.at[place], sems.at[0, sem]))
            stores.append(pltpu.make_async_copy(to.at[place], out.at[place], sems.at[1, sem]))
    for load in loads:
        load.start()
    handed = []
    index = lax.axis_index("dp") * lax.axis_size("blk") + lax.axis_index("blk")
    devices = lax.axis_size("dp") * lax.axis_size("blk")
    width = g_vec.shape[1]
    parts = width // LANES
    for i in range(g_vec.shape[0]):
        for part in range(parts):
            lines[i * parts + part : i * parts + part + 1, :] = g_vec[i : i + 1, part * LANES : (part + 1) * LANES]
    row = 0
    for i, one in enumerate(short):
        size = one.shape[0]
        at = index * size
        turn[0:1, :] = lines[pl.ds(row + at // LANES, 1), :]
        turned = pltpu.roll(turn[...], (LANES - at % LANES) % LANES, 1)
        one[...] = turned[0:1, 0:size].reshape(size)
        handed.append(pltpu.make_async_copy(one, outs[6 + i], sems.at[0, len(loads) + i]))
        handed[-1].start()
        row += devices * size // LANES
    for load, store in zip(loads, stores):
        load.wait()
        store.start()
    for store in stores + handed:
        store.wait()


def finish(values, sizes):
    vmem, anywhere = pl.BlockSpec(memory_space=pltpu.VMEM), pl.BlockSpec(memory_space=pl.ANY)
    long = [(one.shape, one.dtype) for one in values[:6]]
    short = [((size,), F32) for size in sizes]
    return pl.pallas_call(
        finish_kernel,
        out_shape=[jax.ShapeDtypeStruct(*one) for one in long + short],
        in_specs=[anywhere] * 6 + [vmem],
        out_specs=[anywhere] * (6 + len(sizes)),
        scratch_shapes=[pltpu.VMEM(*one) for one in long + short]
        + [pltpu.VMEM((8, LANES), F32), pltpu.VMEM((values[6].size // LANES, LANES), F32)]
        + [pltpu.SemaphoreType.DMA((2, 4 + 2 * values[0].shape[0] + len(sizes)))],
    )(*values)


def by_collectives(lengths, vectors, sizes, tokens, cotangent, weights):
    axes = ("dp", "blk")
    width = tokens.shape[2]
    blocks = width // LANES

    def exchange(rows):
        return lax.all_to_all(rows.reshape(tokens.shape), "blk", 0, 0, tiled=True)

    packed = lax.all_gather(jnp.concatenate(vectors), axes, axis=0)
    starts = [sum(sizes[:i]) for i in range(len(sizes))]
    full = [packed[:, at : at + size].reshape(-1, width) for at, size in zip(starts, sizes)]
    vec = jnp.concatenate(full, axis=0).astype(F32)
    vec = jnp.pad(vec, ((0, VEC_ROWS - vec.shape[0]), (0, 0)))
    whole = [lax.all_gather(one, axes, axis=0, tiled=True) for one in weights]
    whole[QKV] = whole[QKV].reshape(width, 3, blocks, LANES).swapaxes(1, 2).reshape(width, 3 * width)
    result, grad_x, *grads, g_vec = run_local(
        lengths, vec, exchange(tokens).reshape(-1, width), exchange(cotangent).reshape(-1, width), whole
    )
    grads[QKV] = grads[QKV].reshape(width, blocks, 3, LANES).swapaxes(1, 2).reshape(width, 3 * width)
    grads = [lax.psum_scatter(one.astype(F32), axes, scatter_dimension=0, tiled=True) for one in grads]
    g_vec = lax.psum(g_vec, axes).reshape(-1)
    index = lax.axis_index(axes)
    devices = lax.axis_size(axes)
    own = [
        lax.dynamic_slice(g_vec, (devices * at + index * size,), (size,)) for at, size in zip(starts, sizes)
    ]
    return (exchange(result), exchange(grad_x), *grads, *own)


def body(
    tokens, lengths, attn_gain, attn_shift, w_qkv, qv_bias, w_proj, proj_bias,
    mlp_gain, mlp_shift, w_expand, expand_bias, w_reduce, reduce_bias, cotangent,
):
    vectors = (attn_gain, attn_shift, qv_bias, proj_bias, mlp_gain, mlp_shift, reduce_bias, expand_bias)
    sizes = [one.shape[0] for one in vectors]
    weights = (w_qkv, w_proj, w_expand, w_reduce)
    sized = (lax.axis_size("dp"), lax.axis_size("blk")) == (SPREAD[Z] * SPREAD[Y], SPREAD[X] * SPREAD[C])
    if sized and all(one.shape[0] % 16 == 0 for one in weights):
        outs = finish(run_group(jnp.transpose(lengths, (1, 2, 0)), vectors, tokens, cotangent, weights), sizes)
    else:
        outs = by_collectives(lengths, vectors, sizes, tokens, cotangent, weights)
    result, grad_x, g_qkv, g_proj, g_expand, g_reduce, ag, as_, qv, pb, mg, ms, rb, eb = outs
    return (result, grad_x, ag, as_, g_qkv, qv, g_proj, pb, mg, ms, g_expand, eb, g_reduce, rb)


def solution(mesh):
    both = ("dp", "blk")
    rows = P(None, both, None)
    vector, matrix = P(both), P(both, None)
    weights = (
        vector, vector, matrix, vector, matrix, vector, vector, vector, matrix, vector, matrix, vector,
    )
    return jax.shard_map(
        body,
        mesh=mesh,
        in_specs=(rows, P(None, "dp", None)) + weights + (rows,),
        out_specs=(rows, rows) + weights,
        check_vma=False,
    )
```

```python
import math
import typing

import jax
import jax.numpy as jnp
from jax import lax
from jax.experimental import pallas as pl
from jax.experimental.pallas import tpu as pltpu
from jax.sharding import PartitionSpec as P

HEAD_DIM = 32
LONG_IMG = 784
SHORT_IMG = 196
LANES = 128
HEADS_IN_BLOCK = LANES // HEAD_DIM
LONG_KEYS = 896
BF = jnp.bfloat16
F32 = jnp.float32
epsilon = 1e-06
LOG2E = math.log2(math.e)
SCALE = 1.0 / math.sqrt(HEAD_DIM)
MASKED = -1e30
ROWS = 512
A_GAIN, A_SHIFT, Q_BIAS, V_BIAS, P_BIAS, M_GAIN, M_SHIFT, R_BIAS, E_BIAS = range(9)
VEC_ROWS = 16
PACKED = 16
TRIO = 3 * LANES
CHUNKS = 4
Z, Y, X, C = range(4)
SPREAD = (4, 2, 2, 2)
QKV, PROJ, EXPAND, REDUCE = range(4)
GATHER_ORDER = ((X, Z, Y), (X, Z, Y), (X, Z, Y), (Z, Y, X))
SCATTER_ORDER = ((C, X, Y, Z), (C, Y, Z, X), (C, Y, Z, X), (C, X, Y, Z))


def copies_before(order, stage):
    return sum(SPREAD[axis] - 1 for axis in order[:stage])


def nt(left, right):
    return lax.dot_general(left, right, (((1,), (1,)), ((), ())), preferred_element_type=F32)


def nn(left, right):
    return lax.dot_general(left, right, (((1,), (0,)), ((), ())), preferred_element_type=F32)


def tn(left, right):
    return lax.dot_general(left, right, (((0,), (0,)), ((), ())), preferred_element_type=F32)


def pieces(total, size):
    return [(at, min(size, total - at)) for at in range(0, total, size)]


def lanes(rows, width=LANES):
    return lax.broadcasted_iota(jnp.int32, (rows, width), 1)


def to_canonical(swapped, natural, moved):
    total = natural.shape[0]
    tail = LONG_IMG + SHORT_IMG
    moved[0:LONG_IMG] = natural[SHORT_IMG:tail]
    moved[LONG_IMG:tail] = natural[0:SHORT_IMG]
    moved[tail:total] = natural[tail:total]


def to_natural(ordered, moved):
    total = ordered.shape[0]
    tail = LONG_IMG + SHORT_IMG
    moved[SHORT_IMG:tail] = ordered[0:LONG_IMG]
    moved[0:SHORT_IMG] = ordered[LONG_IMG:tail]
    moved[tail:total] = ordered[tail:total]


def norm_parts(values):
    centered = values - jnp.mean(values, axis=-1, keepdims=True)
    inverse = lax.rsqrt(jnp.mean(centered * centered, axis=-1, keepdims=True) + epsilon)
    return centered * inverse, inverse


def norm_back(gradient, normed, inverse, gain):
    scaled = gradient * gain
    return inverse * (
        scaled
        - jnp.mean(scaled, axis=-1, keepdims=True)
        - normed * jnp.mean(scaled * normed, axis=-1, keepdims=True)
    )


def gelu_parts(values):
    phi = 0.5 + 0.5 * lax.erf(values * math.sqrt(0.5))
    bell = jnp.exp2(values * values * (-0.5 * LOG2E) + math.log2(1.0 / math.sqrt(2.0 * math.pi)))
    return values * phi, phi + values * bell


def fill_masks(aug_q, aug_k):
    total = aug_q.shape[0]
    row = lax.broadcasted_iota(jnp.int32, (total, LANES), 0)
    segment = (row >= LONG_IMG).astype(jnp.int32) + (row >= LONG_IMG + SHORT_IMG).astype(jnp.int32)
    place = lanes(total) % HEAD_DIM
    aug_q[...] = jnp.where(place == segment, 1.0, 0.0).astype(BF)
    aug_k[...] = jnp.where((place < 3) & (place != segment), MASKED, 0.0).astype(BF)


def attend_tiles(total, size):
    tail = total - LONG_IMG
    first = total - 2 * LANES
    return [(at, n, 0, LONG_KEYS, True, at) for at, n in pieces(LONG_IMG, size)] + [
        (LONG_IMG + at, n, first, 2 * LANES, False, at) for at, n in pieces(tail, size)
    ]


def get(ref, at, n):
    cols = pl.ds(at if isinstance(at, int) else pl.multiple_of(at, LANES), n)
    value = ref[:, cols] if len(ref.shape) == 2 else ref[:, :, :, :, :, cols]
    return value.reshape(-1, n)


def put(ref, value, at, n):
    cols = pl.ds(at if isinstance(at, int) else pl.multiple_of(at, LANES), n)
    if len(ref.shape) == 2:
        ref[:, cols] = value
    else:
        ref[:, :, :, :, :, cols] = value.reshape(ref.shape[:-1] + (n,))


def get_rows(ref, part, parts):
    if len(ref.shape) == 2:
        rows = ref.shape[0] // parts
        return ref[pl.ds(pl.multiple_of(part * rows, rows), rows)]
    each = ref.shape[0] // parts
    value = ref[pl.ds(part * each, each)]
    return value.reshape(-1, value.shape[-1])


def put_rows(ref, value, part, parts):
    if len(ref.shape) == 2:
        rows = ref.shape[0] // parts
        ref[pl.ds(pl.multiple_of(part * rows, rows), rows)] = value
    else:
        each = ref.shape[0] // parts
        ref[pl.ds(part * each, each)] = value.reshape((each,) + ref.shape[1:])


def of_block(ref, j, offset=0):
    return ref.at[:, pl.ds(pl.multiple_of(offset + j * LANES, LANES), LANES)]


def of_trio(ref, j, which):
    return ref.at[:, pl.ds(pl.multiple_of(j * TRIO + which * LANES, LANES), LANES)]


def forward_head(j, head, qkv, attended, inverse, e_long, e_tail, aug_q, aug_k, size=400):
    total, width = attended.shape
    q, k, v = (of_trio(qkv, j, i) for i in range(3))
    attended, inverse = of_block(attended, j), of_block(inverse, j)
    mine = lanes(1) // HEAD_DIM == head
    ka = jnp.where(mine, k[...], aug_k[...])
    va = jnp.where(mine, v[...], jnp.ones_like(aug_k[...]))
    at = j * HEADS_IN_BLOCK + head
    for row, rows, key, keys, is_long, place in attend_tiles(total, size):
        here = pl.ds(row, rows)
        scores = nt(jnp.where(mine, q[here], aug_q[here]), ka[key : key + keys])
        exps = jnp.exp2(scores - jnp.max(scores, axis=1, keepdims=True)).astype(BF)
        store = e_long if is_long else e_tail
        store[at, place : place + rows, :] = exps
        product = nn(exps, va[key : key + keys])
        inv = 1.0 / pltpu.roll(product, HEAD_DIM, 1)
        attended[here] = jnp.where(mine, (product * inv).astype(BF), attended[here])
        inverse[here] = jnp.where(mine, inv, inverse[here])


def backward_prepare(j, qkv, attended, inverse, d_att, scaled_b, aug_b, q_t, s_t, k_b):
    total, width = attended.shape
    for at, n in pieces(total, ROWS):
        here = pl.ds(at, n)
        scaled = of_block(d_att, j)[here].astype(F32) * of_block(inverse, j)[here]
        inner = scaled * of_block(attended, j)[here].astype(F32)
        from_group = lax.broadcasted_iota(jnp.int32, (LANES, LANES), 0) // HEAD_DIM
        to_group = lanes(LANES) // HEAD_DIM
        spread = jnp.where((from_group + 1) % HEADS_IN_BLOCK == to_group, 1.0, 0.0).astype(BF)
        high = inner.astype(BF)
        low = (inner - high.astype(F32)).astype(BF)
        sums = nn(high, spread) + nn(low, spread)
        sum_high = sums.astype(BF)
        sum_low = (sums - sum_high.astype(F32)).astype(BF)
        place = lanes(n) % HEAD_DIM
        zeros = jnp.zeros_like(sum_high)
        aug_b[here] = jnp.where(place == 0, -sum_high, jnp.where(place == 1, -sum_low, zeros))
        scaled = scaled.astype(BF)
        scaled_b[here] = scaled
        s_t[:, at : at + n] = scaled.T
        q_t[:, at : at + n] = of_trio(qkv, j, 0)[here].T
        k_b[here] = of_trio(qkv, j, 1)[here]


def backward_head(j, head, qkv, e_long, e_tail, scaled_b, aug_b, q_t, s_t, k_b, dk_t, dv_t, size=400):
    total = scaled_b.shape[0]
    dq, v = of_trio(qkv, j, 0), of_trio(qkv, j, 2)
    mine = lanes(1) // HEAD_DIM == head
    following = lanes(1) // HEAD_DIM == (head + 1) % HEADS_IN_BLOCK
    va = jnp.where(mine, v[...], jnp.ones_like(k_b[...]))
    at = j * HEADS_IN_BLOCK + head
    of_head = pl.ds(pl.multiple_of(head * HEAD_DIM, HEAD_DIM), HEAD_DIM)
    sums_of = {}
    for row, rows, key, keys, is_long, where in attend_tiles(total, size):
        here = pl.ds(row, rows)
        store = e_long if is_long else e_tail
        exps = store[at, where : where + rows, :]
        side = jnp.where(following, aug_b[here], jnp.zeros_like(aug_b[here]))
        left = jnp.where(mine, scaled_b[here], side)
        d_scores = (exps.astype(F32) * nt(left, va[key : key + keys])).astype(BF)
        dq_here = (nn(d_scores, k_b[key : key + keys]) * SCALE).astype(BF)
        dq[here] = jnp.where(mine, dq_here, dq[here])
        more_v = nn(s_t[of_head, row : row + rows], exps)
        more_k = nn(q_t[of_head, row : row + rows], d_scores)
        if is_long in sums_of:
            more_v, more_k = sums_of[is_long][0] + more_v, sums_of[is_long][1] + more_k
        sums_of[is_long] = (more_v, more_k)
    first = total - 2 * LANES
    both = LONG_KEYS - first
    for ref, which, factor in ((dv_t, 0, 1.0), (dk_t, 1, 1.0 / LOG2E)):
        long_part, tail_part = (sums_of[is_long][which] * factor for is_long in (True, False))
        ref[of_head, 0:first] = long_part[:, :first].astype(BF)
        ref[of_head, first:LONG_KEYS] = (long_part[:, first:] + tail_part[:, :both]).astype(BF)
        ref[of_head, LONG_KEYS:total] = tail_part[:, both:].astype(BF)


def trio_columns(ref, j, width):
    return ref.shape[-1] - 3 * width + j * TRIO


def all_forward(b, transfers):
    total, width = b.attended.shape
    unrolled = 2

    def block(j, carried):
        transfers.before_block(j)
        here = pl.ds(pl.multiple_of(j * LANES, LANES), LANES)
        w_trio = get(b.w_qkv, trio_columns(b.w_qkv, j, width), TRIO)
        for at, n in pieces(total, ROWS):
            projected = nn(b.x_in[at : at + n], w_trio)
            q, k, v = (projected[:, i * LANES : (i + 1) * LANES] for i in range(3))
            q = (q + b.vec[Q_BIAS : Q_BIAS + 1, here]) * (SCALE * LOG2E)
            v = v + b.vec[V_BIAS : V_BIAS + 1, here]
            for i, value in enumerate((q, k, v)):
                of_trio(b.qkv, j, i)[at : at + n] = value.astype(BF)

        def step(i, inside):
            for one in range(unrolled):
                forward_head(
                    j, i * unrolled + one, b.qkv, b.attended, b.inverse,
                    b.e_long, b.e_tail, b.aug_q, b.aug_k,
                )
            transfers.after_forward(j * (HEADS_IN_BLOCK // unrolled) + i)
            return inside

        lax.fori_loop(0, HEADS_IN_BLOCK // unrolled, step, 0)
        return carried

    lax.fori_loop(0, width // LANES, block, 0)


def weight_of_block(b, j, transfers):
    trio = pl.ds(pl.multiple_of(j * TRIO, LANES), TRIO)
    at = trio_columns(b.w_qkv, j, b.attended.shape[1])
    put(b.w_qkv, nn(b.ha_t[...], b.qkv[:, trio]).astype(BF), at, TRIO)
    transfers.have_qkv(j)


def all_backward(b, transfers):
    total, width = b.attended.shape
    unrolled = 2
    keep = (b.scaled_b, b.aug_b, b.q_t, b.s_t, b.k_b)

    blocks = width // LANES

    def block(number, carried):
        j = blocks - 1 - number
        pl.when(number > 0)(lambda: weight_of_block(b, j + 1, transfers))
        backward_prepare(j, b.qkv, b.attended, b.inverse, b.d_exp, *keep)

        def step(i, inside):
            for one in range(unrolled):
                backward_head(
                    j, i * unrolled + one, b.qkv, b.e_long, b.e_tail, *keep, b.dk_t, b.dv_t
                )
            transfers.after_backward(number * (HEADS_IN_BLOCK // unrolled) + i)
            return inside

        lax.fori_loop(0, HEADS_IN_BLOCK // unrolled, step, 0)
        of_trio(b.qkv, j, 1)[...] = b.dk_t[...].T
        of_trio(b.qkv, j, 2)[...] = b.dv_t[...].T
        here = pl.ds(pl.multiple_of(j * LANES, LANES), LANES)
        trio = pl.ds(pl.multiple_of(j * TRIO, LANES), TRIO)
        for row, which in ((Q_BIAS, 0), (V_BIAS, 2)):
            values = of_trio(b.qkv, j, which)[...].astype(F32)
            b.g_vec[row : row + 1, here] = jnp.sum(values, axis=0, keepdims=True)
        w_trio = get(b.w_qkv, trio_columns(b.w_qkv, j, width), TRIO)
        for at, n in pieces(total, ROWS):
            b.acc_b[at : at + n] = b.acc_b[at : at + n] + nt(b.qkv[at : at + n, trio], w_trio)
        return carried

    lax.fori_loop(0, blocks, block, 0)


class Buffers(typing.NamedTuple):
    x_in: typing.Any
    ha_t: typing.Any
    cot: typing.Any
    xc: typing.Any
    qkv: typing.Any
    attended: typing.Any
    inverse: typing.Any
    e_long: typing.Any
    e_tail: typing.Any
    aug_q: typing.Any
    aug_k: typing.Any
    middle: typing.Any
    acc_a: typing.Any
    acc_b: typing.Any
    hb: typing.Any
    act: typing.Any
    d_exp: typing.Any
    scaled_b: typing.Any
    aug_b: typing.Any
    q_t: typing.Any
    s_t: typing.Any
    k_b: typing.Any
    dk_t: typing.Any
    dv_t: typing.Any
    vec: typing.Any
    g_vec: typing.Any
    w_qkv: typing.Any
    w_proj: typing.Any
    w_expand: typing.Any
    w_reduce: typing.Any


def buffers(total, width, weights):
    heads = width // HEAD_DIM
    rows, lane, turned = (total, width), (total, LANES), (LANES, total)
    shapes = Buffers(
        x_in=(rows, BF),
        ha_t=((width, total), BF),
        cot=(rows, BF),
        xc=(rows, BF),
        qkv=((total, 3 * width), BF),
        attended=(rows, BF),
        inverse=(rows, F32),
        e_long=((heads, LONG_IMG, LONG_KEYS), BF),
        e_tail=((heads, total - LONG_IMG, 2 * LANES), BF),
        aug_q=(lane, BF),
        aug_k=(lane, BF),
        middle=(rows, F32),
        acc_a=(rows, F32),
        acc_b=(rows, F32),
        hb=(rows, BF),
        act=(rows, BF),
        d_exp=(rows, BF),
        scaled_b=(lane, BF),
        aug_b=(lane, BF),
        q_t=(turned, BF),
        s_t=(turned, BF),
        k_b=(lane, BF),
        dk_t=(turned, BF),
        dv_t=(turned, BF),
        vec=((VEC_ROWS, width), F32),
        g_vec=((VEC_ROWS, width), F32),
        w_qkv=(weights[QKV], BF),
        w_proj=(weights[PROJ], BF),
        w_expand=(weights[EXPAND], BF),
        w_reduce=(weights[REDUCE], BF),
    )
    return [pltpu.VMEM(*one) for one in shapes]


def compute(b, transfers):
    total, width = b.xc.shape
    ff = b.w_expand.shape[-1]
    acc_a, acc_b, vec, g_vec = b.acc_a, b.acc_b, b.vec, b.g_vec

    def by_rows(function):
        def step(i, carried):
            function(pl.ds(pl.multiple_of(i * ROWS, ROWS), ROWS))
            return carried

        lax.fori_loop(0, total // ROWS, step, 0)

    def vector(row):
        return vec[pl.ds(row, 1), :]

    def add_sum(row, values):
        g_vec[pl.ds(row, 1), :] = g_vec[pl.ds(row, 1), :] + jnp.sum(values, axis=0, keepdims=True)

    def load(source):
        @by_rows
        def _(rows):
            acc_a[rows] = source[rows].astype(F32)

        to_canonical(swapped, acc_a, acc_b)

    def loaded(rows):
        return jnp.where(swapped, acc_b[rows], acc_a[rows])

    def unload(values, moved, target):
        to_natural(values, moved)

        @by_rows
        def _(rows):
            target[rows] = jnp.where(swapped, moved[rows], values[rows]).astype(BF)

    transfers.begin()
    g_vec[...] = jnp.zeros_like(g_vec)
    fill_masks(b.aug_q, b.aug_k)
    transfers.enter()
    transfers.need_tokens()
    swapped = jnp.broadcast_to(transfers.first_length(), (1, width)) == SHORT_IMG
    load(b.x_in)

    @by_rows
    def _(rows):
        values = loaded(rows)
        b.xc[rows] = values.astype(BF)
        normed, _ = norm_parts(values)
        b.x_in[rows] = (normed * vector(A_GAIN) + vector(A_SHIFT)).astype(BF)

    transfers.need_first()
    for at, n in pieces(total, ROWS):
        b.ha_t[:, at : at + n] = b.x_in[at : at + n].T

    all_forward(b, transfers)

    transfers.need_cotangent()
    cot, middle, hb, act, d_exp, attended = b.cot, b.middle, b.hb, b.act, b.d_exp, b.attended
    w_proj, w_expand, w_reduce = b.w_proj, b.w_expand, b.w_reduce
    load(cot)

    @by_rows
    def _(rows):
        cot[rows] = loaded(rows).astype(BF)

    transfers.need_proj()

    @by_rows
    def _(rows):
        mid = b.xc[rows].astype(F32) + (nn(attended[rows], get(w_proj, 0, width)) + vector(P_BIAS))
        middle[rows] = mid
        normed, _ = norm_parts(mid)
        hb[rows] = (normed * vector(M_GAIN) + vector(M_SHIFT)).astype(BF)
        acc_a[rows] = mid + vector(R_BIAS)
        acc_b[rows] = jnp.zeros_like(mid)
        add_sum(R_BIAS, cot[rows].astype(F32))

    transfers.need_mlp()
    parts = ff // width

    def one_part(part, carried):
        w_in, w_out = get(w_expand, part * width, width), get_rows(w_reduce, part, parts)
        tiles = pieces(total, ROWS // 2)
        todo = []
        for step in range(len(tiles) + 1):
            if step < len(tiles):
                at, n = tiles[step]
                rows = slice(at, at + n)
                todo.append((rows, nn(hb[rows], w_in) + vector(E_BIAS + part), nt(cot[rows], w_out)))
            if step:
                rows, expanded, d_act = todo.pop(0)
                value, slope = gelu_parts(expanded)
                low = value.astype(BF)
                act[rows] = low
                d_low = (d_act * slope).astype(BF)
                d_exp[rows] = d_low
                acc_a[rows] = acc_a[rows] + nn(low, w_out)
                acc_b[rows] = acc_b[rows] + nt(d_low, w_in)
                add_sum(E_BIAS + part, d_low.astype(F32))
        put_rows(w_reduce, tn(act[...], cot[...]).astype(BF), part, parts)
        put(w_expand, tn(hb[...], d_exp[...]).astype(BF), part * width, width)
        transfers.after_part(part)
        return carried

    lax.fori_loop(0, parts, one_part, 0)

    d_att = d_exp

    @by_rows
    def _(rows):
        gradient = acc_b[rows]
        normed, inv = norm_parts(middle[rows])
        d_mid = cot[rows].astype(F32) + norm_back(gradient, normed, inv, vector(M_GAIN))
        add_sum(M_GAIN, gradient * normed)
        add_sum(M_SHIFT, gradient)
        middle[rows] = d_mid
        d_branch = d_mid.astype(BF)
        act[rows] = d_branch
        add_sum(P_BIAS, d_branch.astype(F32))
        d_att[rows] = nt(d_branch, get(w_proj, 0, width)).astype(BF)

    put(w_proj, tn(attended[...], act[...]).astype(BF), 0, width)
    transfers.have_proj()
    unload(acc_a, acc_b, hb)
    transfers.have_result()
    acc_b[...] = jnp.zeros_like(acc_b)
    all_backward(b, transfers)
    weight_of_block(b, 0, transfers)

    @by_rows
    def _(rows):
        gradient = acc_b[rows]
        normed, inv = norm_parts(b.xc[rows].astype(F32))
        add_sum(A_GAIN, gradient * normed)
        add_sum(A_SHIFT, gradient)
        acc_a[rows] = middle[rows] + norm_back(gradient, normed, inv, vector(A_GAIN))

    transfers.have_vectors()
    unload(acc_a, acc_b, act)
    transfers.have_grad()


class Local:
    def __init__(self, b, lengths, ins, outs, sems):
        self.b, self.lengths, self.outs = b, lengths, outs
        targets = (b.x_in, b.cot) + tuple(b[-4:])
        self.loads = [pltpu.make_async_copy(one, target, sems.at[i]) for i, (one, target) in enumerate(zip(ins, targets))]
        sources = (b.hb, b.act) + tuple(b[-4:])
        self.stores = [pltpu.make_async_copy(one, out, sems.at[6 + i]) for i, (one, out) in enumerate(zip(sources, outs))]

    def begin(self):
        for copy in self.loads:
            copy.start()

    def enter(self):
        pass

    def first_length(self):
        return jnp.full((1, 1), self.lengths[lax.axis_index("blk"), 0, 0], jnp.int32).astype(F32)

    def need_tokens(self):
        self.loads[0].wait()

    def need_first(self):
        self.loads[2 + QKV].wait()

    def before_block(self, j):
        pass

    def after_forward(self, i):
        pass

    def need_cotangent(self):
        self.loads[1].wait()

    def need_proj(self):
        self.loads[2 + PROJ].wait()

    def need_mlp(self):
        self.loads[2 + EXPAND].wait()
        self.loads[2 + REDUCE].wait()

    def after_part(self, part):
        pass

    def have_proj(self):
        for which in (PROJ, EXPAND, REDUCE):
            self.stores[2 + which].start()

    def have_result(self):
        self.stores[0].start()

    def after_backward(self, i):
        pass

    def have_qkv(self, j):
        pass

    def have_vectors(self):
        self.stores[2 + QKV].start()

    def have_grad(self):
        self.stores[1].start()
        for copy in self.stores:
            copy.wait()


def local_kernel(lengths, vec, x_in, cot_in, w_qkv, w_proj, w_expand, w_reduce,
                 result, grad_x, g_qkv, g_proj, g_expand, g_reduce, g_vec, *scratch):
    b = Buffers(*scratch[:-1])
    b.vec[...] = vec[...]
    ins = (x_in, cot_in, w_qkv, w_proj, w_expand, w_reduce)
    outs = (result, grad_x, g_qkv, g_proj, g_expand, g_reduce)
    compute(b, Local(b, lengths, ins, outs, scratch[-1]))
    g_vec[...] = b.g_vec[...]


def run_local(lengths, vec, x_in, cot_in, weights):
    vmem, anywhere = pl.BlockSpec(memory_space=pltpu.VMEM), pl.BlockSpec(memory_space=pl.ANY)
    total, width = x_in.shape
    like = (x_in, x_in) + tuple(weights)
    return pl.pallas_call(
        local_kernel,
        out_shape=[jax.ShapeDtypeStruct(one.shape, BF) for one in like]
        + [jax.ShapeDtypeStruct((VEC_ROWS, width), F32)],
        in_specs=[pl.BlockSpec(memory_space=pltpu.SMEM), vmem] + [anywhere] * 6,
        out_specs=[anywhere] * 6 + [vmem],
        scratch_shapes=buffers(total, width, [one.shape for one in weights]) + [pltpu.SemaphoreType.DMA((12,))],
        compiler_params=pltpu.CompilerParams(vmem_limit_bytes=62 * 2**20),
    )(lengths, vec, x_in, cot_in, *weights)


UNITS = (
    (QKV, 0, LANES + TRIO), (QKV, LANES + TRIO, TRIO), (QKV, LANES + 2 * TRIO, TRIO), (QKV, LANES + 3 * TRIO, TRIO),
    (PROJ, 0, 6 * LANES),
    (EXPAND, 0, 8 * LANES), (EXPAND, 8 * LANES, 8 * LANES), (REDUCE, 0, 4 * LANES), (REDUCE, 0, 4 * LANES),
)
HALVES = {7: pl.ds(0, SPREAD[Z] // 2), 8: pl.ds(SPREAD[Z] // 2, SPREAD[Z] // 2)}
EARLY_UNITS, PROJ_UNITS, EXPAND_UNITS, REDUCE_UNITS = (0, 1, 2, 3), (4,), (5, 6), (7, 8)
VECTOR_TILES = ((QKV, 0), (PROJ, 4 * LANES), (PROJ, 5 * LANES))
CHUNK_COPIES = 6


def schedule():
    entries = {}

    def enter(t, which, stage, chunk):
        entries.setdefault(t, []).append((which, stage, chunk))

    for chunk in range(CHUNKS):
        for stage, later in enumerate((1, 3, 5, 7)):
            enter(chunk + later, EXPAND, stage, chunk)
        for stage, later in enumerate((1, 3, 4)):
            enter(chunk + later, REDUCE, stage, chunk)
    enter(CHUNKS + 3, REDUCE, None, 0)
    enter(CHUNKS + 6, REDUCE, 3, 0)
    for stage, t in enumerate((5, 7, 9, 11)):
        enter(t, PROJ, stage, 0)
    for number, times in enumerate(((8, 9, 10, 11), (10, 11, 12, 13), (12, 13, 14, 15), (13, 14, 15, 16))):
        for stage, t in enumerate(times):
            enter(t, QKV, stage, CHUNKS - 1 - number)
    return entries


SCHEDULE = schedule()


class Group:
    def __init__(self, b, ins, outs, scratch):
        self.b = b
        self.tokens, self.cotangent, self.vectors, self.shards = ins
        self.result, self.grad_x, self.outs, self.g_total = outs
        (self.lengths, self.own_lengths, self.own_qkv, self.own_vec, self.packed, self.turn, self.tile, self.arrived,
         self.local_sem, self.token_sem, self.ag_sem, self.rs_sem) = scratch
        self.weights = tuple(b[-4:])
        dp, blk = lax.axis_index("dp"), lax.axis_index("blk")
        z, y, x, c = dp // SPREAD[Y], dp % SPREAD[Y], blk // SPREAD[C], blk % SPREAD[C]
        self.mine = (z, y, x, c)
        self.index = dp * (SPREAD[X] * SPREAD[C]) + blk
        self.blk = blk
        n_blk = SPREAD[X] * SPREAD[C]
        self.others = [(dp, (blk + k) % n_blk) for k in range(1, n_blk)]
        z_places = [(z + k) % SPREAD[Z] for k in range(1, SPREAD[Z])]
        self.along = (
            [((place * SPREAD[Y] + y, blk), place) for place in z_places],
            [((dp + 1 - 2 * y, blk), 1 - y)],
            [((dp, blk + SPREAD[C] * (1 - 2 * x)), 1 - x)],
            [((dp, blk + 1 - 2 * c), 1 - c)],
        )
        height = self.tokens.shape[1]

        def rows(ref):
            return lambda i: ref.at[pl.ds(pl.multiple_of(i * height, height), height)]

        def part(ref):
            return lambda i: ref.at[i]

        moves = (
            (part(self.tokens), rows(b.x_in)),
            (part(self.cotangent), rows(b.cot)),
            (rows(b.hb), part(self.result)),
            (rows(b.act), part(self.grad_x)),
        )
        self.swaps = [
            [
                self.remote(source(device[1]), target(blk), self.token_sem.at[i, k], self.token_sem.at[4 + i, k], device)
                for k, device in enumerate(self.others)
            ]
            for i, (source, target) in enumerate(moves)
        ]
        self.kept = [
            pltpu.make_async_copy(source(blk), target(blk), self.local_sem.at[i])
            for i, (source, target) in enumerate(moves)
        ]

    @staticmethod
    def remote(source, target, send, recv, device):
        return pltpu.make_async_remote_copy(
            src_ref=source, dst_ref=target, send_sem=send, recv_sem=recv,
            device_id=device, device_id_type=pl.DeviceIdType.MESH,
        )

    @staticmethod
    def start(copies):
        for copy in copies:
            copy.start()

    @staticmethod
    def arrive(copies):
        for copy in copies:
            copy.wait_recv()

    @staticmethod
    def sent(copies):
        for copy in copies:
            copy.wait_send()

    def place(self, free, at=None):
        index = [slice(None) if axis in free else self.mine[axis] for axis in range(4)]
        for axis, value in (at or {}).items():
            index[axis] = value
        return tuple(index)


    def gather(self, unit, stage):
        which, first, columns = UNITS[unit]
        w, order = self.weights[which], GATHER_ORDER[which]
        cols = (slice(None), pl.ds(first, columns))

        def one(i, view, device):
            return self.remote(view, view, self.ag_sem.at[0, unit, i], self.ag_sem.at[1, unit, i], device)

        half = {Z: HALVES[unit]} if unit in HALVES else {}
        if stage == 0 and unit in HALVES:
            if unit != min(HALVES):
                return []
            half = {}
        if stage < 3:
            view = w.at[self.place(order[:stage], half) + cols]
            return [one(copies_before(order, stage) + k, view, device) for k, (device, _) in enumerate(self.along[order[stage]])]
        device, _ = self.along[C][0]
        last = order[2]
        if stage == 3:
            return [one(5, w.at[self.place(order[:2], half) + cols], device)]
        (_, other), = self.along[last]
        return [one(6, w.at[self.place(order[:2], {last: other, **half}) + cols], device)]

    def gather_on(self, units, stage):
        for unit in units:
            copies = self.gather(unit, stage)
            self.arrive(copies)
            self.sent(copies)
            if stage < 2:
                self.start(self.gather(unit, stage + 1))
            if stage in (1, 2):
                self.start(self.gather(unit, stage + 2))

    def gathered(self, units):
        for unit in units:
            for stage in (3, 4):
                copies = self.gather(unit, stage)
                self.arrive(copies)
                self.sent(copies)

    def unpack(self, tile):
        which, first = VECTOR_TILES[tile]
        w = self.weights[which]
        all_of = w[:, :, :, :, 0:PACKED, first : first + LANES].astype(F32)
        total = jnp.sum(all_of.reshape(-1, PACKED, LANES), axis=0)
        for i in range(PACKED):
            row, at = divmod(tile * PACKED + i, 4)
            self.b.vec[row : row + 1, at * LANES : (at + 1) * LANES] = total[i : i + 1, :]


    def chunk_view(self, which, chunk):
        if which == REDUCE:
            return chunk, slice(None)
        if which == QKV:
            return None, pl.ds(LANES + chunk * TRIO, TRIO) if chunk else pl.ds(0, LANES + TRIO)
        return None, pl.ds(chunk * 4 * LANES, 4 * LANES)

    def scatter(self, which, stage, chunk):
        w, order = self.weights[which], SCATTER_ORDER[which]
        axis, rest = order[stage], order[stage + 1 :]
        buffer = self.arrived[which][stage]
        at_z, cols = self.chunk_view(which, chunk)
        first = (which * CHUNKS + chunk) * CHUNK_COPIES + copies_before(order, stage)
        copies, terms = [], []
        for k, (device, other) in enumerate(self.along[axis]):
            at = {axis: other}
            if at_z is not None and Z in rest:
                at[Z] = at_z
            source = w.at[self.place(rest, at) + (slice(None), cols)]
            lead = (k,) if axis == Z else ()
            free = tuple(at_z if one == Z and at_z is not None else slice(None) for one in sorted(rest))
            target = buffer.at[lead + free + (slice(None), cols)]
            copies.append(self.remote(source, target, self.rs_sem.at[0, first + k], self.rs_sem.at[1, first + k], device))
            terms.append(target)
        return copies, terms

    def scatter_start(self, which, stage, chunk):
        self.start(self.scatter(which, stage, chunk)[0])

    def scatter_on(self, which, stage, chunk):
        w, order = self.weights[which], SCATTER_ORDER[which]
        copies, terms = self.scatter(which, stage, chunk)
        self.arrive(copies)
        rest = order[stage + 1 :]
        at_z, cols = self.chunk_view(which, chunk)
        at = {Z: at_z} if at_z is not None and Z in rest else None
        here = self.place(rest, at) + (slice(None), cols)
        sums = None
        if which == QKV and not chunk:
            sums = self.vector_sums(self.place(rest), terms)
        if len(terms) == 1 and rest:
            w[here] = w[here] + terms[0][...]
        else:
            total = w[here].astype(F32)
            for term in terms:
                total = total + term[...].astype(F32)
            if rest:
                w[here] = total.astype(BF)
            else:
                self.keep(which, chunk, total)
        if sums is not None:
            half = PACKED // 2
            exact = sums[..., :half, :] + sums[..., half:, :]
            if rest:
                high = exact.astype(BF).astype(F32)
                w[self.place(rest) + (slice(None), pl.ds(0, LANES))] = jnp.concatenate([high, exact - high], axis=-2).astype(BF)
            else:
                self.g_total[...] = exact
        if rest and not (which == REDUCE and rest == (Z,)):
            self.scatter_start(which, stage + 1, chunk)
        self.sent(copies)

    def vector_sums(self, here, terms):
        total = self.weights[QKV][here + (slice(None), pl.ds(0, LANES))].astype(F32)
        for term in terms:
            total = total + term[...][..., 0:LANES].astype(F32)
        return total

    def keep(self, which, chunk, total):
        out = self.outs[which]
        if which == QKV:
            width = out.shape[1] // 3
            if not chunk:
                total = total[:, LANES:]
            for i in range(3):
                out[:, i * width + chunk * LANES : i * width + (chunk + 1) * LANES] = total[:, i * LANES : (i + 1) * LANES]
        else:
            out[:, self.chunk_view(which, chunk)[1]] = total

    def tick(self, t):
        for which, stage, chunk in SCHEDULE.get(t, ()):
            if stage is None:
                self.scatter_start(which, 3, chunk)
            else:
                self.scatter_on(which, stage, chunk)


    def spread_vectors(self):
        g_vec, lines, tile = self.b.g_vec, self.packed, self.tile
        parts = g_vec.shape[1] // LANES
        for i in range(lines.shape[0]):
            lines[i : i + 1, :] = g_vec[i // parts : i // parts + 1, i % parts * LANES : (i % parts + 1) * LANES]
        tile[...] = jnp.zeros_like(tile)
        devices = math.prod(SPREAD)
        for device in range(0, devices, SPREAD[C]):
            row = 0
            for i, one in enumerate(self.own_vec):
                size = one.shape[0]
                if device * size % LANES == 0:
                    at = row + device * size // LANES
                    tile[i : i + 1, :] = lines[at : at + 1, :]
                row += devices * size // LANES
            high = tile[...].astype(BF).astype(F32)
            value = jnp.concatenate([high, tile[...] - high], axis=0).astype(BF)
            pair = device // SPREAD[C]
            place = (pair // (SPREAD[X] * SPREAD[Y]), pair // SPREAD[X] % SPREAD[Y], pair % SPREAD[X])
            for core in range(SPREAD[C]):
                self.weights[QKV][place + (core, slice(None), pl.ds(0, LANES))] = value


    def begin(self):
        self.peers = self.others + [device for axis in (Y, Z) for device, _ in self.along[axis]]
        for device in self.peers:
            pl.semaphore_signal(
                pltpu.get_barrier_semaphore(), inc=1, device_id=device, device_id_type=pl.DeviceIdType.MESH
            )
        count = len(self.vectors)
        loads = [
            pltpu.make_async_copy(one, target, self.local_sem.at[4 + i])
            for i, (one, target) in enumerate(zip(self.vectors, self.own_vec))
        ]
        loads.append(pltpu.make_async_copy(self.shards[QKV], self.own_qkv, self.local_sem.at[8 + count]))
        width = self.shards[PROJ].shape[1]
        slots = [self.weights[which].at[self.mine] for which in range(4)]
        self.own = [
            pltpu.make_async_copy(
                self.shards[which], slots[which].at[:, pl.ds(0, self.shards[which].shape[1])],
                self.local_sem.at[4 + count + which],
            )
            for which in (PROJ, EXPAND, REDUCE)
        ]
        loads.append(pltpu.make_async_copy(self.lengths, self.own_lengths, self.local_sem.at[4 + count + QKV]))
        loads[-2], loads[-1] = loads[-1], loads[-2]
        self.start(loads + self.own + self.kept[:2])
        self.packed[...] = jnp.zeros_like(self.packed)
        row = 0
        for load, own in zip(loads, self.own_vec):
            load.wait()
            size = own.shape[0]
            self.turn[...] = jnp.zeros_like(self.turn)
            self.turn[0:1, 0:size] = own[...].astype(F32).reshape(1, size)
            at = self.index * size
            self.packed[pl.ds(row + at // LANES, 1), :] = pltpu.roll(self.turn[...], at % LANES, 1)[0:1, :]
            row += math.prod(SPREAD) * size // LANES
        for load in loads[count:]:
            load.wait()
        w = self.weights[QKV]
        for j in range(width // LANES):
            for i in range(3):
                to = LANES + j * TRIO + i * LANES
                w[self.mine + (slice(None), pl.ds(to, LANES))] = self.own_qkv[:, i * width + j * LANES : i * width + (j + 1) * LANES]
        for tile, (which, first) in enumerate(VECTOR_TILES):
            values = self.packed[tile * PACKED : (tile + 1) * PACKED, :].astype(BF)
            self.weights[which][self.mine + (slice(None), pl.ds(first, LANES))] = values

    def enter(self):
        pl.semaphore_wait(pltpu.get_barrier_semaphore(), len(self.peers))
        for unit in EARLY_UNITS:
            self.start(self.gather(unit, 0))
        self.start(self.swaps[0])
        for copy in self.own:
            copy.wait()
        for unit in PROJ_UNITS + EXPAND_UNITS:
            self.start(self.gather(unit, 0))

    def first_length(self):
        first = self.own_lengths[0][0:1, :].astype(F32)
        lane = lax.broadcasted_iota(jnp.int32, first.shape, 1)
        return jnp.sum(jnp.where(lane == self.blk, first, 0.0), axis=1, keepdims=True)

    def need_tokens(self):
        self.gather_on(EARLY_UNITS, 0)
        self.gather_on(EARLY_UNITS[:2], 1)
        self.gather_on(EARLY_UNITS[:1], 2)
        self.gather_on(EARLY_UNITS[2:3], 1)
        self.gather_on(EARLY_UNITS[1:2], 2)
        self.gather_on(EARLY_UNITS[3:], 1)
        self.start(self.gather(REDUCE_UNITS[0], 0))
        self.gathered(EARLY_UNITS[:1])
        self.unpack(0)
        self.kept[0].wait()
        self.arrive(self.swaps[0])
        self.sent(self.swaps[0])
        self.start(self.swaps[1])

    def need_first(self):
        self.gather_on(PROJ_UNITS + EXPAND_UNITS, 0)
        self.gather_on(EARLY_UNITS[2:3], 2)

    def before_block(self, j):
        for unit in EARLY_UNITS[1:]:
            pl.when(j == unit)(lambda unit=unit: self.gathered((unit,)))

    def after_forward(self, i):
        steps = (
            lambda: (self.gather_on(EARLY_UNITS[3:], 2), self.gather_on(REDUCE_UNITS, 0)),
            lambda: None,
            lambda: self.gather_on(PROJ_UNITS, 1),
            lambda: (self.gather_on(REDUCE_UNITS, 1), self.gather_on(EXPAND_UNITS[:1], 1)),
            lambda: self.gather_on(PROJ_UNITS, 2),
            lambda: self.gather_on(EXPAND_UNITS[1:], 1),
            lambda: self.gather_on(EXPAND_UNITS[:1], 2),
            lambda: self.gather_on(REDUCE_UNITS[:1], 2),
        )
        for at, step in enumerate(steps):
            pl.when(i == at)(lambda step=step: [step(), None][1])

    def need_cotangent(self):
        self.kept[1].wait()
        self.arrive(self.swaps[1])
        self.sent(self.swaps[1])

    def need_proj(self):
        self.gathered(PROJ_UNITS)
        self.unpack(1)
        self.unpack(2)

    def need_mlp(self):
        self.gathered(EXPAND_UNITS[:1] + REDUCE_UNITS[:1])

    def after_part(self, part):
        for at in range(CHUNKS):
            @pl.when(part == at)
            def _(at=at):
                self.scatter_start(REDUCE, 0, at)
                self.scatter_start(EXPAND, 0, at)
                if at == 0:
                    self.gather_on(EXPAND_UNITS[1:] + REDUCE_UNITS[1:], 2)
                if at == 1:
                    self.gathered(EXPAND_UNITS[1:] + REDUCE_UNITS[1:])
                self.tick(at)

    def have_proj(self):
        self.scatter_start(PROJ, 0, 0)
        self.tick(CHUNKS)

    def have_result(self):
        self.start(self.swaps[2] + self.kept[2:3])

    def after_backward(self, i):
        for at in range(2 * CHUNKS):
            pl.when(i == at)(lambda at=at: self.tick(CHUNKS + 1 + at))

    def have_qkv(self, j):
        for at in range(1, CHUNKS):
            pl.when(j == at)(lambda at=at: self.scatter_start(QKV, 0, at))

    def have_vectors(self):
        self.spread_vectors()
        self.scatter_start(QKV, 0, 0)

    def have_grad(self):
        end = 3 * CHUNKS + 1
        self.tick(end)
        self.start(self.swaps[3] + self.kept[3:4])
        for t in range(end + 1, max(SCHEDULE) + 1):
            self.tick(t)
        for i in (2, 3):
            self.kept[i].wait()
            self.arrive(self.swaps[i])
            self.sent(self.swaps[i])


N_VECTORS = 8


def group_kernel(*refs):
    refs = list(refs)

    def take(n):
        taken = refs[:n]
        del refs[:n]
        return taken

    (lengths,), vectors, (tokens, cotangent), shards = take(1), take(N_VECTORS), take(2), take(4)
    (result, grad_x), outs, (g_total,) = take(2), take(4), take(1)
    b = Buffers(*take(len(Buffers._fields)))
    (own_lengths, own_qkv), own_vec, (packed, turn, tile) = take(2), take(N_VECTORS), take(3)
    arrived = [take(4) for _ in range(4)]
    scratch = [lengths, own_lengths, own_qkv, own_vec, packed, turn, tile, arrived] + refs
    group = Group(b, (tokens, cotangent, vectors, shards), (result, grad_x, outs, g_total), scratch)
    compute(b, group)


def run_group(lengths, vectors, tokens, cotangent, weights):
    vmem, anywhere = pl.BlockSpec(memory_space=pltpu.VMEM), pl.BlockSpec(memory_space=pl.ANY)
    blk, height, width = tokens.shape
    extra = [0] * 4
    for which, _ in VECTOR_TILES:
        extra[which] += LANES
    shapes = [SPREAD + (one.shape[0], one.shape[1] + more) for one, more in zip(weights, extra)]
    landing = []
    for which, shape in enumerate(shapes):
        for stage, axis in enumerate(SCATTER_ORDER[which]):
            rest = sorted(SCATTER_ORDER[which][stage + 1 :])
            lead = (SPREAD[Z] - 1,) if axis == Z else ()
            landing.append(pltpu.VMEM(lead + tuple(SPREAD[one] for one in rest) + shape[4:], BF))
    packed_rows = math.prod(SPREAD) * sum(one.shape[0] for one in vectors) // LANES
    dma = pltpu.SemaphoreType.DMA
    return pl.pallas_call(
        group_kernel,
        out_shape=[jax.ShapeDtypeStruct(tokens.shape, BF)] * 2
        + [jax.ShapeDtypeStruct(one.shape, F32) for one in weights]
        + [jax.ShapeDtypeStruct((N_VECTORS, LANES), F32)],
        in_specs=[anywhere] * (N_VECTORS + 7),
        out_specs=[anywhere] * 2 + [vmem] * 5,
        scratch_shapes=buffers(blk * height, width, shapes)
        + [pltpu.VMEM(lengths.shape, lengths.dtype), pltpu.VMEM(weights[QKV].shape, BF)]
        + [pltpu.VMEM(one.shape, BF) for one in vectors]
        + [pltpu.VMEM((packed_rows, LANES), F32), pltpu.VMEM((8, LANES), F32), pltpu.VMEM((N_VECTORS, LANES), F32)]
        + landing
        + [dma((17,)), dma((8, 3)), dma((2, len(UNITS), 7)), dma((2, 4 * CHUNKS * CHUNK_COPIES))],
        compiler_params=pltpu.CompilerParams(
            vmem_limit_bytes=62 * 2**20, collective_id=0, has_side_effects=True
        ),
    )(lengths, *vectors, tokens, cotangent, *weights)


def finish_kernel(result, grad_x, g_qkv, g_proj, g_expand, g_reduce, g_vec, *refs):
    sources = (result, grad_x, g_qkv, g_proj, g_expand, g_reduce)
    outs, refs = refs[: 6 + N_VECTORS], refs[6 + N_VECTORS :]
    held, short = refs[:6], refs[6 : 6 + N_VECTORS]
    turn, sems = refs[6 + N_VECTORS :]
    loads, stores = [], []
    for source, to, out in zip(sources, held, outs):
        places = range(source.shape[0]) if len(source.shape) == 3 else (slice(None),)
        for place in places:
            sem = len(loads)
            loads.append(pltpu.make_async_copy(source.at[place], to.at[place], sems.at[0, sem]))
            stores.append(pltpu.make_async_copy(to.at[place], out.at[place], sems.at[1, sem]))
    for load in loads:
        load.start()
    handed = []
    index = lax.axis_index("dp") * lax.axis_size("blk") + lax.axis_index("blk")
    for i, one in enumerate(short):
        size = one.shape[0]
        at = index * size
        turn[0:1, :] = g_vec[i : i + 1, :]
        turned = pltpu.roll(turn[...], (LANES - at % LANES) % LANES, 1)
        one[...] = turned[0:1, 0:size].reshape(size)
        handed.append(pltpu.make_async_copy(one, outs[6 + i], sems.at[0, len(loads) + i]))
        handed[-1].start()
    for load, store in zip(loads, stores):
        load.wait()
        store.start()
    for store in stores + handed:
        store.wait()


def finish(values, sizes):
    vmem, anywhere = pl.BlockSpec(memory_space=pltpu.VMEM), pl.BlockSpec(memory_space=pl.ANY)
    long = [(one.shape, one.dtype) for one in values[:6]]
    short = [((size,), F32) for size in sizes]
    return pl.pallas_call(
        finish_kernel,
        out_shape=[jax.ShapeDtypeStruct(*one) for one in long + short],
        in_specs=[anywhere] * 6 + [vmem],
        out_specs=[anywhere] * (6 + len(sizes)),
        scratch_shapes=[pltpu.VMEM(*one) for one in long + short]
        + [pltpu.VMEM((8, LANES), F32)]
        + [pltpu.SemaphoreType.DMA((2, 4 + 2 * values[0].shape[0] + len(sizes)))],
    )(*values)


def by_collectives(lengths, vectors, sizes, tokens, cotangent, weights):
    axes = ("dp", "blk")
    width = tokens.shape[2]
    blocks = width // LANES

    def exchange(rows):
        return lax.all_to_all(rows.reshape(tokens.shape), "blk", 0, 0, tiled=True)

    packed = lax.all_gather(jnp.concatenate(vectors), axes, axis=0)
    starts = [sum(sizes[:i]) for i in range(len(sizes))]
    full = [packed[:, at : at + size].reshape(-1, width) for at, size in zip(starts, sizes)]
    vec = jnp.concatenate(full, axis=0).astype(F32)
    vec = jnp.pad(vec, ((0, VEC_ROWS - vec.shape[0]), (0, 0)))
    whole = [lax.all_gather(one, axes, axis=0, tiled=True) for one in weights]
    whole[QKV] = whole[QKV].reshape(width, 3, blocks, LANES).swapaxes(1, 2).reshape(width, 3 * width)
    result, grad_x, *grads, g_vec = run_local(
        lengths, vec, exchange(tokens).reshape(-1, width), exchange(cotangent).reshape(-1, width), whole
    )
    grads[QKV] = grads[QKV].reshape(width, blocks, 3, LANES).swapaxes(1, 2).reshape(width, 3 * width)
    grads = [lax.psum_scatter(one.astype(F32), axes, scatter_dimension=0, tiled=True) for one in grads]
    g_vec = lax.psum(g_vec, axes).reshape(-1)
    index = lax.axis_index(axes)
    devices = lax.axis_size(axes)
    own = [
        lax.dynamic_slice(g_vec, (devices * at + index * size,), (size,)) for at, size in zip(starts, sizes)
    ]
    return (exchange(result), exchange(grad_x), *grads, *own)


def body(
    tokens, lengths, attn_gain, attn_shift, w_qkv, qv_bias, w_proj, proj_bias,
    mlp_gain, mlp_shift, w_expand, expand_bias, w_reduce, reduce_bias, cotangent,
):
    vectors = (attn_gain, attn_shift, qv_bias, proj_bias, mlp_gain, mlp_shift, reduce_bias, expand_bias)
    sizes = [one.shape[0] for one in vectors]
    weights = (w_qkv, w_proj, w_expand, w_reduce)
    sized = (lax.axis_size("dp"), lax.axis_size("blk")) == (SPREAD[Z] * SPREAD[Y], SPREAD[X] * SPREAD[C])
    if sized and all(one.shape[0] % 16 == 0 for one in weights):
        outs = finish(run_group(jnp.transpose(lengths, (1, 2, 0)), vectors, tokens, cotangent, weights), sizes)
    else:
        outs = by_collectives(lengths, vectors, sizes, tokens, cotangent, weights)
    result, grad_x, g_qkv, g_proj, g_expand, g_reduce, ag, as_, qv, pb, mg, ms, rb, eb = outs
    return (result, grad_x, ag, as_, g_qkv, qv, g_proj, pb, mg, ms, g_expand, eb, g_reduce, rb)


def solution(mesh):
    both = ("dp", "blk")
    rows = P(None, both, None)
    vector, matrix = P(both), P(both, None)
    weights = (
        vector, vector, matrix, vector, matrix, vector, vector, vector, matrix, vector, matrix, vector,
    )
    return jax.shard_map(
        body,
        mesh=mesh,
        in_specs=(rows, P(None, "dp", None)) + weights + (rows,),
        out_specs=(rows, rows) + weights,
        check_vma=False,
    )
```

```python
import math
import typing

import jax
import jax.numpy as jnp
from jax import lax
from jax.experimental import pallas as pl
from jax.experimental.pallas import tpu as pltpu
from jax.sharding import PartitionSpec as P

HEAD_DIM = 32
LONG_IMG = 784
SHORT_IMG = 196
LANES = 128
HEADS_IN_BLOCK = LANES // HEAD_DIM
LONG_KEYS = 896
BF = jnp.bfloat16
F32 = jnp.float32
epsilon = 1e-06
LOG2E = math.log2(math.e)
SCALE = 1.0 / math.sqrt(HEAD_DIM)
MASKED = -1e30
ROWS = 512
A_GAIN, A_SHIFT, Q_BIAS, V_BIAS, P_BIAS, M_GAIN, M_SHIFT, R_BIAS, E_BIAS = range(9)
VEC_ROWS = 16
PACKED = 16
TRIO = 3 * LANES
CHUNKS = 4
Z, Y, X, C = range(4)
SPREAD = (4, 2, 2, 2)
QKV, PROJ, EXPAND, REDUCE = range(4)
GATHER_ORDER = ((X, Z, Y), (X, Z, Y), (X, Z, Y), (Z, Y, X))
SCATTER_ORDER = ((C, X, Y, Z), (C, Y, Z, X), (C, Y, Z, X), (C, X, Y, Z))


def copies_before(order, stage):
    return sum(SPREAD[axis] - 1 for axis in order[:stage])


def nt(left, right):
    return lax.dot_general(left, right, (((1,), (1,)), ((), ())), preferred_element_type=F32)


def nn(left, right):
    return lax.dot_general(left, right, (((1,), (0,)), ((), ())), preferred_element_type=F32)


def tn(left, right):
    return lax.dot_general(left, right, (((0,), (0,)), ((), ())), preferred_element_type=F32)


def pieces(total, size):
    return [(at, min(size, total - at)) for at in range(0, total, size)]


def lanes(rows, width=LANES):
    return lax.broadcasted_iota(jnp.int32, (rows, width), 1)


def to_canonical(swapped, natural, moved):
    total = natural.shape[0]
    tail = LONG_IMG + SHORT_IMG
    moved[0:LONG_IMG] = natural[SHORT_IMG:tail]
    moved[LONG_IMG:tail] = natural[0:SHORT_IMG]
    moved[tail:total] = natural[tail:total]


def to_natural(ordered, moved):
    total = ordered.shape[0]
    tail = LONG_IMG + SHORT_IMG
    moved[SHORT_IMG:tail] = ordered[0:LONG_IMG]
    moved[0:SHORT_IMG] = ordered[LONG_IMG:tail]
    moved[tail:total] = ordered[tail:total]


def norm_parts(values):
    centered = values - jnp.mean(values, axis=-1, keepdims=True)
    inverse = lax.rsqrt(jnp.mean(centered * centered, axis=-1, keepdims=True) + epsilon)
    return centered * inverse, inverse


def norm_back(gradient, normed, inverse, gain):
    scaled = gradient * gain
    return inverse * (
        scaled
        - jnp.mean(scaled, axis=-1, keepdims=True)
        - normed * jnp.mean(scaled * normed, axis=-1, keepdims=True)
    )


def gelu_parts(values):
    phi = 0.5 + 0.5 * lax.erf(values * math.sqrt(0.5))
    bell = jnp.exp2(values * values * (-0.5 * LOG2E) + math.log2(1.0 / math.sqrt(2.0 * math.pi)))
    return values * phi, phi + values * bell


def fill_masks(aug_q, aug_k):
    total = aug_q.shape[0]
    row = lax.broadcasted_iota(jnp.int32, (total, LANES), 0)
    segment = (row >= LONG_IMG).astype(jnp.int32) + (row >= LONG_IMG + SHORT_IMG).astype(jnp.int32)
    place = lanes(total) % HEAD_DIM
    aug_q[...] = jnp.where(place == segment, 1.0, 0.0).astype(BF)
    aug_k[...] = jnp.where((place < 3) & (place != segment), MASKED, 0.0).astype(BF)


def attend_tiles(total, size):
    tail = total - LONG_IMG
    first = total - 2 * LANES
    return [(at, n, 0, LONG_KEYS, True, at) for at, n in pieces(LONG_IMG, size)] + [
        (LONG_IMG + at, n, first, 2 * LANES, False, at) for at, n in pieces(tail, size)
    ]


def get(ref, at, n):
    cols = pl.ds(at if isinstance(at, int) else pl.multiple_of(at, LANES), n)
    value = ref[:, cols] if len(ref.shape) == 2 else ref[:, :, :, :, :, cols]
    return value.reshape(-1, n)


def put(ref, value, at, n):
    cols = pl.ds(at if isinstance(at, int) else pl.multiple_of(at, LANES), n)
    if len(ref.shape) == 2:
        ref[:, cols] = value
    else:
        ref[:, :, :, :, :, cols] = value.reshape(ref.shape[:-1] + (n,))


def get_rows(ref, part, parts):
    if len(ref.shape) == 2:
        rows = ref.shape[0] // parts
        return ref[pl.ds(pl.multiple_of(part * rows, rows), rows)]
    each = ref.shape[0] // parts
    value = ref[pl.ds(part * each, each)]
    return value.reshape(-1, value.shape[-1])


def put_rows(ref, value, part, parts):
    if len(ref.shape) == 2:
        rows = ref.shape[0] // parts
        ref[pl.ds(pl.multiple_of(part * rows, rows), rows)] = value
    else:
        each = ref.shape[0] // parts
        ref[pl.ds(part * each, each)] = value.reshape((each,) + ref.shape[1:])


def of_block(ref, j, offset=0):
    return ref.at[:, pl.ds(pl.multiple_of(offset + j * LANES, LANES), LANES)]


def of_trio(ref, j, which):
    return ref.at[:, pl.ds(pl.multiple_of(j * TRIO + which * LANES, LANES), LANES)]


def forward_head(j, head, qkv, attended, inverse, e_long, e_tail, aug_q, aug_k, size=400):
    total, width = attended.shape
    q, k, v = (of_trio(qkv, j, i) for i in range(3))
    attended, inverse = of_block(attended, j), of_block(inverse, j)
    mine = lanes(1) // HEAD_DIM == head
    ka = jnp.where(mine, k[...], aug_k[...])
    va = jnp.where(mine, v[...], jnp.ones_like(aug_k[...]))
    at = j * HEADS_IN_BLOCK + head
    for row, rows, key, keys, is_long, place in attend_tiles(total, size):
        here = pl.ds(row, rows)
        scores = nt(jnp.where(mine, q[here], aug_q[here]), ka[key : key + keys])
        exps = jnp.exp2(scores - jnp.max(scores, axis=1, keepdims=True)).astype(BF)
        store = e_long if is_long else e_tail
        store[at, place : place + rows, :] = exps
        product = nn(exps, va[key : key + keys])
        inv = 1.0 / pltpu.roll(product, HEAD_DIM, 1)
        attended[here] = jnp.where(mine, (product * inv).astype(BF), attended[here])
        inverse[here] = jnp.where(mine, inv, inverse[here])


def backward_prepare(j, qkv, attended, inverse, d_att, scaled_b, aug_b, q_t, s_t, k_b):
    total, width = attended.shape
    for at, n in pieces(total, ROWS):
        here = pl.ds(at, n)
        scaled = of_block(d_att, j)[here].astype(F32) * of_block(inverse, j)[here]
        inner = scaled * of_block(attended, j)[here].astype(F32)
        from_group = lax.broadcasted_iota(jnp.int32, (LANES, LANES), 0) // HEAD_DIM
        to_group = lanes(LANES) // HEAD_DIM
        spread = jnp.where((from_group + 1) % HEADS_IN_BLOCK == to_group, 1.0, 0.0).astype(BF)
        high = inner.astype(BF)
        low = (inner - high.astype(F32)).astype(BF)
        sums = nn(high, spread) + nn(low, spread)
        sum_high = sums.astype(BF)
        sum_low = (sums - sum_high.astype(F32)).astype(BF)
        place = lanes(n) % HEAD_DIM
        zeros = jnp.zeros_like(sum_high)
        aug_b[here] = jnp.where(place == 0, -sum_high, jnp.where(place == 1, -sum_low, zeros))
        scaled = scaled.astype(BF)
        scaled_b[here] = scaled
        s_t[:, at : at + n] = scaled.T
        q_t[:, at : at + n] = of_trio(qkv, j, 0)[here].T
        k_b[here] = of_trio(qkv, j, 1)[here]


def backward_head(j, head, qkv, e_long, e_tail, scaled_b, aug_b, q_t, s_t, k_b, dk_t, dv_t, size=400):
    total = scaled_b.shape[0]
    dq, v = of_trio(qkv, j, 0), of_trio(qkv, j, 2)
    mine = lanes(1) // HEAD_DIM == head
    following = lanes(1) // HEAD_DIM == (head + 1) % HEADS_IN_BLOCK
    va = jnp.where(mine, v[...], jnp.ones_like(k_b[...]))
    at = j * HEADS_IN_BLOCK + head
    of_head = pl.ds(pl.multiple_of(head * HEAD_DIM, HEAD_DIM), HEAD_DIM)
    sums_of = {}
    for row, rows, key, keys, is_long, where in attend_tiles(total, size):
        here = pl.ds(row, rows)
        store = e_long if is_long else e_tail
        exps = store[at, where : where + rows, :]
        side = jnp.where(following, aug_b[here], jnp.zeros_like(aug_b[here]))
        left = jnp.where(mine, scaled_b[here], side)
        d_scores = (exps.astype(F32) * nt(left, va[key : key + keys])).astype(BF)
        dq_here = (nn(d_scores, k_b[key : key + keys]) * SCALE).astype(BF)
        dq[here] = jnp.where(mine, dq_here, dq[here])
        more_v = nn(s_t[of_head, row : row + rows], exps)
        more_k = nn(q_t[of_head, row : row + rows], d_scores)
        if is_long in sums_of:
            more_v, more_k = sums_of[is_long][0] + more_v, sums_of[is_long][1] + more_k
        sums_of[is_long] = (more_v, more_k)
    first = total - 2 * LANES
    both = LONG_KEYS - first
    for ref, which, factor in ((dv_t, 0, 1.0), (dk_t, 1, 1.0 / LOG2E)):
        long_part, tail_part = (sums_of[is_long][which] * factor for is_long in (True, False))
        ref[of_head, 0:first] = long_part[:, :first].astype(BF)
        ref[of_head, first:LONG_KEYS] = (long_part[:, first:] + tail_part[:, :both]).astype(BF)
        ref[of_head, LONG_KEYS:total] = tail_part[:, both:].astype(BF)


def trio_columns(ref, j, width):
    return ref.shape[-1] - 3 * width + j * TRIO


def all_forward(b, transfers):
    total, width = b.attended.shape
    unrolled = 2

    def block(j, carried):
        transfers.before_block(j)
        here = pl.ds(pl.multiple_of(j * LANES, LANES), LANES)
        w_trio = get(b.w_qkv, trio_columns(b.w_qkv, j, width), TRIO)
        for at, n in pieces(total, ROWS):
            projected = nn(b.x_in[at : at + n], w_trio)
            q, k, v = (projected[:, i * LANES : (i + 1) * LANES] for i in range(3))
            q = (q + b.vec[Q_BIAS : Q_BIAS + 1, here]) * (SCALE * LOG2E)
            v = v + b.vec[V_BIAS : V_BIAS + 1, here]
            for i, value in enumerate((q, k, v)):
                of_trio(b.qkv, j, i)[at : at + n] = value.astype(BF)

        def step(i, inside):
            for one in range(unrolled):
                forward_head(
                    j, i * unrolled + one, b.qkv, b.attended, b.inverse,
                    b.e_long, b.e_tail, b.aug_q, b.aug_k,
                )
            transfers.after_forward(j * (HEADS_IN_BLOCK // unrolled) + i)
            return inside

        lax.fori_loop(0, HEADS_IN_BLOCK // unrolled, step, 0)
        return carried

    lax.fori_loop(0, width // LANES, block, 0)


def weight_of_block(b, j, transfers):
    trio = pl.ds(pl.multiple_of(j * TRIO, LANES), TRIO)
    at = trio_columns(b.w_qkv, j, b.attended.shape[1])
    put(b.w_qkv, nn(b.ha_t[...], b.qkv[:, trio]).astype(BF), at, TRIO)
    transfers.have_qkv(j)


def all_backward(b, transfers):
    total, width = b.attended.shape
    unrolled = 2
    keep = (b.scaled_b, b.aug_b, b.q_t, b.s_t, b.k_b)

    blocks = width // LANES

    def block(number, carried):
        j = blocks - 1 - number
        pl.when(number > 0)(lambda: weight_of_block(b, j + 1, transfers))
        backward_prepare(j, b.qkv, b.attended, b.inverse, b.d_exp, *keep)

        def step(i, inside):
            for one in range(unrolled):
                backward_head(
                    j, i * unrolled + one, b.qkv, b.e_long, b.e_tail, *keep, b.dk_t, b.dv_t
                )
            transfers.after_backward(number * (HEADS_IN_BLOCK // unrolled) + i)
            return inside

        lax.fori_loop(0, HEADS_IN_BLOCK // unrolled, step, 0)
        of_trio(b.qkv, j, 1)[...] = b.dk_t[...].T
        of_trio(b.qkv, j, 2)[...] = b.dv_t[...].T
        here = pl.ds(pl.multiple_of(j * LANES, LANES), LANES)
        trio = pl.ds(pl.multiple_of(j * TRIO, LANES), TRIO)
        for row, which in ((Q_BIAS, 0), (V_BIAS, 2)):
            values = of_trio(b.qkv, j, which)[...].astype(F32)
            b.g_vec[row : row + 1, here] = jnp.sum(values, axis=0, keepdims=True)
        w_trio = get(b.w_qkv, trio_columns(b.w_qkv, j, width), TRIO)
        for at, n in pieces(total, ROWS):
            b.acc_b[at : at + n] = b.acc_b[at : at + n] + nt(b.qkv[at : at + n, trio], w_trio)
        return carried

    lax.fori_loop(0, blocks, block, 0)


class Buffers(typing.NamedTuple):
    x_in: typing.Any
    ha_t: typing.Any
    cot: typing.Any
    xc: typing.Any
    qkv: typing.Any
    attended: typing.Any
    inverse: typing.Any
    e_long: typing.Any
    e_tail: typing.Any
    aug_q: typing.Any
    aug_k: typing.Any
    middle: typing.Any
    acc_a: typing.Any
    acc_b: typing.Any
    hb: typing.Any
    act: typing.Any
    d_exp: typing.Any
    scaled_b: typing.Any
    aug_b: typing.Any
    q_t: typing.Any
    s_t: typing.Any
    k_b: typing.Any
    dk_t: typing.Any
    dv_t: typing.Any
    vec: typing.Any
    g_vec: typing.Any
    w_qkv: typing.Any
    w_proj: typing.Any
    w_expand: typing.Any
    w_reduce: typing.Any


def buffers(total, width, weights):
    heads = width // HEAD_DIM
    rows, lane, turned = (total, width), (total, LANES), (LANES, total)
    shapes = Buffers(
        x_in=(rows, BF),
        ha_t=((width, total), BF),
        cot=(rows, BF),
        xc=(rows, BF),
        qkv=((total, 3 * width), BF),
        attended=(rows, BF),
        inverse=(rows, F32),
        e_long=((heads, LONG_IMG, LONG_KEYS), BF),
        e_tail=((heads, total - LONG_IMG, 2 * LANES), BF),
        aug_q=(lane, BF),
        aug_k=(lane, BF),
        middle=(rows, F32),
        acc_a=(rows, F32),
        acc_b=(rows, F32),
        hb=(rows, BF),
        act=(rows, BF),
        d_exp=(rows, BF),
        scaled_b=(lane, BF),
        aug_b=(lane, BF),
        q_t=(turned, BF),
        s_t=(turned, BF),
        k_b=(lane, BF),
        dk_t=(turned, BF),
        dv_t=(turned, BF),
        vec=((VEC_ROWS, width), F32),
        g_vec=((VEC_ROWS, width), F32),
        w_qkv=(weights[QKV], BF),
        w_proj=(weights[PROJ], BF),
        w_expand=(weights[EXPAND], BF),
        w_reduce=(weights[REDUCE], BF),
    )
    return [pltpu.VMEM(*one) for one in shapes]


def compute(b, transfers):
    total, width = b.xc.shape
    ff = b.w_expand.shape[-1]
    acc_a, acc_b, vec, g_vec = b.acc_a, b.acc_b, b.vec, b.g_vec

    def by_rows(function):
        def step(i, carried):
            function(pl.ds(pl.multiple_of(i * ROWS, ROWS), ROWS))
            return carried

        lax.fori_loop(0, total // ROWS, step, 0)

    def vector(row):
        return vec[pl.ds(row, 1), :]

    def add_sum(row, values):
        g_vec[pl.ds(row, 1), :] = g_vec[pl.ds(row, 1), :] + jnp.sum(values, axis=0, keepdims=True)

    def load(source):
        @by_rows
        def _(rows):
            acc_a[rows] = source[rows].astype(F32)

        to_canonical(swapped, acc_a, acc_b)

    def loaded(rows):
        return jnp.where(swapped, acc_b[rows], acc_a[rows])

    def unload(values, moved, target):
        to_natural(values, moved)

        @by_rows
        def _(rows):
            target[rows] = jnp.where(swapped, moved[rows], values[rows]).astype(BF)

    transfers.begin()
    g_vec[...] = jnp.zeros_like(g_vec)
    fill_masks(b.aug_q, b.aug_k)
    transfers.enter()
    transfers.need_tokens()
    swapped = jnp.broadcast_to(transfers.first_length(), (1, width)) == SHORT_IMG
    load(b.x_in)

    @by_rows
    def _(rows):
        values = loaded(rows)
        b.xc[rows] = values.astype(BF)
        normed, _ = norm_parts(values)
        b.x_in[rows] = (normed * vector(A_GAIN) + vector(A_SHIFT)).astype(BF)

    transfers.need_first()
    for at, n in pieces(total, ROWS):
        b.ha_t[:, at : at + n] = b.x_in[at : at + n].T

    all_forward(b, transfers)

    transfers.need_cotangent()
    cot, middle, hb, act, d_exp, attended = b.cot, b.middle, b.hb, b.act, b.d_exp, b.attended
    w_proj, w_expand, w_reduce = b.w_proj, b.w_expand, b.w_reduce
    load(cot)

    @by_rows
    def _(rows):
        cot[rows] = loaded(rows).astype(BF)

    transfers.need_proj()

    @by_rows
    def _(rows):
        mid = b.xc[rows].astype(F32) + (nn(attended[rows], get(w_proj, 0, width)) + vector(P_BIAS))
        middle[rows] = mid
        normed, _ = norm_parts(mid)
        hb[rows] = (normed * vector(M_GAIN) + vector(M_SHIFT)).astype(BF)
        acc_a[rows] = mid + vector(R_BIAS)
        acc_b[rows] = jnp.zeros_like(mid)
        add_sum(R_BIAS, cot[rows].astype(F32))

    transfers.need_mlp()
    parts = ff // width

    def one_part(part, carried):
        w_in, w_out = get(w_expand, part * width, width), get_rows(w_reduce, part, parts)
        tiles = pieces(total, ROWS // 2)
        todo = []
        for step in range(len(tiles) + 1):
            if step < len(tiles):
                at, n = tiles[step]
                rows = slice(at, at + n)
                todo.append((rows, nn(hb[rows], w_in) + vector(E_BIAS + part), nt(cot[rows], w_out)))
            if step:
                rows, expanded, d_act = todo.pop(0)
                value, slope = gelu_parts(expanded)
                low = value.astype(BF)
                act[rows] = low
                d_low = (d_act * slope).astype(BF)
                d_exp[rows] = d_low
                acc_a[rows] = acc_a[rows] + nn(low, w_out)
                acc_b[rows] = acc_b[rows] + nt(d_low, w_in)
                add_sum(E_BIAS + part, d_low.astype(F32))
        put_rows(w_reduce, tn(act[...], cot[...]).astype(BF), part, parts)
        put(w_expand, tn(hb[...], d_exp[...]).astype(BF), part * width, width)
        transfers.after_part(part)
        return carried

    lax.fori_loop(0, parts, one_part, 0)

    d_att = d_exp

    @by_rows
    def _(rows):
        gradient = acc_b[rows]
        normed, inv = norm_parts(middle[rows])
        d_mid = cot[rows].astype(F32) + norm_back(gradient, normed, inv, vector(M_GAIN))
        add_sum(M_GAIN, gradient * normed)
        add_sum(M_SHIFT, gradient)
        middle[rows] = d_mid
        d_branch = d_mid.astype(BF)
        act[rows] = d_branch
        add_sum(P_BIAS, d_branch.astype(F32))
        d_att[rows] = nt(d_branch, get(w_proj, 0, width)).astype(BF)

    put(w_proj, tn(attended[...], act[...]).astype(BF), 0, width)
    transfers.have_proj()
    unload(acc_a, acc_b, hb)
    transfers.have_result()
    acc_b[...] = jnp.zeros_like(acc_b)
    all_backward(b, transfers)
    weight_of_block(b, 0, transfers)

    @by_rows
    def _(rows):
        gradient = acc_b[rows]
        normed, inv = norm_parts(b.xc[rows].astype(F32))
        add_sum(A_GAIN, gradient * normed)
        add_sum(A_SHIFT, gradient)
        acc_a[rows] = middle[rows] + norm_back(gradient, normed, inv, vector(A_GAIN))

    transfers.have_vectors()
    unload(acc_a, acc_b, act)
    transfers.have_grad()


class Local:
    def __init__(self, b, lengths, ins, outs, sems):
        self.b, self.lengths, self.outs = b, lengths, outs
        targets = (b.x_in, b.cot) + tuple(b[-4:])
        self.loads = [pltpu.make_async_copy(one, target, sems.at[i]) for i, (one, target) in enumerate(zip(ins, targets))]
        sources = (b.hb, b.act) + tuple(b[-4:])
        self.stores = [pltpu.make_async_copy(one, out, sems.at[6 + i]) for i, (one, out) in enumerate(zip(sources, outs))]

    def begin(self):
        for copy in self.loads:
            copy.start()

    def enter(self):
        pass

    def first_length(self):
        return jnp.full((1, 1), self.lengths[lax.axis_index("blk"), 0, 0], jnp.int32).astype(F32)

    def need_tokens(self):
        self.loads[0].wait()

    def need_first(self):
        self.loads[2 + QKV].wait()

    def before_block(self, j):
        pass

    def after_forward(self, i):
        pass

    def need_cotangent(self):
        self.loads[1].wait()

    def need_proj(self):
        self.loads[2 + PROJ].wait()

    def need_mlp(self):
        self.loads[2 + EXPAND].wait()
        self.loads[2 + REDUCE].wait()

    def after_part(self, part):
        pass

    def have_proj(self):
        for which in (PROJ, EXPAND, REDUCE):
            self.stores[2 + which].start()

    def have_result(self):
        self.stores[0].start()

    def after_backward(self, i):
        pass

    def have_qkv(self, j):
        pass

    def have_vectors(self):
        self.stores[2 + QKV].start()

    def have_grad(self):
        self.stores[1].start()
        for copy in self.stores:
            copy.wait()


def local_kernel(lengths, vec, x_in, cot_in, w_qkv, w_proj, w_expand, w_reduce,
                 result, grad_x, g_qkv, g_proj, g_expand, g_reduce, g_vec, *scratch):
    b = Buffers(*scratch[:-1])
    b.vec[...] = vec[...]
    ins = (x_in, cot_in, w_qkv, w_proj, w_expand, w_reduce)
    outs = (result, grad_x, g_qkv, g_proj, g_expand, g_reduce)
    compute(b, Local(b, lengths, ins, outs, scratch[-1]))
    g_vec[...] = b.g_vec[...]


def run_local(lengths, vec, x_in, cot_in, weights):
    vmem, anywhere = pl.BlockSpec(memory_space=pltpu.VMEM), pl.BlockSpec(memory_space=pl.ANY)
    total, width = x_in.shape
    like = (x_in, x_in) + tuple(weights)
    return pl.pallas_call(
        local_kernel,
        out_shape=[jax.ShapeDtypeStruct(one.shape, BF) for one in like]
        + [jax.ShapeDtypeStruct((VEC_ROWS, width), F32)],
        in_specs=[pl.BlockSpec(memory_space=pltpu.SMEM), vmem] + [anywhere] * 6,
        out_specs=[anywhere] * 6 + [vmem],
        scratch_shapes=buffers(total, width, [one.shape for one in weights]) + [pltpu.SemaphoreType.DMA((12,))],
        compiler_params=pltpu.CompilerParams(vmem_limit_bytes=62 * 2**20),
    )(lengths, vec, x_in, cot_in, *weights)


UNITS = (
    (QKV, 0, LANES + TRIO), (QKV, LANES + TRIO, TRIO), (QKV, LANES + 2 * TRIO, TRIO), (QKV, LANES + 3 * TRIO, TRIO),
    (PROJ, 0, 6 * LANES),
    (EXPAND, 0, 8 * LANES), (EXPAND, 8 * LANES, 8 * LANES), (REDUCE, 0, 4 * LANES), (REDUCE, 0, 4 * LANES),
)
HALVES = {7: pl.ds(0, SPREAD[Z] // 2), 8: pl.ds(SPREAD[Z] // 2, SPREAD[Z] // 2)}
EARLY_UNITS, PROJ_UNITS, EXPAND_UNITS, REDUCE_UNITS = (0, 1, 2, 3), (4,), (5, 6), (7, 8)
VECTOR_TILES = ((QKV, 0), (PROJ, 4 * LANES), (PROJ, 5 * LANES))
VECTORS = CHUNKS
CHUNK_COPIES = 6
CHUNKS_BEFORE = (0, CHUNKS + 1, CHUNKS + 2, 2 * CHUNKS + 2)


def schedule():
    entries = {}

    def enter(t, which, stage, chunk):
        entries.setdefault(t, []).append((which, stage, chunk))

    for chunk in range(CHUNKS):
        for stage, later in enumerate((2, 4, 6, 8)):
            enter(chunk + later, EXPAND, stage, chunk)
        for stage, later in enumerate((1, 3, 5)):
            enter(chunk + later, REDUCE, stage, chunk)
    enter(8, REDUCE, None, 0)
    enter(11, REDUCE, 3, 0)
    for stage, t in enumerate((6, 8, 10, 12)):
        enter(t, PROJ, stage, 0)
    for number, times in enumerate(((8, 9, 10, 11), (10, 11, 12, 13), (12, 13, 14, 15), (13, 14, 15, 16))):
        for stage, t in enumerate(times):
            enter(t, QKV, stage, CHUNKS - 1 - number)
    for stage, t in enumerate((15, 16, 17)):
        enter(t, QKV, stage + 1, VECTORS)
    return entries


SCHEDULE = schedule()


class Group:
    def __init__(self, b, ins, outs, scratch):
        self.b = b
        self.tokens, self.cotangent, self.vectors, self.shards = ins
        self.result, self.grad_x, self.outs, self.g_total = outs
        (self.lengths, self.own_lengths, self.own_qkv, self.own_vec, self.packed, self.turn, self.tile, self.arrived,
         self.local_sem, self.token_sem, self.ag_sem, self.rs_sem) = scratch
        self.weights = tuple(b[-4:])
        dp, blk = lax.axis_index("dp"), lax.axis_index("blk")
        z, y, x, c = dp // SPREAD[Y], dp % SPREAD[Y], blk // SPREAD[C], blk % SPREAD[C]
        self.mine = (z, y, x, c)
        self.index = dp * (SPREAD[X] * SPREAD[C]) + blk
        self.blk = blk
        n_blk = SPREAD[X] * SPREAD[C]
        self.others = [(dp, (blk + k) % n_blk) for k in range(1, n_blk)]
        z_places = [(z + k) % SPREAD[Z] for k in range(1, SPREAD[Z])]
        self.along = (
            [((place * SPREAD[Y] + y, blk), place) for place in z_places],
            [((dp + 1 - 2 * y, blk), 1 - y)],
            [((dp, blk + SPREAD[C] * (1 - 2 * x)), 1 - x)],
            [((dp, blk + 1 - 2 * c), 1 - c)],
        )
        height = self.tokens.shape[1]

        def rows(ref):
            return lambda i: ref.at[pl.ds(pl.multiple_of(i * height, height), height)]

        def part(ref):
            return lambda i: ref.at[i]

        moves = (
            (part(self.tokens), rows(b.x_in)),
            (part(self.cotangent), rows(b.cot)),
            (rows(b.hb), part(self.result)),
            (rows(b.act), part(self.grad_x)),
        )
        self.swaps = [
            [
                self.remote(source(device[1]), target(blk), self.token_sem.at[i, k], self.token_sem.at[4 + i, k], device)
                for k, device in enumerate(self.others)
            ]
            for i, (source, target) in enumerate(moves)
        ]
        self.kept = [
            pltpu.make_async_copy(source(blk), target(blk), self.local_sem.at[i])
            for i, (source, target) in enumerate(moves)
        ]

    @staticmethod
    def remote(source, target, send, recv, device):
        return pltpu.make_async_remote_copy(
            src_ref=source, dst_ref=target, send_sem=send, recv_sem=recv,
            device_id=device, device_id_type=pl.DeviceIdType.MESH,
        )

    @staticmethod
    def start(copies):
        for copy in copies:
            copy.start()

    @staticmethod
    def arrive(copies):
        for copy in copies:
            copy.wait_recv()

    @staticmethod
    def sent(copies):
        for copy in copies:
            copy.wait_send()

    def place(self, free, at=None):
        index = [slice(None) if axis in free else self.mine[axis] for axis in range(4)]
        for axis, value in (at or {}).items():
            index[axis] = value
        return tuple(index)


    def gather(self, unit, stage):
        which, first, columns = UNITS[unit]
        w, order = self.weights[which], GATHER_ORDER[which]
        cols = (slice(None), pl.ds(first, columns))

        def one(i, view, device):
            return self.remote(view, view, self.ag_sem.at[0, unit, i], self.ag_sem.at[1, unit, i], device)

        half = {Z: HALVES[unit]} if unit in HALVES else {}
        if stage == 0 and unit in HALVES:
            if unit != min(HALVES):
                return []
            half = {}
        if stage < 3:
            view = w.at[self.place(order[:stage], half) + cols]
            return [one(copies_before(order, stage) + k, view, device) for k, (device, _) in enumerate(self.along[order[stage]])]
        device, _ = self.along[C][0]
        last = order[2]
        if stage == 3:
            return [one(5, w.at[self.place(order[:2], half) + cols], device)]
        (_, other), = self.along[last]
        return [one(6, w.at[self.place(order[:2], {last: other, **half}) + cols], device)]

    def gather_on(self, units, stage):
        for unit in units:
            copies = self.gather(unit, stage)
            self.arrive(copies)
            self.sent(copies)
            if stage < 2:
                self.start(self.gather(unit, stage + 1))
            if stage in (1, 2):
                self.start(self.gather(unit, stage + 2))

    def gathered(self, units):
        for unit in units:
            for stage in (3, 4):
                copies = self.gather(unit, stage)
                self.arrive(copies)
                self.sent(copies)

    def unpack(self, tile):
        which, first = VECTOR_TILES[tile]
        w = self.weights[which]
        all_of = w[:, :, :, :, 0:PACKED, first : first + LANES].astype(F32)
        total = jnp.sum(all_of.reshape(-1, PACKED, LANES), axis=0)
        for i in range(PACKED):
            row, at = divmod(tile * PACKED + i, 4)
            self.b.vec[row : row + 1, at * LANES : (at + 1) * LANES] = total[i : i + 1, :]


    def chunk_view(self, which, chunk):
        if which == REDUCE:
            return chunk, slice(None)
        if which == QKV:
            return None, pl.ds(0, LANES) if chunk == VECTORS else pl.ds(LANES + chunk * TRIO, TRIO)
        return None, pl.ds(chunk * 4 * LANES, 4 * LANES)

    def scatter(self, which, stage, chunk):
        w, order = self.weights[which], SCATTER_ORDER[which]
        axis, rest = order[stage], order[stage + 1 :]
        buffer = self.arrived[which][stage]
        at_z, cols = self.chunk_view(which, chunk)
        first = (CHUNKS_BEFORE[which] + chunk) * CHUNK_COPIES + copies_before(order, stage)
        copies, terms = [], []
        for k, (device, other) in enumerate(self.along[axis]):
            at = {axis: other}
            if at_z is not None and Z in rest:
                at[Z] = at_z
            source = w.at[self.place(rest, at) + (slice(None), cols)]
            lead = (k,) if axis == Z else ()
            free = tuple(at_z if one == Z and at_z is not None else slice(None) for one in sorted(rest))
            target = buffer.at[lead + free + (slice(None), cols)]
            copies.append(self.remote(source, target, self.rs_sem.at[0, first + k], self.rs_sem.at[1, first + k], device))
            terms.append(target)
        return copies, terms

    def scatter_start(self, which, stage, chunk):
        self.start(self.scatter(which, stage, chunk)[0])

    def scatter_on(self, which, stage, chunk):
        w, order = self.weights[which], SCATTER_ORDER[which]
        copies, terms = self.scatter(which, stage, chunk)
        self.arrive(copies)
        rest = order[stage + 1 :]
        at_z, cols = self.chunk_view(which, chunk)
        at = {Z: at_z} if at_z is not None and Z in rest else None
        here = self.place(rest, at) + (slice(None), cols)
        if which == QKV and chunk == VECTORS:
            self.add_vectors(here, terms, rest)
        elif len(terms) == 1 and rest:
            w[here] = w[here] + terms[0][...]
        else:
            total = w[here].astype(F32)
            for term in terms:
                total = total + term[...].astype(F32)
            if rest:
                w[here] = total.astype(BF)
            else:
                self.keep(which, chunk, total)
        if rest and not (which == REDUCE and rest == (Z,)):
            self.scatter_start(which, stage + 1, chunk)
        self.sent(copies)

    def add_vectors(self, here, terms, rest):
        w = self.weights[QKV]
        total = w[here].astype(F32)
        for term in terms:
            total = total + term[...].astype(F32)
        half = PACKED // 2
        exact = total[..., :half, :] + total[..., half:, :]
        if rest:
            high = exact.astype(BF).astype(F32)
            w[here] = jnp.concatenate([high, exact - high], axis=-2).astype(BF)
        else:
            self.g_total[...] = exact

    def keep(self, which, chunk, total):
        out = self.outs[which]
        if which == QKV:
            width = out.shape[1] // 3
            for i in range(3):
                out[:, i * width + chunk * LANES : i * width + (chunk + 1) * LANES] = total[:, i * LANES : (i + 1) * LANES]
        else:
            out[:, self.chunk_view(which, chunk)[1]] = total

    def tick(self, t):
        for which, stage, chunk in SCHEDULE.get(t, ()):
            if stage is None:
                self.scatter_start(which, 3, chunk)
            else:
                self.scatter_on(which, stage, chunk)


    def spread_vectors(self):
        g_vec, lines, tile = self.b.g_vec, self.packed, self.tile
        parts = g_vec.shape[1] // LANES
        for i in range(lines.shape[0]):
            lines[i : i + 1, :] = g_vec[i // parts : i // parts + 1, i % parts * LANES : (i % parts + 1) * LANES]
        tile[...] = jnp.zeros_like(tile)
        devices = math.prod(SPREAD)
        for device in range(0, devices, SPREAD[C]):
            row = 0
            for i, one in enumerate(self.own_vec):
                size = one.shape[0]
                if device * size % LANES == 0:
                    at = row + device * size // LANES
                    tile[i : i + 1, :] = lines[at : at + 1, :]
                row += devices * size // LANES
            high = tile[...].astype(BF).astype(F32)
            value = jnp.concatenate([high, tile[...] - high], axis=0).astype(BF)
            pair = device // SPREAD[C]
            place = (pair // (SPREAD[X] * SPREAD[Y]), pair // SPREAD[X] % SPREAD[Y], pair % SPREAD[X])
            for core in range(SPREAD[C]):
                self.weights[QKV][place + (core, slice(None), pl.ds(0, LANES))] = value


    def begin(self):
        self.peers = self.others + [device for axis in (Y, Z) for device, _ in self.along[axis]]
        for device in self.peers:
            pl.semaphore_signal(
                pltpu.get_barrier_semaphore(), inc=1, device_id=device, device_id_type=pl.DeviceIdType.MESH
            )
        count = len(self.vectors)
        loads = [
            pltpu.make_async_copy(one, target, self.local_sem.at[4 + i])
            for i, (one, target) in enumerate(zip(self.vectors, self.own_vec))
        ]
        loads.append(pltpu.make_async_copy(self.shards[QKV], self.own_qkv, self.local_sem.at[8 + count]))
        width = self.shards[PROJ].shape[1]
        slots = [self.weights[which].at[self.mine] for which in range(4)]
        self.own = [
            pltpu.make_async_copy(
                self.shards[which], slots[which].at[:, pl.ds(0, self.shards[which].shape[1])],
                self.local_sem.at[4 + count + which],
            )
            for which in (PROJ, EXPAND, REDUCE)
        ]
        loads.append(pltpu.make_async_copy(self.lengths, self.own_lengths, self.local_sem.at[4 + count + QKV]))
        loads[-2], loads[-1] = loads[-1], loads[-2]
        self.start(loads + self.own + self.kept[:2])
        self.packed[...] = jnp.zeros_like(self.packed)
        row = 0
        for load, own in zip(loads, self.own_vec):
            load.wait()
            size = own.shape[0]
            self.turn[...] = jnp.zeros_like(self.turn)
            self.turn[0:1, 0:size] = own[...].astype(F32).reshape(1, size)
            at = self.index * size
            self.packed[pl.ds(row + at // LANES, 1), :] = pltpu.roll(self.turn[...], at % LANES, 1)[0:1, :]
            row += math.prod(SPREAD) * size // LANES
        for load in loads[count:]:
            load.wait()
        w = self.weights[QKV]
        for j in range(width // LANES):
            for i in range(3):
                to = LANES + j * TRIO + i * LANES
                w[self.mine + (slice(None), pl.ds(to, LANES))] = self.own_qkv[:, i * width + j * LANES : i * width + (j + 1) * LANES]
        for tile, (which, first) in enumerate(VECTOR_TILES):
            values = self.packed[tile * PACKED : (tile + 1) * PACKED, :].astype(BF)
            self.weights[which][self.mine + (slice(None), pl.ds(first, LANES))] = values

    def enter(self):
        pl.semaphore_wait(pltpu.get_barrier_semaphore(), len(self.peers))
        for unit in EARLY_UNITS:
            self.start(self.gather(unit, 0))
        self.start(self.swaps[0])
        for copy in self.own:
            copy.wait()
        for unit in PROJ_UNITS + EXPAND_UNITS:
            self.start(self.gather(unit, 0))

    def first_length(self):
        first = self.own_lengths[0][0:1, :].astype(F32)
        lane = lax.broadcasted_iota(jnp.int32, first.shape, 1)
        return jnp.sum(jnp.where(lane == self.blk, first, 0.0), axis=1, keepdims=True)

    def need_tokens(self):
        self.gather_on(EARLY_UNITS, 0)
        self.gather_on(EARLY_UNITS[:2], 1)
        self.gather_on(EARLY_UNITS[:1], 2)
        self.gather_on(EARLY_UNITS[2:3], 1)
        self.gather_on(EARLY_UNITS[1:2], 2)
        self.gather_on(EARLY_UNITS[3:], 1)
        self.start(self.gather(REDUCE_UNITS[0], 0))
        self.gathered(EARLY_UNITS[:1])
        self.unpack(0)
        self.kept[0].wait()
        self.arrive(self.swaps[0])
        self.sent(self.swaps[0])
        self.start(self.swaps[1])

    def need_first(self):
        self.gather_on(PROJ_UNITS + EXPAND_UNITS, 0)
        self.gather_on(EARLY_UNITS[2:3], 2)

    def before_block(self, j):
        for unit in EARLY_UNITS[1:]:
            pl.when(j == unit)(lambda unit=unit: self.gathered((unit,)))

    def after_forward(self, i):
        steps = (
            lambda: (self.gather_on(EARLY_UNITS[3:], 2), self.gather_on(REDUCE_UNITS, 0)),
            lambda: None,
            lambda: self.gather_on(PROJ_UNITS, 1),
            lambda: (self.gather_on(REDUCE_UNITS, 1), self.gather_on(EXPAND_UNITS[:1], 1)),
            lambda: self.gather_on(PROJ_UNITS, 2),
            lambda: self.gather_on(EXPAND_UNITS[1:], 1),
            lambda: self.gather_on(EXPAND_UNITS[:1], 2),
            lambda: self.gather_on(REDUCE_UNITS[:1], 2),
        )
        for at, step in enumerate(steps):
            pl.when(i == at)(lambda step=step: [step(), None][1])

    def need_cotangent(self):
        self.kept[1].wait()
        self.arrive(self.swaps[1])
        self.sent(self.swaps[1])

    def need_proj(self):
        self.gathered(PROJ_UNITS)
        self.unpack(1)
        self.unpack(2)

    def need_mlp(self):
        self.gathered(EXPAND_UNITS[:1] + REDUCE_UNITS[:1])

    def after_part(self, part):
        for at in range(CHUNKS):
            @pl.when(part == at)
            def _(at=at):
                self.scatter_start(REDUCE, 0, at)
                self.scatter_start(EXPAND, 0, at)
                if at == 0:
                    self.gather_on(EXPAND_UNITS[1:] + REDUCE_UNITS[1:], 2)
                if at == 1:
                    self.gathered(EXPAND_UNITS[1:] + REDUCE_UNITS[1:])
                self.tick(at)

    def have_proj(self):
        self.scatter_start(PROJ, 0, 0)
        self.tick(CHUNKS)

    def have_result(self):
        self.start(self.swaps[2] + self.kept[2:3])

    def after_backward(self, i):
        for at in range(2 * CHUNKS):
            pl.when(i == at)(lambda at=at: self.tick(CHUNKS + 1 + at))

    def have_qkv(self, j):
        if isinstance(j, int):
            self.scatter_start(QKV, 0, j)
            return
        for at in range(1, CHUNKS):
            pl.when(j == at)(lambda at=at: self.scatter_start(QKV, 0, at))

    def have_vectors(self):
        self.tick(3 * CHUNKS + 1)
        self.spread_vectors()
        self.scatter_start(QKV, 0, VECTORS)

    def have_grad(self):
        self.scatter_on(QKV, 0, VECTORS)
        self.start(self.swaps[3] + self.kept[3:4])
        for t in range(3 * CHUNKS + 2, max(SCHEDULE) + 1):
            self.tick(t)
        for i in (2, 3):
            self.kept[i].wait()
            self.arrive(self.swaps[i])
            self.sent(self.swaps[i])


N_VECTORS = 8


def group_kernel(*refs):
    refs = list(refs)

    def take(n):
        taken = refs[:n]
        del refs[:n]
        return taken

    (lengths,), vectors, (tokens, cotangent), shards = take(1), take(N_VECTORS), take(2), take(4)
    (result, grad_x), outs, (g_total,) = take(2), take(4), take(1)
    b = Buffers(*take(len(Buffers._fields)))
    (own_lengths, own_qkv), own_vec, (packed, turn, tile) = take(2), take(N_VECTORS), take(3)
    arrived = [take(4) for _ in range(4)]
    scratch = [lengths, own_lengths, own_qkv, own_vec, packed, turn, tile, arrived] + refs
    group = Group(b, (tokens, cotangent, vectors, shards), (result, grad_x, outs, g_total), scratch)
    compute(b, group)


def run_group(lengths, vectors, tokens, cotangent, weights):
    vmem, anywhere = pl.BlockSpec(memory_space=pltpu.VMEM), pl.BlockSpec(memory_space=pl.ANY)
    blk, height, width = tokens.shape
    extra = [0] * 4
    for which, _ in VECTOR_TILES:
        extra[which] += LANES
    shapes = [SPREAD + (one.shape[0], one.shape[1] + more) for one, more in zip(weights, extra)]
    landing = []
    for which, shape in enumerate(shapes):
        for stage, axis in enumerate(SCATTER_ORDER[which]):
            rest = sorted(SCATTER_ORDER[which][stage + 1 :])
            lead = (SPREAD[Z] - 1,) if axis == Z else ()
            landing.append(pltpu.VMEM(lead + tuple(SPREAD[one] for one in rest) + shape[4:], BF))
    packed_rows = math.prod(SPREAD) * sum(one.shape[0] for one in vectors) // LANES
    dma = pltpu.SemaphoreType.DMA
    return pl.pallas_call(
        group_kernel,
        out_shape=[jax.ShapeDtypeStruct(tokens.shape, BF)] * 2
        + [jax.ShapeDtypeStruct(one.shape, F32) for one in weights]
        + [jax.ShapeDtypeStruct((N_VECTORS, LANES), F32)],
        in_specs=[anywhere] * (N_VECTORS + 7),
        out_specs=[anywhere] * 2 + [vmem] * 5,
        scratch_shapes=buffers(blk * height, width, shapes)
        + [pltpu.VMEM(lengths.shape, lengths.dtype), pltpu.VMEM(weights[QKV].shape, BF)]
        + [pltpu.VMEM(one.shape, BF) for one in vectors]
        + [pltpu.VMEM((packed_rows, LANES), F32), pltpu.VMEM((8, LANES), F32), pltpu.VMEM((N_VECTORS, LANES), F32)]
        + landing
        + [dma((17,)), dma((8, 3)), dma((2, len(UNITS), 7)), dma((2, (CHUNKS_BEFORE[-1] + CHUNKS) * CHUNK_COPIES))],
        compiler_params=pltpu.CompilerParams(
            vmem_limit_bytes=62 * 2**20, collective_id=0, has_side_effects=True
        ),
    )(lengths, *vectors, tokens, cotangent, *weights)


def finish_kernel(result, grad_x, g_qkv, g_proj, g_expand, g_reduce, g_vec, *refs):
    sources = (result, grad_x, g_qkv, g_proj, g_expand, g_reduce)
    outs, refs = refs[: 6 + N_VECTORS], refs[6 + N_VECTORS :]
    held, short = refs[:6], refs[6 : 6 + N_VECTORS]
    turn, sems = refs[6 + N_VECTORS :]
    loads, stores = [], []
    for source, to, out in zip(sources, held, outs):
        places = range(source.shape[0]) if len(source.shape) == 3 else (slice(None),)
        for place in places:
            sem = len(loads)
            loads.append(pltpu.make_async_copy(source.at[place], to.at[place], sems.at[0, sem]))
            stores.append(pltpu.make_async_copy(to.at[place], out.at[place], sems.at[1, sem]))
    for load in loads:
        load.start()
    handed = []
    index = lax.axis_index("dp") * lax.axis_size("blk") + lax.axis_index("blk")
    for i, one in enumerate(short):
        size = one.shape[0]
        at = index * size
        turn[0:1, :] = g_vec[i : i + 1, :]
        turned = pltpu.roll(turn[...], (LANES - at % LANES) % LANES, 1)
        one[...] = turned[0:1, 0:size].reshape(size)
        handed.append(pltpu.make_async_copy(one, outs[6 + i], sems.at[0, len(loads) + i]))
        handed[-1].start()
    for load, store in zip(loads, stores):
        load.wait()
        store.start()
    for store in stores + handed:
        store.wait()


def finish(values, sizes):
    vmem, anywhere = pl.BlockSpec(memory_space=pltpu.VMEM), pl.BlockSpec(memory_space=pl.ANY)
    long = [(one.shape, one.dtype) for one in values[:6]]
    short = [((size,), F32) for size in sizes]
    return pl.pallas_call(
        finish_kernel,
        out_shape=[jax.ShapeDtypeStruct(*one) for one in long + short],
        in_specs=[anywhere] * 6 + [vmem],
        out_specs=[anywhere] * (6 + len(sizes)),
        scratch_shapes=[pltpu.VMEM(*one) for one in long + short]
        + [pltpu.VMEM((8, LANES), F32)]
        + [pltpu.SemaphoreType.DMA((2, 4 + 2 * values[0].shape[0] + len(sizes)))],
    )(*values)


def by_collectives(lengths, vectors, sizes, tokens, cotangent, weights):
    axes = ("dp", "blk")
    width = tokens.shape[2]
    blocks = width // LANES

    def exchange(rows):
        return lax.all_to_all(rows.reshape(tokens.shape), "blk", 0, 0, tiled=True)

    packed = lax.all_gather(jnp.concatenate(vectors), axes, axis=0)
    starts = [sum(sizes[:i]) for i in range(len(sizes))]
    full = [packed[:, at : at + size].reshape(-1, width) for at, size in zip(starts, sizes)]
    vec = jnp.concatenate(full, axis=0).astype(F32)
    vec = jnp.pad(vec, ((0, VEC_ROWS - vec.shape[0]), (0, 0)))
    whole = [lax.all_gather(one, axes, axis=0, tiled=True) for one in weights]
    whole[QKV] = whole[QKV].reshape(width, 3, blocks, LANES).swapaxes(1, 2).reshape(width, 3 * width)
    result, grad_x, *grads, g_vec = run_local(
        lengths, vec, exchange(tokens).reshape(-1, width), exchange(cotangent).reshape(-1, width), whole
    )
    grads[QKV] = grads[QKV].reshape(width, blocks, 3, LANES).swapaxes(1, 2).reshape(width, 3 * width)
    grads = [lax.psum_scatter(one.astype(F32), axes, scatter_dimension=0, tiled=True) for one in grads]
    g_vec = lax.psum(g_vec, axes).reshape(-1)
    index = lax.axis_index(axes)
    devices = lax.axis_size(axes)
    own = [
        lax.dynamic_slice(g_vec, (devices * at + index * size,), (size,)) for at, size in zip(starts, sizes)
    ]
    return (exchange(result), exchange(grad_x), *grads, *own)


def body(
    tokens, lengths, attn_gain, attn_shift, w_qkv, qv_bias, w_proj, proj_bias,
    mlp_gain, mlp_shift, w_expand, expand_bias, w_reduce, reduce_bias, cotangent,
):
    vectors = (attn_gain, attn_shift, qv_bias, proj_bias, mlp_gain, mlp_shift, reduce_bias, expand_bias)
    sizes = [one.shape[0] for one in vectors]
    weights = (w_qkv, w_proj, w_expand, w_reduce)
    sized = (lax.axis_size("dp"), lax.axis_size("blk")) == (SPREAD[Z] * SPREAD[Y], SPREAD[X] * SPREAD[C])
    if sized and all(one.shape[0] % 16 == 0 for one in weights):
        outs = finish(run_group(jnp.transpose(lengths, (1, 2, 0)), vectors, tokens, cotangent, weights), sizes)
    else:
        outs = by_collectives(lengths, vectors, sizes, tokens, cotangent, weights)
    result, grad_x, g_qkv, g_proj, g_expand, g_reduce, ag, as_, qv, pb, mg, ms, rb, eb = outs
    return (result, grad_x, ag, as_, g_qkv, qv, g_proj, pb, mg, ms, g_expand, eb, g_reduce, rb)


def solution(mesh):
    both = ("dp", "blk")
    rows = P(None, both, None)
    vector, matrix = P(both), P(both, None)
    weights = (
        vector, vector, matrix, vector, matrix, vector, vector, vector, matrix, vector, matrix, vector,
    )
    return jax.shard_map(
        body,
        mesh=mesh,
        in_specs=(rows, P(None, "dp", None)) + weights + (rows,),
        out_specs=(rows, rows) + weights,
        check_vma=False,
    )
```

```python
import math
import typing

import jax
import jax.numpy as jnp
from jax import lax
from jax.experimental import pallas as pl
from jax.experimental.pallas import tpu as pltpu
from jax.sharding import PartitionSpec as P

HEAD_DIM = 32
LONG_IMG = 784
SHORT_IMG = 196
LANES = 128
HEADS_IN_BLOCK = LANES // HEAD_DIM
LONG_KEYS = 896
BF = jnp.bfloat16
F32 = jnp.float32
epsilon = 1e-06
LOG2E = math.log2(math.e)
SCALE = 1.0 / math.sqrt(HEAD_DIM)
MASKED = -1e30
ROWS = 512
A_GAIN, A_SHIFT, Q_BIAS, V_BIAS, P_BIAS, M_GAIN, M_SHIFT, R_BIAS, E_BIAS = range(9)
VEC_ROWS = 16
PACKED = 16
TRIO = 3 * LANES
CHUNKS = 4
Z, Y, X, C = range(4)
SPREAD = (4, 2, 2, 2)
QKV, PROJ, EXPAND, REDUCE = range(4)
GATHER_ORDER = ((X, Z, Y), (X, Z, Y), (X, Z, Y), (Z, Y, X))
SCATTER_ORDER = ((C, X, Y, Z), (C, Y, Z, X), (C, Y, Z, X), (C, X, Y, Z))


def copies_before(order, stage):
    return sum(SPREAD[axis] - 1 for axis in order[:stage])


def nt(left, right):
    return lax.dot_general(left, right, (((1,), (1,)), ((), ())), preferred_element_type=F32)


def nn(left, right):
    return lax.dot_general(left, right, (((1,), (0,)), ((), ())), preferred_element_type=F32)


def tn(left, right):
    return lax.dot_general(left, right, (((0,), (0,)), ((), ())), preferred_element_type=F32)


def pieces(total, size):
    return [(at, min(size, total - at)) for at in range(0, total, size)]


def lanes(rows, width=LANES):
    return lax.broadcasted_iota(jnp.int32, (rows, width), 1)


def to_canonical(swapped, natural, moved):
    total = natural.shape[0]
    tail = LONG_IMG + SHORT_IMG
    moved[0:LONG_IMG] = natural[SHORT_IMG:tail]
    moved[LONG_IMG:tail] = natural[0:SHORT_IMG]
    moved[tail:total] = natural[tail:total]


def to_natural(ordered, moved):
    total = ordered.shape[0]
    tail = LONG_IMG + SHORT_IMG
    moved[SHORT_IMG:tail] = ordered[0:LONG_IMG]
    moved[0:SHORT_IMG] = ordered[LONG_IMG:tail]
    moved[tail:total] = ordered[tail:total]


def norm_parts(values):
    centered = values - jnp.mean(values, axis=-1, keepdims=True)
    inverse = lax.rsqrt(jnp.mean(centered * centered, axis=-1, keepdims=True) + epsilon)
    return centered * inverse, inverse


def norm_back(gradient, normed, inverse, gain):
    scaled = gradient * gain
    return inverse * (
        scaled
        - jnp.mean(scaled, axis=-1, keepdims=True)
        - normed * jnp.mean(scaled * normed, axis=-1, keepdims=True)
    )


def gelu_parts(values):
    phi = 0.5 + 0.5 * lax.erf(values * math.sqrt(0.5))
    bell = jnp.exp2(values * values * (-0.5 * LOG2E) + math.log2(1.0 / math.sqrt(2.0 * math.pi)))
    return values * phi, phi + values * bell


def fill_masks(aug_q, aug_k):
    total = aug_q.shape[0]
    row = lax.broadcasted_iota(jnp.int32, (total, LANES), 0)
    segment = (row >= LONG_IMG).astype(jnp.int32) + (row >= LONG_IMG + SHORT_IMG).astype(jnp.int32)
    place = lanes(total) % HEAD_DIM
    aug_q[...] = jnp.where(place == segment, 1.0, 0.0).astype(BF)
    aug_k[...] = jnp.where((place < 3) & (place != segment), MASKED, 0.0).astype(BF)


def attend_tiles(total, size):
    tail = total - LONG_IMG
    first = total - 2 * LANES
    return [(at, n, 0, LONG_KEYS, True, at) for at, n in pieces(LONG_IMG, size)] + [
        (LONG_IMG + at, n, first, 2 * LANES, False, at) for at, n in pieces(tail, size)
    ]


def get(ref, at, n):
    cols = pl.ds(at if isinstance(at, int) else pl.multiple_of(at, LANES), n)
    value = ref[:, cols] if len(ref.shape) == 2 else ref[:, :, :, :, :, cols]
    return value.reshape(-1, n)


def put(ref, value, at, n):
    cols = pl.ds(at if isinstance(at, int) else pl.multiple_of(at, LANES), n)
    if len(ref.shape) == 2:
        ref[:, cols] = value
    else:
        ref[:, :, :, :, :, cols] = value.reshape(ref.shape[:-1] + (n,))


def get_rows(ref, part, parts):
    if len(ref.shape) == 2:
        rows = ref.shape[0] // parts
        return ref[pl.ds(pl.multiple_of(part * rows, rows), rows)]
    each = ref.shape[0] // parts
    value = ref[pl.ds(part * each, each)]
    return value.reshape(-1, value.shape[-1])


def put_rows(ref, value, part, parts):
    if len(ref.shape) == 2:
        rows = ref.shape[0] // parts
        ref[pl.ds(pl.multiple_of(part * rows, rows), rows)] = value
    else:
        each = ref.shape[0] // parts
        ref[pl.ds(part * each, each)] = value.reshape((each,) + ref.shape[1:])


def of_block(ref, j, offset=0):
    return ref.at[:, pl.ds(pl.multiple_of(offset + j * LANES, LANES), LANES)]


def of_trio(ref, j, which):
    return ref.at[:, pl.ds(pl.multiple_of(j * TRIO + which * LANES, LANES), LANES)]


def forward_head(j, head, qkv, attended, inverse, e_long, e_tail, aug_q, aug_k, size=400):
    total, width = attended.shape
    q, k, v = (of_trio(qkv, j, i) for i in range(3))
    attended, inverse = of_block(attended, j), of_block(inverse, j)
    mine = lanes(1) // HEAD_DIM == head
    ka = jnp.where(mine, k[...], aug_k[...])
    va = jnp.where(mine, v[...], jnp.ones_like(aug_k[...]))
    at = j * HEADS_IN_BLOCK + head
    for row, rows, key, keys, is_long, place in attend_tiles(total, size):
        here = pl.ds(row, rows)
        scores = nt(jnp.where(mine, q[here], aug_q[here]), ka[key : key + keys])
        exps = jnp.exp2(scores - jnp.max(scores, axis=1, keepdims=True)).astype(BF)
        store = e_long if is_long else e_tail
        store[at, place : place + rows, :] = exps
        product = nn(exps, va[key : key + keys])
        inv = 1.0 / pltpu.roll(product, HEAD_DIM, 1)
        attended[here] = jnp.where(mine, (product * inv).astype(BF), attended[here])
        inverse[here] = jnp.where(mine, inv, inverse[here])


def backward_prepare(j, qkv, attended, inverse, d_att, scaled_b, aug_b, q_t, s_t, k_b):
    total, width = attended.shape
    for at, n in pieces(total, ROWS):
        here = pl.ds(at, n)
        scaled = of_block(d_att, j)[here].astype(F32) * of_block(inverse, j)[here]
        inner = scaled * of_block(attended, j)[here].astype(F32)
        from_group = lax.broadcasted_iota(jnp.int32, (LANES, LANES), 0) // HEAD_DIM
        to_group = lanes(LANES) // HEAD_DIM
        spread = jnp.where((from_group + 1) % HEADS_IN_BLOCK == to_group, 1.0, 0.0).astype(BF)
        high = inner.astype(BF)
        low = (inner - high.astype(F32)).astype(BF)
        sums = nn(high, spread) + nn(low, spread)
        sum_high = sums.astype(BF)
        sum_low = (sums - sum_high.astype(F32)).astype(BF)
        place = lanes(n) % HEAD_DIM
        zeros = jnp.zeros_like(sum_high)
        aug_b[here] = jnp.where(place == 0, -sum_high, jnp.where(place == 1, -sum_low, zeros))
        scaled = scaled.astype(BF)
        scaled_b[here] = scaled
        s_t[:, at : at + n] = scaled.T
        q_t[:, at : at + n] = of_trio(qkv, j, 0)[here].T
        k_b[here] = of_trio(qkv, j, 1)[here]


def backward_head(j, head, qkv, e_long, e_tail, scaled_b, aug_b, q_t, s_t, k_b, dk_t, dv_t, size=400):
    total = scaled_b.shape[0]
    dq, v = of_trio(qkv, j, 0), of_trio(qkv, j, 2)
    mine = lanes(1) // HEAD_DIM == head
    following = lanes(1) // HEAD_DIM == (head + 1) % HEADS_IN_BLOCK
    va = jnp.where(mine, v[...], jnp.ones_like(k_b[...]))
    at = j * HEADS_IN_BLOCK + head
    of_head = pl.ds(pl.multiple_of(head * HEAD_DIM, HEAD_DIM), HEAD_DIM)
    sums_of = {}
    for row, rows, key, keys, is_long, where in attend_tiles(total, size):
        here = pl.ds(row, rows)
        store = e_long if is_long else e_tail
        exps = store[at, where : where + rows, :]
        side = jnp.where(following, aug_b[here], jnp.zeros_like(aug_b[here]))
        left = jnp.where(mine, scaled_b[here], side)
        d_scores = (exps.astype(F32) * nt(left, va[key : key + keys])).astype(BF)
        dq_here = (nn(d_scores, k_b[key : key + keys]) * SCALE).astype(BF)
        dq[here] = jnp.where(mine, dq_here, dq[here])
        more_v = nn(s_t[of_head, row : row + rows], exps)
        more_k = nn(q_t[of_head, row : row + rows], d_scores)
        if is_long in sums_of:
            more_v, more_k = sums_of[is_long][0] + more_v, sums_of[is_long][1] + more_k
        sums_of[is_long] = (more_v, more_k)
    first = total - 2 * LANES
    both = LONG_KEYS - first
    for ref, which, factor in ((dv_t, 0, 1.0), (dk_t, 1, 1.0 / LOG2E)):
        long_part, tail_part = (sums_of[is_long][which] * factor for is_long in (True, False))
        ref[of_head, 0:first] = long_part[:, :first].astype(BF)
        ref[of_head, first:LONG_KEYS] = (long_part[:, first:] + tail_part[:, :both]).astype(BF)
        ref[of_head, LONG_KEYS:total] = tail_part[:, both:].astype(BF)


def trio_columns(ref, j, width):
    return ref.shape[-1] - 3 * width + j * TRIO


def all_forward(b, transfers):
    total, width = b.attended.shape
    unrolled = 2

    def block(j, carried):
        transfers.before_block(j)
        here = pl.ds(pl.multiple_of(j * LANES, LANES), LANES)
        w_trio = get(b.w_qkv, trio_columns(b.w_qkv, j, width), TRIO)
        for at, n in pieces(total, ROWS):
            projected = nn(b.x_in[at : at + n], w_trio)
            q, k, v = (projected[:, i * LANES : (i + 1) * LANES] for i in range(3))
            q = (q + b.vec[Q_BIAS : Q_BIAS + 1, here]) * (SCALE * LOG2E)
            v = v + b.vec[V_BIAS : V_BIAS + 1, here]
            for i, value in enumerate((q, k, v)):
                of_trio(b.qkv, j, i)[at : at + n] = value.astype(BF)

        def step(i, inside):
            for one in range(unrolled):
                forward_head(
                    j, i * unrolled + one, b.qkv, b.attended, b.inverse,
                    b.e_long, b.e_tail, b.aug_q, b.aug_k,
                )
            transfers.after_forward(j * (HEADS_IN_BLOCK // unrolled) + i)
            return inside

        lax.fori_loop(0, HEADS_IN_BLOCK // unrolled, step, 0)
        return carried

    lax.fori_loop(0, width // LANES, block, 0)


def weight_of_block(b, j, transfers):
    trio = pl.ds(pl.multiple_of(j * TRIO, LANES), TRIO)
    at = trio_columns(b.w_qkv, j, b.attended.shape[1])
    put(b.w_qkv, nn(b.ha_t[...], b.qkv[:, trio]).astype(BF), at, TRIO)
    transfers.have_qkv(j)


def all_backward(b, transfers):
    total, width = b.attended.shape
    unrolled = 2
    keep = (b.scaled_b, b.aug_b, b.q_t, b.s_t, b.k_b)

    blocks = width // LANES

    def block(number, carried):
        j = blocks - 1 - number
        pl.when(number > 0)(lambda: weight_of_block(b, j + 1, transfers))
        backward_prepare(j, b.qkv, b.attended, b.inverse, b.d_exp, *keep)

        def step(i, inside):
            for one in range(unrolled):
                backward_head(
                    j, i * unrolled + one, b.qkv, b.e_long, b.e_tail, *keep, b.dk_t, b.dv_t
                )
            transfers.after_backward(number * (HEADS_IN_BLOCK // unrolled) + i)
            return inside

        lax.fori_loop(0, HEADS_IN_BLOCK // unrolled, step, 0)
        of_trio(b.qkv, j, 1)[...] = b.dk_t[...].T
        of_trio(b.qkv, j, 2)[...] = b.dv_t[...].T
        here = pl.ds(pl.multiple_of(j * LANES, LANES), LANES)
        trio = pl.ds(pl.multiple_of(j * TRIO, LANES), TRIO)
        for row, which in ((Q_BIAS, 0), (V_BIAS, 2)):
            values = of_trio(b.qkv, j, which)[...].astype(F32)
            b.g_vec[row : row + 1, here] = jnp.sum(values, axis=0, keepdims=True)
        w_trio = get(b.w_qkv, trio_columns(b.w_qkv, j, width), TRIO)
        for at, n in pieces(total, ROWS):
            b.acc_b[at : at + n] = b.acc_b[at : at + n] + nt(b.qkv[at : at + n, trio], w_trio)
        return carried

    lax.fori_loop(0, blocks, block, 0)


class Buffers(typing.NamedTuple):
    x_in: typing.Any
    ha_t: typing.Any
    cot: typing.Any
    xc: typing.Any
    qkv: typing.Any
    attended: typing.Any
    inverse: typing.Any
    e_long: typing.Any
    e_tail: typing.Any
    aug_q: typing.Any
    aug_k: typing.Any
    middle: typing.Any
    acc_a: typing.Any
    acc_b: typing.Any
    hb: typing.Any
    act: typing.Any
    d_exp: typing.Any
    scaled_b: typing.Any
    aug_b: typing.Any
    q_t: typing.Any
    s_t: typing.Any
    k_b: typing.Any
    dk_t: typing.Any
    dv_t: typing.Any
    vec: typing.Any
    g_vec: typing.Any
    w_qkv: typing.Any
    w_proj: typing.Any
    w_expand: typing.Any
    w_reduce: typing.Any


def buffers(total, width, weights):
    heads = width // HEAD_DIM
    rows, lane, turned = (total, width), (total, LANES), (LANES, total)
    shapes = Buffers(
        x_in=(rows, BF),
        ha_t=((width, total), BF),
        cot=(rows, BF),
        xc=(rows, BF),
        qkv=((total, 3 * width), BF),
        attended=(rows, BF),
        inverse=(rows, F32),
        e_long=((heads, LONG_IMG, LONG_KEYS), BF),
        e_tail=((heads, total - LONG_IMG, 2 * LANES), BF),
        aug_q=(lane, BF),
        aug_k=(lane, BF),
        middle=(rows, F32),
        acc_a=(rows, F32),
        acc_b=(rows, F32),
        hb=(rows, BF),
        act=(rows, BF),
        d_exp=(rows, BF),
        scaled_b=(lane, BF),
        aug_b=(lane, BF),
        q_t=(turned, BF),
        s_t=(turned, BF),
        k_b=(lane, BF),
        dk_t=(turned, BF),
        dv_t=(turned, BF),
        vec=((VEC_ROWS, width), F32),
        g_vec=((VEC_ROWS, width), F32),
        w_qkv=(weights[QKV], BF),
        w_proj=(weights[PROJ], BF),
        w_expand=(weights[EXPAND], BF),
        w_reduce=(weights[REDUCE], BF),
    )
    return [pltpu.VMEM(*one) for one in shapes]


def compute(b, transfers):
    total, width = b.xc.shape
    ff = b.w_expand.shape[-1]
    acc_a, acc_b, vec, g_vec = b.acc_a, b.acc_b, b.vec, b.g_vec

    def by_rows(function):
        def step(i, carried):
            function(pl.ds(pl.multiple_of(i * ROWS, ROWS), ROWS))
            return carried

        lax.fori_loop(0, total // ROWS, step, 0)

    def vector(row):
        return vec[pl.ds(row, 1), :]

    def add_sum(row, values):
        g_vec[pl.ds(row, 1), :] = g_vec[pl.ds(row, 1), :] + jnp.sum(values, axis=0, keepdims=True)

    def load(source):
        @by_rows
        def _(rows):
            acc_a[rows] = source[rows].astype(F32)

        to_canonical(swapped, acc_a, acc_b)

    def loaded(rows):
        return jnp.where(swapped, acc_b[rows], acc_a[rows])

    def unload(values, moved, target):
        to_natural(values, moved)

        @by_rows
        def _(rows):
            target[rows] = jnp.where(swapped, moved[rows], values[rows]).astype(BF)

    transfers.begin()
    g_vec[...] = jnp.zeros_like(g_vec)
    fill_masks(b.aug_q, b.aug_k)
    transfers.enter()
    transfers.need_tokens()
    swapped = jnp.broadcast_to(transfers.first_length(), (1, width)) == SHORT_IMG
    load(b.x_in)

    @by_rows
    def _(rows):
        values = loaded(rows)
        b.xc[rows] = values.astype(BF)
        normed, _ = norm_parts(values)
        b.x_in[rows] = (normed * vector(A_GAIN) + vector(A_SHIFT)).astype(BF)

    transfers.need_first()
    for at, n in pieces(total, ROWS):
        b.ha_t[:, at : at + n] = b.x_in[at : at + n].T

    all_forward(b, transfers)

    transfers.need_cotangent()
    cot, middle, hb, act, d_exp, attended = b.cot, b.middle, b.hb, b.act, b.d_exp, b.attended
    w_proj, w_expand, w_reduce = b.w_proj, b.w_expand, b.w_reduce
    load(cot)

    @by_rows
    def _(rows):
        cot[rows] = loaded(rows).astype(BF)

    transfers.need_proj()

    @by_rows
    def _(rows):
        mid = b.xc[rows].astype(F32) + (nn(attended[rows], get(w_proj, 0, width)) + vector(P_BIAS))
        middle[rows] = mid
        normed, _ = norm_parts(mid)
        hb[rows] = (normed * vector(M_GAIN) + vector(M_SHIFT)).astype(BF)
        acc_a[rows] = mid + vector(R_BIAS)
        acc_b[rows] = jnp.zeros_like(mid)
        add_sum(R_BIAS, cot[rows].astype(F32))

    transfers.need_mlp()
    parts = ff // width

    def one_part(part, carried):
        w_in, w_out = get(w_expand, part * width, width), get_rows(w_reduce, part, parts)
        tiles = pieces(total, ROWS // 2)
        todo = []
        for step in range(len(tiles) + 1):
            if step < len(tiles):
                at, n = tiles[step]
                rows = slice(at, at + n)
                todo.append((rows, nn(hb[rows], w_in) + vector(E_BIAS + part), nt(cot[rows], w_out)))
            if step:
                rows, expanded, d_act = todo.pop(0)
                value, slope = gelu_parts(expanded)
                low = value.astype(BF)
                act[rows] = low
                d_low = (d_act * slope).astype(BF)
                d_exp[rows] = d_low
                acc_a[rows] = acc_a[rows] + nn(low, w_out)
                acc_b[rows] = acc_b[rows] + nt(d_low, w_in)
                add_sum(E_BIAS + part, d_low.astype(F32))
        put_rows(w_reduce, tn(act[...], cot[...]).astype(BF), part, parts)
        put(w_expand, tn(hb[...], d_exp[...]).astype(BF), part * width, width)
        transfers.after_part(part)
        return carried

    lax.fori_loop(0, parts, one_part, 0)

    d_att = d_exp

    @by_rows
    def _(rows):
        gradient = acc_b[rows]
        normed, inv = norm_parts(middle[rows])
        d_mid = cot[rows].astype(F32) + norm_back(gradient, normed, inv, vector(M_GAIN))
        add_sum(M_GAIN, gradient * normed)
        add_sum(M_SHIFT, gradient)
        middle[rows] = d_mid
        d_branch = d_mid.astype(BF)
        act[rows] = d_branch
        add_sum(P_BIAS, d_branch.astype(F32))
        d_att[rows] = nt(d_branch, get(w_proj, 0, width)).astype(BF)

    put(w_proj, tn(attended[...], act[...]).astype(BF), 0, width)
    transfers.have_proj()
    unload(acc_a, acc_b, hb)
    transfers.have_result()
    acc_b[...] = jnp.zeros_like(acc_b)
    all_backward(b, transfers)
    weight_of_block(b, 0, transfers)

    @by_rows
    def _(rows):
        gradient = acc_b[rows]
        normed, inv = norm_parts(b.xc[rows].astype(F32))
        add_sum(A_GAIN, gradient * normed)
        add_sum(A_SHIFT, gradient)
        acc_a[rows] = middle[rows] + norm_back(gradient, normed, inv, vector(A_GAIN))

    transfers.have_vectors()
    unload(acc_a, acc_b, act)
    transfers.have_grad()


class Local:
    def __init__(self, b, lengths, ins, outs, sems):
        self.b, self.lengths, self.outs = b, lengths, outs
        targets = (b.x_in, b.cot) + tuple(b[-4:])
        self.loads = [pltpu.make_async_copy(one, target, sems.at[i]) for i, (one, target) in enumerate(zip(ins, targets))]
        sources = (b.hb, b.act) + tuple(b[-4:])
        self.stores = [pltpu.make_async_copy(one, out, sems.at[6 + i]) for i, (one, out) in enumerate(zip(sources, outs))]

    def begin(self):
        for copy in self.loads:
            copy.start()

    def enter(self):
        pass

    def first_length(self):
        return jnp.full((1, 1), self.lengths[lax.axis_index("blk"), 0, 0], jnp.int32).astype(F32)

    def need_tokens(self):
        self.loads[0].wait()

    def need_first(self):
        self.loads[2 + QKV].wait()

    def before_block(self, j):
        pass

    def after_forward(self, i):
        pass

    def need_cotangent(self):
        self.loads[1].wait()

    def need_proj(self):
        self.loads[2 + PROJ].wait()

    def need_mlp(self):
        self.loads[2 + EXPAND].wait()
        self.loads[2 + REDUCE].wait()

    def after_part(self, part):
        pass

    def have_proj(self):
        for which in (PROJ, EXPAND, REDUCE):
            self.stores[2 + which].start()

    def have_result(self):
        self.stores[0].start()

    def after_backward(self, i):
        pass

    def have_qkv(self, j):
        pass

    def have_vectors(self):
        self.stores[2 + QKV].start()

    def have_grad(self):
        self.stores[1].start()
        for copy in self.stores:
            copy.wait()


def local_kernel(lengths, vec, x_in, cot_in, w_qkv, w_proj, w_expand, w_reduce,
                 result, grad_x, g_qkv, g_proj, g_expand, g_reduce, g_vec, *scratch):
    b = Buffers(*scratch[:-1])
    b.vec[...] = vec[...]
    ins = (x_in, cot_in, w_qkv, w_proj, w_expand, w_reduce)
    outs = (result, grad_x, g_qkv, g_proj, g_expand, g_reduce)
    compute(b, Local(b, lengths, ins, outs, scratch[-1]))
    g_vec[...] = b.g_vec[...]


def run_local(lengths, vec, x_in, cot_in, weights):
    vmem, anywhere = pl.BlockSpec(memory_space=pltpu.VMEM), pl.BlockSpec(memory_space=pl.ANY)
    total, width = x_in.shape
    like = (x_in, x_in) + tuple(weights)
    return pl.pallas_call(
        local_kernel,
        out_shape=[jax.ShapeDtypeStruct(one.shape, BF) for one in like]
        + [jax.ShapeDtypeStruct((VEC_ROWS, width), F32)],
        in_specs=[pl.BlockSpec(memory_space=pltpu.SMEM), vmem] + [anywhere] * 6,
        out_specs=[anywhere] * 6 + [vmem],
        scratch_shapes=buffers(total, width, [one.shape for one in weights]) + [pltpu.SemaphoreType.DMA((12,))],
        compiler_params=pltpu.CompilerParams(vmem_limit_bytes=62 * 2**20),
    )(lengths, vec, x_in, cot_in, *weights)


UNITS = (
    (QKV, 0, LANES + TRIO), (QKV, LANES + TRIO, TRIO), (QKV, LANES + 2 * TRIO, TRIO), (QKV, LANES + 3 * TRIO, TRIO),
    (PROJ, 0, 6 * LANES),
    (EXPAND, 0, 8 * LANES), (EXPAND, 8 * LANES, 8 * LANES), (REDUCE, 0, 4 * LANES), (REDUCE, 0, 4 * LANES),
)
HALVES = {7: pl.ds(0, SPREAD[Z] // 2), 8: pl.ds(SPREAD[Z] // 2, SPREAD[Z] // 2)}
EARLY_UNITS, PROJ_UNITS, EXPAND_UNITS, REDUCE_UNITS = (0, 1, 2, 3), (4,), (5, 6), (7, 8)
VECTOR_TILES = ((QKV, 0), (PROJ, 4 * LANES), (PROJ, 5 * LANES))
VECTORS = CHUNKS
CHUNK_COPIES = 6
CHUNKS_BEFORE = (0, CHUNKS + 1, CHUNKS + 2, 2 * CHUNKS + 2)


def schedule():
    entries = {}

    def enter(t, which, stage, chunk):
        entries.setdefault(t, []).append((which, stage, chunk))

    for chunk in range(CHUNKS):
        for stage, later in enumerate((2, 4, 6, 8)):
            enter(chunk + later, EXPAND, stage, chunk)
        for stage, later in enumerate((1, 3, 5)):
            enter(chunk + later, REDUCE, stage, chunk)
    enter(8, REDUCE, None, 0)
    enter(11, REDUCE, 3, 0)
    for stage, t in enumerate((6, 8, 10, 12)):
        enter(t, PROJ, stage, 0)
    for number, times in enumerate(((8, 9, 10, 11), (10, 11, 12, 13), (12, 13, 14, 15), (13, 14, 15, 16))):
        for stage, t in enumerate(times):
            enter(t, QKV, stage, CHUNKS - 1 - number)
    for stage, t in enumerate((15, 16, 17)):
        enter(t, QKV, stage + 1, VECTORS)
    return entries


SCHEDULE = schedule()


class Group:
    def __init__(self, b, ins, outs, scratch):
        self.b = b
        self.tokens, self.cotangent, self.vectors, self.shards = ins
        self.result, self.grad_x, held, targets = outs
        self.outs, self.g_total = held[:4], held[4]
        (self.lengths, self.own_lengths, self.own_qkv, self.own_vec, self.packed, self.turn, self.tile, self.arrived,
         self.local_sem, self.token_sem, self.ag_sem, self.rs_sem) = scratch
        self.weights = tuple(b[-4:])
        self.handed = [
            pltpu.make_async_copy(one, target, self.local_sem.at[17 + i])
            for i, (one, target) in enumerate(zip(held, targets))
        ]
        dp, blk = lax.axis_index("dp"), lax.axis_index("blk")
        z, y, x, c = dp // SPREAD[Y], dp % SPREAD[Y], blk // SPREAD[C], blk % SPREAD[C]
        self.mine = (z, y, x, c)
        self.index = dp * (SPREAD[X] * SPREAD[C]) + blk
        self.blk = blk
        n_blk = SPREAD[X] * SPREAD[C]
        self.others = [(dp, (blk + k) % n_blk) for k in range(1, n_blk)]
        z_places = [(z + k) % SPREAD[Z] for k in range(1, SPREAD[Z])]
        self.along = (
            [((place * SPREAD[Y] + y, blk), place) for place in z_places],
            [((dp + 1 - 2 * y, blk), 1 - y)],
            [((dp, blk + SPREAD[C] * (1 - 2 * x)), 1 - x)],
            [((dp, blk + 1 - 2 * c), 1 - c)],
        )
        height = self.tokens.shape[1]

        def rows(ref):
            return lambda i: ref.at[pl.ds(pl.multiple_of(i * height, height), height)]

        def part(ref):
            return lambda i: ref.at[i]

        moves = (
            (part(self.tokens), rows(b.x_in)),
            (part(self.cotangent), rows(b.cot)),
            (rows(b.hb), part(self.result)),
            (rows(b.act), part(self.grad_x)),
        )
        self.swaps = [
            [
                self.remote(source(device[1]), target(blk), self.token_sem.at[i, k], self.token_sem.at[4 + i, k], device)
                for k, device in enumerate(self.others)
            ]
            for i, (source, target) in enumerate(moves)
        ]
        self.kept = [
            pltpu.make_async_copy(source(blk), target(blk), self.local_sem.at[i])
            for i, (source, target) in enumerate(moves)
        ]

    @staticmethod
    def remote(source, target, send, recv, device):
        return pltpu.make_async_remote_copy(
            src_ref=source, dst_ref=target, send_sem=send, recv_sem=recv,
            device_id=device, device_id_type=pl.DeviceIdType.MESH,
        )

    @staticmethod
    def start(copies):
        for copy in copies:
            copy.start()

    @staticmethod
    def arrive(copies):
        for copy in copies:
            copy.wait_recv()

    @staticmethod
    def sent(copies):
        for copy in copies:
            copy.wait_send()

    def place(self, free, at=None):
        index = [slice(None) if axis in free else self.mine[axis] for axis in range(4)]
        for axis, value in (at or {}).items():
            index[axis] = value
        return tuple(index)


    def gather(self, unit, stage):
        which, first, columns = UNITS[unit]
        w, order = self.weights[which], GATHER_ORDER[which]
        cols = (slice(None), pl.ds(first, columns))

        def one(i, view, device):
            return self.remote(view, view, self.ag_sem.at[0, unit, i], self.ag_sem.at[1, unit, i], device)

        half = {Z: HALVES[unit]} if unit in HALVES else {}
        if stage == 0 and unit in HALVES:
            if unit != min(HALVES):
                return []
            half = {}
        if stage < 3:
            view = w.at[self.place(order[:stage], half) + cols]
            return [one(copies_before(order, stage) + k, view, device) for k, (device, _) in enumerate(self.along[order[stage]])]
        device, _ = self.along[C][0]
        last = order[2]
        if stage == 3:
            return [one(5, w.at[self.place(order[:2], half) + cols], device)]
        (_, other), = self.along[last]
        return [one(6, w.at[self.place(order[:2], {last: other, **half}) + cols], device)]

    def gather_on(self, units, stage):
        for unit in units:
            copies = self.gather(unit, stage)
            self.arrive(copies)
            self.sent(copies)
            if stage < 2:
                self.start(self.gather(unit, stage + 1))
            if stage in (1, 2):
                self.start(self.gather(unit, stage + 2))

    def gathered(self, units):
        for unit in units:
            for stage in (3, 4):
                copies = self.gather(unit, stage)
                self.arrive(copies)
                self.sent(copies)

    def unpack(self, tile):
        which, first = VECTOR_TILES[tile]
        w = self.weights[which]
        all_of = w[:, :, :, :, 0:PACKED, first : first + LANES].astype(F32)
        total = jnp.sum(all_of.reshape(-1, PACKED, LANES), axis=0)
        for i in range(PACKED):
            row, at = divmod(tile * PACKED + i, 4)
            self.b.vec[row : row + 1, at * LANES : (at + 1) * LANES] = total[i : i + 1, :]


    def chunk_view(self, which, chunk):
        if which == REDUCE:
            return chunk, slice(None)
        if which == QKV:
            return None, pl.ds(0, LANES) if chunk == VECTORS else pl.ds(LANES + chunk * TRIO, TRIO)
        return None, pl.ds(chunk * 4 * LANES, 4 * LANES)

    def scatter(self, which, stage, chunk):
        w, order = self.weights[which], SCATTER_ORDER[which]
        axis, rest = order[stage], order[stage + 1 :]
        buffer = self.arrived[which][stage]
        at_z, cols = self.chunk_view(which, chunk)
        first = (CHUNKS_BEFORE[which] + chunk) * CHUNK_COPIES + copies_before(order, stage)
        copies, terms = [], []
        for k, (device, other) in enumerate(self.along[axis]):
            at = {axis: other}
            if at_z is not None and Z in rest:
                at[Z] = at_z
            source = w.at[self.place(rest, at) + (slice(None), cols)]
            lead = (k,) if axis == Z else ()
            free = tuple(at_z if one == Z and at_z is not None else slice(None) for one in sorted(rest))
            target = buffer.at[lead + free + (slice(None), cols)]
            copies.append(self.remote(source, target, self.rs_sem.at[0, first + k], self.rs_sem.at[1, first + k], device))
            terms.append(target)
        return copies, terms

    def scatter_start(self, which, stage, chunk):
        self.start(self.scatter(which, stage, chunk)[0])

    def scatter_on(self, which, stage, chunk):
        w, order = self.weights[which], SCATTER_ORDER[which]
        copies, terms = self.scatter(which, stage, chunk)
        self.arrive(copies)
        rest = order[stage + 1 :]
        at_z, cols = self.chunk_view(which, chunk)
        at = {Z: at_z} if at_z is not None and Z in rest else None
        here = self.place(rest, at) + (slice(None), cols)
        if which == QKV and chunk == VECTORS:
            self.add_vectors(here, terms, rest)
        elif len(terms) == 1 and rest:
            w[here] = w[here] + terms[0][...]
        else:
            total = w[here].astype(F32)
            for term in terms:
                total = total + term[...].astype(F32)
            if rest:
                w[here] = total.astype(BF)
            else:
                self.keep(which, chunk, total)
        if rest and not (which == REDUCE and rest == (Z,)):
            self.scatter_start(which, stage + 1, chunk)
        self.sent(copies)

    def add_vectors(self, here, terms, rest):
        w = self.weights[QKV]
        total = w[here].astype(F32)
        for term in terms:
            total = total + term[...].astype(F32)
        half = PACKED // 2
        exact = total[..., :half, :] + total[..., half:, :]
        if rest:
            high = exact.astype(BF).astype(F32)
            w[here] = jnp.concatenate([high, exact - high], axis=-2).astype(BF)
        else:
            self.g_total[...] = exact

    def keep(self, which, chunk, total):
        out = self.outs[which]
        if which == QKV:
            width = out.shape[1] // 3
            for i in range(3):
                out[:, i * width + chunk * LANES : i * width + (chunk + 1) * LANES] = total[:, i * LANES : (i + 1) * LANES]
        else:
            out[:, self.chunk_view(which, chunk)[1]] = total

    def tick(self, t):
        for which, stage, chunk in SCHEDULE.get(t, ()):
            if stage is None:
                self.scatter_start(which, 3, chunk)
            else:
                self.scatter_on(which, stage, chunk)


    def spread_vectors(self):
        g_vec, lines, tile = self.b.g_vec, self.packed, self.tile
        parts = g_vec.shape[1] // LANES
        for i in range(lines.shape[0]):
            lines[i : i + 1, :] = g_vec[i // parts : i // parts + 1, i % parts * LANES : (i % parts + 1) * LANES]
        tile[...] = jnp.zeros_like(tile)
        devices = math.prod(SPREAD)
        for device in range(0, devices, SPREAD[C]):
            row = 0
            for i, one in enumerate(self.own_vec):
                size = one.shape[0]
                if device * size % LANES == 0:
                    at = row + device * size // LANES
                    tile[i : i + 1, :] = lines[at : at + 1, :]
                row += devices * size // LANES
            high = tile[...].astype(BF).astype(F32)
            value = jnp.concatenate([high, tile[...] - high], axis=0).astype(BF)
            pair = device // SPREAD[C]
            place = (pair // (SPREAD[X] * SPREAD[Y]), pair // SPREAD[X] % SPREAD[Y], pair % SPREAD[X])
            for core in range(SPREAD[C]):
                self.weights[QKV][place + (core, slice(None), pl.ds(0, LANES))] = value


    def begin(self):
        self.peers = self.others + [device for axis in (Y, Z) for device, _ in self.along[axis]]
        for device in self.peers:
            pl.semaphore_signal(
                pltpu.get_barrier_semaphore(), inc=1, device_id=device, device_id_type=pl.DeviceIdType.MESH
            )
        count = len(self.vectors)
        loads = [
            pltpu.make_async_copy(one, target, self.local_sem.at[4 + i])
            for i, (one, target) in enumerate(zip(self.vectors, self.own_vec))
        ]
        loads.append(pltpu.make_async_copy(self.shards[QKV], self.own_qkv, self.local_sem.at[8 + count]))
        width = self.shards[PROJ].shape[1]
        slots = [self.weights[which].at[self.mine] for which in range(4)]
        self.own = [
            pltpu.make_async_copy(
                self.shards[which], slots[which].at[:, pl.ds(0, self.shards[which].shape[1])],
                self.local_sem.at[4 + count + which],
            )
            for which in (PROJ, EXPAND, REDUCE)
        ]
        loads.append(pltpu.make_async_copy(self.lengths, self.own_lengths, self.local_sem.at[4 + count + QKV]))
        loads[-2], loads[-1] = loads[-1], loads[-2]
        self.start(loads + self.own + self.kept[:2])
        self.packed[...] = jnp.zeros_like(self.packed)
        row = 0
        for load, own in zip(loads, self.own_vec):
            load.wait()
            size = own.shape[0]
            self.turn[...] = jnp.zeros_like(self.turn)
            self.turn[0:1, 0:size] = own[...].astype(F32).reshape(1, size)
            at = self.index * size
            self.packed[pl.ds(row + at // LANES, 1), :] = pltpu.roll(self.turn[...], at % LANES, 1)[0:1, :]
            row += math.prod(SPREAD) * size // LANES
        for load in loads[count:]:
            load.wait()
        w = self.weights[QKV]
        for j in range(width // LANES):
            for i in range(3):
                to = LANES + j * TRIO + i * LANES
                w[self.mine + (slice(None), pl.ds(to, LANES))] = self.own_qkv[:, i * width + j * LANES : i * width + (j + 1) * LANES]
        for tile, (which, first) in enumerate(VECTOR_TILES):
            values = self.packed[tile * PACKED : (tile + 1) * PACKED, :].astype(BF)
            self.weights[which][self.mine + (slice(None), pl.ds(first, LANES))] = values

    def enter(self):
        pl.semaphore_wait(pltpu.get_barrier_semaphore(), len(self.peers))
        for unit in EARLY_UNITS:
            self.start(self.gather(unit, 0))
        self.start(self.swaps[0])
        for copy in self.own:
            copy.wait()
        for unit in PROJ_UNITS + EXPAND_UNITS:
            self.start(self.gather(unit, 0))

    def first_length(self):
        first = self.own_lengths[0][0:1, :].astype(F32)
        lane = lax.broadcasted_iota(jnp.int32, first.shape, 1)
        return jnp.sum(jnp.where(lane == self.blk, first, 0.0), axis=1, keepdims=True)

    def need_tokens(self):
        self.gather_on(EARLY_UNITS, 0)
        self.gather_on(EARLY_UNITS[:2], 1)
        self.gather_on(EARLY_UNITS[:1], 2)
        self.gather_on(EARLY_UNITS[2:3], 1)
        self.gather_on(EARLY_UNITS[1:2], 2)
        self.gather_on(EARLY_UNITS[3:], 1)
        self.start(self.gather(REDUCE_UNITS[0], 0))
        self.gathered(EARLY_UNITS[:1])
        self.unpack(0)
        self.kept[0].wait()
        self.arrive(self.swaps[0])
        self.sent(self.swaps[0])
        self.start(self.swaps[1])

    def need_first(self):
        self.gather_on(PROJ_UNITS + EXPAND_UNITS, 0)
        self.gather_on(EARLY_UNITS[2:3], 2)

    def before_block(self, j):
        for unit in EARLY_UNITS[1:]:
            pl.when(j == unit)(lambda unit=unit: self.gathered((unit,)))

    def after_forward(self, i):
        steps = (
            lambda: (self.gather_on(EARLY_UNITS[3:], 2), self.gather_on(REDUCE_UNITS, 0)),
            lambda: None,
            lambda: self.gather_on(PROJ_UNITS, 1),
            lambda: (self.gather_on(REDUCE_UNITS, 1), self.gather_on(EXPAND_UNITS[:1], 1)),
            lambda: self.gather_on(PROJ_UNITS, 2),
            lambda: self.gather_on(EXPAND_UNITS[1:], 1),
            lambda: self.gather_on(EXPAND_UNITS[:1], 2),
            lambda: self.gather_on(REDUCE_UNITS[:1], 2),
        )
        for at, step in enumerate(steps):
            pl.when(i == at)(lambda step=step: [step(), None][1])

    def need_cotangent(self):
        self.kept[1].wait()
        self.arrive(self.swaps[1])
        self.sent(self.swaps[1])

    def need_proj(self):
        self.gathered(PROJ_UNITS)
        self.unpack(1)
        self.unpack(2)

    def need_mlp(self):
        self.gathered(EXPAND_UNITS[:1] + REDUCE_UNITS[:1])

    def after_part(self, part):
        for at in range(CHUNKS):
            @pl.when(part == at)
            def _(at=at):
                self.scatter_start(REDUCE, 0, at)
                self.scatter_start(EXPAND, 0, at)
                if at == 0:
                    self.gather_on(EXPAND_UNITS[1:] + REDUCE_UNITS[1:], 2)
                if at == 1:
                    self.gathered(EXPAND_UNITS[1:] + REDUCE_UNITS[1:])
                self.tick(at)

    def have_proj(self):
        self.scatter_start(PROJ, 0, 0)
        self.tick(CHUNKS)

    def have_result(self):
        self.start(self.swaps[2] + self.kept[2:3])

    def after_backward(self, i):
        for at in range(2 * CHUNKS):
            pl.when(i == at)(lambda at=at: self.tick(CHUNKS + 1 + at))

    def have_qkv(self, j):
        if isinstance(j, int):
            self.scatter_start(QKV, 0, j)
            return
        for at in range(1, CHUNKS):
            pl.when(j == at)(lambda at=at: self.scatter_start(QKV, 0, at))

    def have_vectors(self):
        self.tick(3 * CHUNKS + 1)
        self.spread_vectors()
        self.scatter_start(QKV, 0, VECTORS)

    def have_grad(self):
        self.scatter_on(QKV, 0, VECTORS)
        self.start(self.swaps[3] + self.kept[3:4])
        for t in range(3 * CHUNKS + 2, max(SCHEDULE) + 1):
            self.tick(t)
        self.start(self.handed)
        for copy in self.handed:
            copy.wait()
        for i in (2, 3):
            self.kept[i].wait()
            self.arrive(self.swaps[i])
            self.sent(self.swaps[i])


N_VECTORS = 8


def group_kernel(*refs):
    refs = list(refs)

    def take(n):
        taken = refs[:n]
        del refs[:n]
        return taken

    (lengths,), vectors, (tokens, cotangent), shards = take(1), take(N_VECTORS), take(2), take(4)
    (result, grad_x), outs, (g_total,) = take(2), take(4), take(1)
    b = Buffers(*take(len(Buffers._fields)))
    (own_lengths, own_qkv), own_vec, (packed, turn, tile) = take(2), take(N_VECTORS), take(3)
    arrived = [take(4) for _ in range(4)]
    held = take(5)
    scratch = [lengths, own_lengths, own_qkv, own_vec, packed, turn, tile, arrived] + refs
    group = Group(b, (tokens, cotangent, vectors, shards), (result, grad_x, held, outs + [g_total]), scratch)
    compute(b, group)


def run_group(lengths, vectors, tokens, cotangent, weights):
    anywhere = pl.BlockSpec(memory_space=pl.ANY)
    blk, height, width = tokens.shape
    extra = [0] * 4
    for which, _ in VECTOR_TILES:
        extra[which] += LANES
    shapes = [SPREAD + (one.shape[0], one.shape[1] + more) for one, more in zip(weights, extra)]
    landing = []
    for which, shape in enumerate(shapes):
        for stage, axis in enumerate(SCATTER_ORDER[which]):
            rest = sorted(SCATTER_ORDER[which][stage + 1 :])
            lead = (SPREAD[Z] - 1,) if axis == Z else ()
            landing.append(pltpu.VMEM(lead + tuple(SPREAD[one] for one in rest) + shape[4:], BF))
    packed_rows = math.prod(SPREAD) * sum(one.shape[0] for one in vectors) // LANES
    dma = pltpu.SemaphoreType.DMA
    return pl.pallas_call(
        group_kernel,
        out_shape=[jax.ShapeDtypeStruct(tokens.shape, BF)] * 2
        + [jax.ShapeDtypeStruct(one.shape, F32) for one in weights]
        + [jax.ShapeDtypeStruct((N_VECTORS, LANES), F32)],
        in_specs=[anywhere] * (N_VECTORS + 7),
        out_specs=[anywhere] * 7,
        scratch_shapes=buffers(blk * height, width, shapes)
        + [pltpu.VMEM(lengths.shape, lengths.dtype), pltpu.VMEM(weights[QKV].shape, BF)]
        + [pltpu.VMEM(one.shape, BF) for one in vectors]
        + [pltpu.VMEM((packed_rows, LANES), F32), pltpu.VMEM((8, LANES), F32), pltpu.VMEM((N_VECTORS, LANES), F32)]
        + landing
        + [pltpu.VMEM(one.shape, F32) for one in weights]
        + [pltpu.VMEM((N_VECTORS, LANES), F32)]
        + [dma((22,)), dma((8, 3)), dma((2, len(UNITS), 7)), dma((2, (CHUNKS_BEFORE[-1] + CHUNKS) * CHUNK_COPIES))],
        compiler_params=pltpu.CompilerParams(
            vmem_limit_bytes=62 * 2**20, collective_id=0, has_side_effects=True
        ),
    )(lengths, *vectors, tokens, cotangent, *weights)


def finish_kernel(result, grad_x, g_qkv, g_proj, g_expand, g_reduce, g_vec, *refs):
    sources = (result, grad_x, g_qkv, g_proj, g_expand, g_reduce)
    outs, refs = refs[: 6 + N_VECTORS], refs[6 + N_VECTORS :]
    held, short = refs[:6], refs[6 : 6 + N_VECTORS]
    turn, sems = refs[6 + N_VECTORS :]
    loads, stores = [], []
    for source, to, out in zip(sources, held, outs):
        places = range(source.shape[0]) if len(source.shape) == 3 else (slice(None),)
        for place in places:
            sem = len(loads)
            loads.append(pltpu.make_async_copy(source.at[place], to.at[place], sems.at[0, sem]))
            stores.append(pltpu.make_async_copy(to.at[place], out.at[place], sems.at[1, sem]))
    for load in loads:
        load.start()
    handed = []
    index = lax.axis_index("dp") * lax.axis_size("blk") + lax.axis_index("blk")
    for i, one in enumerate(short):
        size = one.shape[0]
        at = index * size
        turn[0:1, :] = g_vec[i : i + 1, :]
        turned = pltpu.roll(turn[...], (LANES - at % LANES) % LANES, 1)
        one[...] = turned[0:1, 0:size].reshape(size)
        handed.append(pltpu.make_async_copy(one, outs[6 + i], sems.at[0, len(loads) + i]))
        handed[-1].start()
    for load, store in zip(loads, stores):
        load.wait()
        store.start()
    for store in stores + handed:
        store.wait()


def finish(values, sizes):
    vmem, anywhere = pl.BlockSpec(memory_space=pltpu.VMEM), pl.BlockSpec(memory_space=pl.ANY)
    long = [(one.shape, one.dtype) for one in values[:6]]
    short = [((size,), F32) for size in sizes]
    return pl.pallas_call(
        finish_kernel,
        out_shape=[jax.ShapeDtypeStruct(*one) for one in long + short],
        in_specs=[anywhere] * 6 + [vmem],
        out_specs=[anywhere] * (6 + len(sizes)),
        scratch_shapes=[pltpu.VMEM(*one) for one in long + short]
        + [pltpu.VMEM((8, LANES), F32)]
        + [pltpu.SemaphoreType.DMA((2, 4 + 2 * values[0].shape[0] + len(sizes)))],
    )(*values)


def by_collectives(lengths, vectors, sizes, tokens, cotangent, weights):
    axes = ("dp", "blk")
    width = tokens.shape[2]
    blocks = width // LANES

    def exchange(rows):
        return lax.all_to_all(rows.reshape(tokens.shape), "blk", 0, 0, tiled=True)

    packed = lax.all_gather(jnp.concatenate(vectors), axes, axis=0)
    starts = [sum(sizes[:i]) for i in range(len(sizes))]
    full = [packed[:, at : at + size].reshape(-1, width) for at, size in zip(starts, sizes)]
    vec = jnp.concatenate(full, axis=0).astype(F32)
    vec = jnp.pad(vec, ((0, VEC_ROWS - vec.shape[0]), (0, 0)))
    whole = [lax.all_gather(one, axes, axis=0, tiled=True) for one in weights]
    whole[QKV] = whole[QKV].reshape(width, 3, blocks, LANES).swapaxes(1, 2).reshape(width, 3 * width)
    result, grad_x, *grads, g_vec = run_local(
        lengths, vec, exchange(tokens).reshape(-1, width), exchange(cotangent).reshape(-1, width), whole
    )
    grads[QKV] = grads[QKV].reshape(width, blocks, 3, LANES).swapaxes(1, 2).reshape(width, 3 * width)
    grads = [lax.psum_scatter(one.astype(F32), axes, scatter_dimension=0, tiled=True) for one in grads]
    g_vec = lax.psum(g_vec, axes).reshape(-1)
    index = lax.axis_index(axes)
    devices = lax.axis_size(axes)
    own = [
        lax.dynamic_slice(g_vec, (devices * at + index * size,), (size,)) for at, size in zip(starts, sizes)
    ]
    return (exchange(result), exchange(grad_x), *grads, *own)


def body(
    tokens, lengths, attn_gain, attn_shift, w_qkv, qv_bias, w_proj, proj_bias,
    mlp_gain, mlp_shift, w_expand, expand_bias, w_reduce, reduce_bias, cotangent,
):
    vectors = (attn_gain, attn_shift, qv_bias, proj_bias, mlp_gain, mlp_shift, reduce_bias, expand_bias)
    sizes = [one.shape[0] for one in vectors]
    weights = (w_qkv, w_proj, w_expand, w_reduce)
    sized = (lax.axis_size("dp"), lax.axis_size("blk")) == (SPREAD[Z] * SPREAD[Y], SPREAD[X] * SPREAD[C])
    if sized and all(one.shape[0] % 16 == 0 for one in weights):
        outs = finish(run_group(jnp.transpose(lengths, (1, 2, 0)), vectors, tokens, cotangent, weights), sizes)
    else:
        outs = by_collectives(lengths, vectors, sizes, tokens, cotangent, weights)
    result, grad_x, g_qkv, g_proj, g_expand, g_reduce, ag, as_, qv, pb, mg, ms, rb, eb = outs
    return (result, grad_x, ag, as_, g_qkv, qv, g_proj, pb, mg, ms, g_expand, eb, g_reduce, rb)


def solution(mesh):
    both = ("dp", "blk")
    rows = P(None, both, None)
    vector, matrix = P(both), P(both, None)
    weights = (
        vector, vector, matrix, vector, matrix, vector, vector, vector, matrix, vector, matrix, vector,
    )
    return jax.shard_map(
        body,
        mesh=mesh,
        in_specs=(rows, P(None, "dp", None)) + weights + (rows,),
        out_specs=(rows, rows) + weights,
        check_vma=False,
    )
```
